32 devices in a mesh: dp: 4 (over x, core), seq: 2 (over y), vocab: 4 (over z).
Axes of the slice: x: 2, y: 2, z: 4, core: 2. Of those that a mesh axis runs over, the one named last changes fastest.
Arguments:
- queries: bfloat16 [4, 64, 4096], P('dp', 'seq', 'vocab'), may hold values from -64 to 64
- enc_keys: bfloat16 [4, 256, 4096], P('dp', 'seq', 'vocab'), may hold values from -6 to 6
- enc_values: bfloat16 [4, 256, 4096], P('dp', 'seq', 'vocab'), may hold values from -6 to 6
- enc_lengths: int32 [4], P('dp'), may hold values from 64 to 256, as said below
- out_proj: bfloat16 [4096, 4096], P('vocab', 'seq'), may hold values from -0.375 to 0.375
- residual: bfloat16 [4, 64, 4096], P('dp', None, 'seq'), may hold values from -270 to 270
- norm_gain: float32 [4096], P('seq'), may hold values from 0.4 to 1.6
- head_weight: bfloat16 [4096, 32128], P('seq', 'vocab'), may hold values from -1 to 1
- targets: int32 [4, 64], P('dp', 'seq'), may hold values from 0 to 32127
Outputs:
- mean_loss: float32 [], replicated
- head_grad: bfloat16 [4096, 32128], P('seq', 'vocab')
- key_grad: float32 [4, 256, 4096], P('dp', 'seq', 'vocab')
- value_grad: float32 [4, 256, 4096], P('dp', 'seq', 'vocab')
The draws below stay inside these ranges and needn't reach their ends.
Inputs may be any that keep to these rules, and one draw needn't show every extreme that they name: `enc_lengths`: each example has at least 64 unpadded positions; some example has none padded.
All inputs are finite; a program needn't handle non-finite values.
Results may differ from the reference program's by a relative error of at most 0.02.
Values may be sent and summed in bfloat16 or wider, within the bound.
No kernel may reach another device: no remote copies, remote signals or barrier semaphores. Data moves between devices by JAX's collectives and lax.ppermute only.
A program may use at most 192 MiB of HBM per device.

```python
import math
import jax
import jax.numpy as jnp
import numpy as np
from jax import lax

D = 4096
HEADS = 16
HDIM = 256
VOCAB = 32128
EX = 1
TGT_DEV = 32
BATCH = 4
TGT = 64
ENC = 256
N_DP = 4
N_SEQ = 2


def sign_pattern(key):
    chosen = jax.random.bernoulli(jax.random.fold_in(key, 501), 0.5, (D,))
    return jnp.where(chosen, 1.0, -1.0).astype(jnp.float32)


def width_profile():
    position = lax.broadcasted_iota(jnp.float32, (D,), 0) / D
    profile = 0.4 + 1.6 * position
    return profile


def encoder_draw(key):
    base_key = jax.random.fold_in(key, 101)
    full_shape = (BATCH, ENC, HEADS * HDIM)
    drawn = jnp.clip(jax.random.normal(base_key, full_shape, jnp.float32), -6.0, 6.0)
    return drawn


def leading_keys(key):
    drawn = encoder_draw(key)
    return drawn


def draw_enc_keys(key, part):
    drawn = leading_keys(key)
    return drawn.astype(jnp.bfloat16)


def draw_queries(key, part):
    base_key = jax.random.fold_in(key, 201)
    full_shape = (BATCH, TGT, HEADS * HDIM)
    drawn = jnp.clip(2.0 * jax.random.normal(base_key, full_shape, jnp.float32), -12.0, 12.0)
    return drawn.astype(jnp.bfloat16)


def draw_enc_lengths(key, part):
    lengths = jax.random.randint(jax.random.fold_in(key, 301), (BATCH,), ENC // 4, ENC + 1)
    longest = jax.random.randint(jax.random.fold_in(key, 302), (), 0, BATCH)
    shortest = (longest + 1 + jax.random.randint(jax.random.fold_in(key, 303), (), 0, BATCH - 1)) % BATCH
    example_ids = lax.broadcasted_iota(jnp.int32, (BATCH,), 0)
    lengths = jnp.where(example_ids == longest, ENC, lengths)
    lengths = jnp.where(example_ids == shortest, ENC // 4, lengths)
    return lengths.astype(jnp.int32)


def draw_residual(key, part):
    base_key = jax.random.fold_in(key, 401)
    full_shape = (BATCH, TGT, D)
    rising = 0.5 + lax.broadcasted_iota(jnp.float32, (D,), 0) / D
    pattern = sign_pattern(key)
    shared = pattern * width_profile()
    row_factor = jax.random.uniform(jax.random.fold_in(key, 405), (BATCH, TGT, 1), jnp.float32, -2.0, 2.0)
    noise = jnp.clip(jax.random.normal(base_key, full_shape, jnp.float32), -6.0, 6.0) * rising
    drawn = 0.7 * noise + row_factor * shared
    return drawn.astype(jnp.bfloat16)


def draw_head_weight(key, part):
    base_key = jax.random.fold_in(key, 601)
    full_shape = (D, VOCAB)
    rising = 0.5 + lax.broadcasted_iota(jnp.float32, (VOCAB,), 0) / VOCAB
    spread = 2.5 * D ** (-0.5)
    pattern = sign_pattern(key)
    column_factor = jnp.clip(jax.random.normal(jax.random.fold_in(key, 604), (VOCAB,), jnp.float32), -3.0, 3.0)
    shared = 12.0 / D * (pattern * width_profile())[:, None] * column_factor[None, :]
    drawn = jnp.clip(jax.random.normal(base_key, full_shape, jnp.float32), -6.0, 6.0) * spread * rising + shared
    return drawn.astype(jnp.bfloat16)


def set_ends(result, stream_key, least, top_value):
    dims = result.shape
    place = [jax.random.randint(jax.random.fold_in(stream_key, axis), (), 0, dims[axis]) for axis in range(len(dims))]
    result = result.at[tuple(place)].set(least)
    longest = dims.index(max(dims))
    place[longest] = (place[longest] + 1) % dims[longest]
    return result.at[tuple(place)].set(top_value)


def block_scale(stream_key, extent, split, smallest, high):
    factor_of = 1.0
    for dim, blocks in split:
        heights = jax.random.uniform(jax.random.fold_in(jax.random.fold_in(stream_key, 6), dim), (blocks,), jnp.float32, smallest / len(split), high / len(split))
        factor_of = factor_of * jnp.repeat(jnp.exp(heights), extent[dim] // blocks).reshape((-1,) + (1,) * (len(extent) - 1 - dim))
    return factor_of


def cumulative_ranks(amount, slope):
    weights = [(1 << 20) // math.isqrt(standing ** slope) + 1 for standing in range(1, amount + 1)]
    scale = 1 + sum(weights) // (1 << 30)
    return np.cumsum(np.array([max(1, weight // scale) for weight in weights]))


def ranked_ids(key, shape, amount, skew):
    listing = cumulative_ranks(amount, skew)
    pick = jax.random.randint(jax.random.fold_in(key, 1), shape, 0, int(listing[amount - 1]))
    grade = jnp.searchsorted(jnp.asarray(listing, jnp.int32), pick, side="right")
    return jax.random.permutation(jax.random.fold_in(key, 2), amount)[grade].astype(jnp.int32)


def scatter_about(key, shape, deviation, limit, cuts=(), kind=jnp.bfloat16):
    result = jax.random.normal(key, shape, jnp.float32) * deviation
    if len(cuts) > 0:
        result = block_scale(key, shape, cuts, -0.22, 0.18) * result
    return jnp.clip(result, min=-limit, max=limit).astype(kind)


def setup_inputs(seed: int = 0) -> dict:
    key_of = jax.random.split(jax.random.key(seed), 10)
    return {
        "queries": draw_queries(jax.random.fold_in(key_of[9], 71), 0),
        "enc_keys": draw_enc_keys(jax.random.fold_in(key_of[9], 71), 0),
        "enc_values": scatter_about(key_of[2], (BATCH, ENC, HEADS * HDIM), 1.0, 6.0, ((0, 4), (1, 2), (2, 4))),
        "enc_lengths": draw_enc_lengths(jax.random.fold_in(key_of[9], 71), 0),
        "out_proj": scatter_about(key_of[4], (HEADS * HDIM, D), (HEADS * HDIM // 16) ** -0.5, 0.375, ((0, 4), (1, 2))),
        "residual": draw_residual(jax.random.fold_in(key_of[9], 71), 0),
        "norm_gain": jnp.clip(1.0 + 0.12 * jax.random.normal(key_of[6], (D,), jnp.float32), 0.4, 1.6),
        "head_weight": draw_head_weight(jax.random.fold_in(key_of[9], 71), 0),
        "targets": set_ends(ranked_ids(key_of[8], (BATCH, TGT), VOCAB, 2), jax.random.fold_in(key_of[8], 3), 0, VOCAB - 1).astype(jnp.int32),
    }


zloss_weight = 0.0001
norm_epsilon = 1e-06

def settle(term):
    return lax.optimization_barrier(term.astype(jnp.bfloat16)).astype(jnp.float32)

def reference(queries, enc_keys, enc_values, enc_lengths, out_proj, residual, norm_gain, head_weight, targets):
    score_scale = HDIM ** (-0.5)

    def example_pass(inputs):
        query_rows, key_rows, value_rows, length, residual_rows, target_rows = inputs
        query_heads = query_rows.astype(jnp.float32).reshape(TGT, HEADS, HDIM)
        key_heads = key_rows.astype(jnp.float32).reshape(ENC, HEADS, HDIM)
        value_heads = value_rows.astype(jnp.float32).reshape(ENC, HEADS, HDIM)
        scores = jnp.einsum('thd,jhd->htj', query_heads, key_heads) * score_scale
        valid_keys = jnp.arange(ENC, dtype=jnp.int32) < length
        scores = jnp.where(valid_keys[None, None, :], scores, -jnp.inf)
        score_peak = lax.optimization_barrier(jnp.max(scores, axis=-1, keepdims=True))
        score_exp = jnp.exp(scores - score_peak)
        weights_full = score_exp / lax.optimization_barrier(jnp.sum(score_exp, axis=-1, keepdims=True))
        weights_half = weights_full.astype(jnp.bfloat16)
        attended = jnp.einsum('htj,jhd->thd', weights_half.astype(jnp.float32), value_heads)
        attended = attended.reshape(TGT, HEADS * HDIM).astype(jnp.bfloat16)
        mixed_rows = residual_rows.astype(jnp.float32) + jnp.dot(attended, out_proj, preferred_element_type=jnp.float32)
        square_sum = lax.optimization_barrier(jnp.sum(mixed_rows * mixed_rows, axis=-1))
        inverse_rms = lax.rsqrt(square_sum / D + norm_epsilon)
        normed = (mixed_rows * inverse_rms[:, None] * norm_gain).astype(jnp.bfloat16)
        logits = jnp.dot(normed, head_weight, preferred_element_type=jnp.float32)
        row_peak = lax.optimization_barrier(jnp.max(logits, axis=-1))
        log_total = row_peak + jnp.log(lax.optimization_barrier(jnp.sum(jnp.exp(logits - row_peak[:, None]), axis=-1)))
        target_hit = jnp.arange(VOCAB, dtype=jnp.int32)[None, :] == target_rows[:, None]
        target_logit = lax.optimization_barrier(jnp.sum(jnp.where(target_hit, logits, 0.0), axis=-1))
        token_loss = log_total - target_logit + zloss_weight * log_total * log_total
        logit_grad = (jnp.exp(logits - log_total[:, None]) * (1.0 + 2.0 * zloss_weight * log_total)[:, None] - target_hit.astype(jnp.float32)).astype(jnp.bfloat16)
        normed_grad = jnp.dot(logit_grad, head_weight.T, preferred_element_type=jnp.float32)
        gated = normed_grad * norm_gain
        dot_row = lax.optimization_barrier(jnp.sum(gated * mixed_rows, axis=-1))
        mixed_grad = (gated * inverse_rms[:, None] - mixed_rows * (inverse_rms ** 3 * dot_row / D)[:, None]).astype(jnp.bfloat16)
        attended_grad = jnp.dot(mixed_grad, out_proj.T, preferred_element_type=jnp.float32).astype(jnp.bfloat16)
        grad_heads = attended_grad.astype(jnp.float32).reshape(TGT, HEADS, HDIM)
        prob_grad = jnp.einsum('thd,jhd->htj', grad_heads, value_heads)
        score_grad = weights_full * (prob_grad - lax.optimization_barrier(jnp.sum(weights_full * prob_grad, axis=-1, keepdims=True)))
        score_half = (score_grad * score_scale).astype(jnp.bfloat16)
        block_weights = weights_half.astype(jnp.float32).reshape(HEADS, N_SEQ, TGT_DEV, ENC)
        block_scores = score_half.astype(jnp.float32).reshape(HEADS, N_SEQ, TGT_DEV, ENC)
        block_grads = grad_heads.reshape(N_SEQ, TGT_DEV, HEADS, HDIM)
        block_queries = query_heads.reshape(N_SEQ, TGT_DEV, HEADS, HDIM)
        value_part = jnp.einsum('hstj,sthd->sjhd', block_weights, block_grads)
        key_part = jnp.einsum('hstj,sthd->sjhd', block_scores, block_queries)
        value_grad = lax.optimization_barrier(jnp.sum(settle(value_part), axis=0)).reshape(ENC, HEADS * HDIM)
        key_grad = lax.optimization_barrier(jnp.sum(settle(key_part), axis=0)).reshape(ENC, HEADS * HDIM)
        return (token_loss, normed, logit_grad, key_grad, value_grad)
    token_losses, normed_all, grads_all, key_grad, value_grad = lax.map(example_pass, (queries, enc_keys, enc_values, enc_lengths, residual, targets))
    mean_loss = jnp.sum(token_losses) / (BATCH * TGT)

    def group_add(group, accumulated):
        normed_rows = lax.dynamic_slice_in_dim(normed_all, group * EX, EX, 0).reshape(EX * TGT, D)
        grad_rows = lax.dynamic_slice_in_dim(grads_all, group * EX, EX, 0).reshape(EX * TGT, VOCAB)
        return accumulated + settle(jnp.dot(normed_rows.T, grad_rows, preferred_element_type=jnp.float32))
    head_total = lax.fori_loop(0, N_DP, group_add, jnp.zeros((D, VOCAB), jnp.float32))
    return (mean_loss, head_total.astype(jnp.bfloat16), key_grad, value_grad)
```

```python
import functools
import jax
import jax.numpy as jnp
from jax import lax
from jax.experimental import pallas as pl
from jax.experimental.pallas import tpu as pltpu
from jax.sharding import PartitionSpec as P

HDIM = 256
LANES = 128
TILE = 512
MAX_CHUNKS = 4
LOW = -1e30
CODE_TOP = 32767.0

zloss_weight = 0.0001
norm_epsilon = 1e-06
score_scale = HDIM ** (-0.5)
f32, bf16, i32 = jnp.float32, jnp.bfloat16, jnp.int32

VMEM = pl.BlockSpec(memory_space=pltpu.VMEM)
SMEM = pl.BlockSpec(memory_space=pltpu.SMEM)


def sds(shape, dtype):
    return jax.ShapeDtypeStruct(shape, dtype)


def params(mib=40):
    return pltpu.CompilerParams(vmem_limit_bytes=mib * 1024 * 1024)


def cost(flops, nbytes):
    return pl.CostEstimate(flops=int(flops), bytes_accessed=int(nbytes), transcendentals=0)


def dot(a, b, ca, cb):
    return lax.dot_general(a, b, (((ca,), (cb,)), ((), ())), preferred_element_type=f32)


def from_ahead(x, axis, k):
    n = lax.axis_size(axis)
    return lax.ppermute(x, axis, [((i + k) % n, i) for i in range(n)])


def gather_ring(x, axis):
    return [x] + [from_ahead(x, axis, k) for k in range(1, lax.axis_size(axis))]


def scatter_ring(x, axis, rows):
    n = lax.axis_size(axis)
    return [
        lax.ppermute(x[k * rows : (k + 1) * rows], axis, [(i, (i + k) % n) for i in range(n)])
        for k in range(1, n)
    ]


def swap(x, axis, bit):
    n = lax.axis_size(axis)
    return lax.ppermute(x, axis, [(i, i ^ bit) for i in range(n)])


def gather_swaps(x, axis):
    held = [x]
    bit = lax.axis_size(axis) // 2
    while bit:
        held = held + [swap(h, axis, bit) for h in held]
        bit //= 2
    return held


def tree(terms, op=jnp.add):
    while len(terms) > 1:
        half = len(terms) // 2
        rest = terms[2 * half :]
        terms = [op(terms[i], terms[i + half]) for i in range(half)] + rest
    return terms[0]


def three_parts(x):
    hi = x.astype(bf16).astype(f32)
    mid = (x - hi).astype(bf16).astype(f32)
    return hi, mid, x - hi - mid


def lanes(rows):
    return lax.broadcasted_iota(i32, (rows, LANES), 1)


def attend_kernel(n_seq, scal, *refs):
    q_refs = refs[:n_seq]
    k_ref, v_ref, o_ref, q_out, q_twice = refs[n_seq:]
    tgt_rows = q_refs[0].shape[1]
    rows = tgt_rows * n_seq
    enc, features = k_ref.shape[1:]
    for i, r in enumerate(q_refs):
        for at in (i * tgt_rows, rows + i * tgt_rows):
            q_twice[at : at + tgt_rows, :] = r[0]
    q = q_twice[pl.ds(pl.multiple_of(scal[0], 16), rows), :]
    q_out[...] = q
    valid = lax.broadcasted_iota(i32, (rows, enc), 1) < scal[1]
    lane = lanes(rows)
    stat = jnp.zeros((rows, LANES), f32)
    for h in range(features // HDIM):
        at = slice(h * HDIM, (h + 1) * HDIM)
        scores = dot(q[:, at], k_ref[0, :, at], 1, 1) * score_scale
        scores = jnp.where(valid, scores, LOW)
        peak = jnp.max(scores, axis=1, keepdims=True)
        e = jnp.where(valid, jnp.exp(scores - peak), 0.0)
        total = jnp.sum(e, axis=1, keepdims=True)
        some = total > 0.0
        safe = jnp.where(some, total, 1.0)
        o = dot(e.astype(bf16), v_ref[0, :, at], 1, 0) / safe
        o_ref[:, at] = o.astype(bf16)
        lse = jnp.where(some, peak + jnp.log(safe), LOW)
        for i, part in enumerate(three_parts(lse)):
            stat = jnp.where(lane == 3 * h + i, part, stat)
    o_ref[:, features:] = stat.astype(bf16)


def project_kernel(n_seq, own_rows, *refs):
    o_refs = refs[:n_seq]
    p_ref, mixed_ref, own_ref, att_ref, lse_ref, att = refs[n_seq:]
    rows, features = att.shape

    @pl.when(pl.program_id(0) == 0)
    def _():
        stats = [r[:, features:].astype(f32) for r in o_refs]
        lane = lanes(rows)
        lse_all = jnp.zeros((rows, LANES), f32)
        for h in range(features // HDIM):
            at = slice(h * HDIM, (h + 1) * HDIM)
            lses = [
                s[:, 3 * h : 3 * h + 1] + s[:, 3 * h + 1 : 3 * h + 2] + s[:, 3 * h + 2 : 3 * h + 3]
                for s in stats
            ]
            top = tree(lses, jnp.maximum)
            lse = top + jnp.log(tree([jnp.exp(x - top) for x in lses]))
            o = tree([jnp.exp(x - lse) * r[:, at].astype(f32) for x, r in zip(lses, o_refs)])
            att[:, at] = o.astype(bf16)
            lse_all = jnp.where(lane == h, lse, lse_all)
        att_ref[...] = att[...]
        lse_ref[...] = lse_all

    part = dot(att[...], p_ref[...], 1, 0)
    mixed_ref[...] = part.astype(bf16)
    own_ref[...] = part[:own_rows]


def norm_kernel(n_got, scal, *refs):
    own_ref, got_refs = refs[0], refs[1 : 1 + n_got]
    residual_ref, gain_ref, mixed_ref, ng_ref = refs[1 + n_got :]
    rows, width = own_ref.shape
    res = residual_ref[0, pl.ds(pl.multiple_of(scal[2], 16), rows), :].astype(f32)
    mixed = own_ref[...] + res
    for r in got_refs:
        mixed = mixed + r[...].astype(f32)
    mixed_ref[...] = mixed
    ng_ref[:, :width] = (mixed * gain_ref[...]).astype(bf16)
    square = jnp.sum(mixed * mixed, axis=1, keepdims=True)
    lane = lanes(rows)
    stat = jnp.zeros((rows, LANES), f32)
    for i, part in enumerate(three_parts(square)):
        stat = jnp.where(lane == i, part, stat)
    ng_ref[:, width:] = stat.astype(bf16)


def logits_kernel(first, cols, ng_ref, w_ref, code_ref, stat_ref, z):
    j = pl.program_id(0)
    rows, width = z.shape[0], w_ref.shape[0]
    part = dot(ng_ref[:, :width], w_ref[...], 1, 0)
    if first + z.shape[1] > cols:
        at = first + j * TILE + lax.broadcasted_iota(i32, part.shape, 1)
        part = jnp.where(at < cols, part, 0.0)
    z[:, pl.ds(pl.multiple_of(j * TILE, TILE), TILE)] = part

    @pl.when(j == pl.num_programs(0) - 1)
    def _():
        val = z[...]
        peak = jnp.maximum(jnp.max(jnp.abs(val), axis=1, keepdims=True), 1e-30)
        code_ref[...] = jnp.round(val * (CODE_TOP / peak)).astype(i32).astype(jnp.int16)
        s = ng_ref[:, width:].astype(f32)
        square = s[:, 0:1] + s[:, 1:2] + s[:, 2:3]
        lane = lanes(rows)
        stat_ref[...] = jnp.where(lane == 0, peak / CODE_TOP, jnp.where(lane == 1, square, 0.0))


def hidden_kernel(chunk, first, cols, n_seq, features, scal, *refs):
    code_refs, sc_refs = refs[:n_seq], refs[n_seq : 2 * n_seq]
    refs = refs[2 * n_seq :]
    if chunk:
        tgt_ref, w_ref, acc_prev, st_prev, acc_ref, e_ref, st_ref, lhs = refs
    else:
        tgt_ref, w_ref, acc_ref, e_ref, st_ref, lhs = refs
    j = pl.program_id(0)
    rows, size = e_ref.shape
    partial_cols = first + size > cols

    @pl.when(j == 0)
    def _():
        z = tree([c[...].astype(i32).astype(f32) * s[:, 0:1] for c, s in zip(code_refs, sc_refs)])
        square = tree([s[:, 1:2] for s in sc_refs])
        inv = lax.rsqrt(square / features + norm_epsilon)
        z = z * inv
        at = first + lax.broadcasted_iota(i32, (rows, size), 1)
        hit = at == tgt_ref[:, 0:1]
        if partial_cols:
            z = jnp.where(at < cols, z, LOW)
            hit = hit & (at < cols)
        here = jnp.sum(jnp.where(hit, z, 0.0), axis=1, keepdims=True)
        peak = jnp.max(z, axis=1, keepdims=True)
        if chunk:
            old = st_prev[...]
            peak = jnp.maximum(peak, old[:, 0:1])
            fade = jnp.exp(old[:, 0:1] - peak)
            acc_ref[:rows, :] = acc_prev[:rows, :] * fade
            acc_ref[rows:, :] = acc_prev[rows:, :]
        else:
            old = jnp.zeros((rows, LANES), f32)
            fade = 0.0
            acc_ref[...] = jnp.zeros_like(acc_ref)
        e = jnp.exp(z - peak)
        total = jnp.sum(e, axis=1, keepdims=True) + old[:, 1:2] * fade
        eh = e.astype(bf16)
        e_ref[...] = eh
        lhs[:rows, :] = eh
        lhs[rows:, :] = hit.astype(f32).astype(bf16)
        lane = lanes(rows)
        st = jnp.where(lane == 0, peak, old)
        st = jnp.where(lane == 1, total, st)
        st = jnp.where(lane == 2, here + old[:, 2:3], st)
        st = jnp.where(lane == 3, inv, st)
        st_ref[...] = jnp.where(lane == 8 + chunk, peak, st)

    w = w_ref[...]
    if partial_cols:
        at = first + j * TILE + lax.broadcasted_iota(i32, (1, TILE), 1)
        w = jnp.where(at < cols, w, jnp.zeros_like(w))
    left = lhs[:, pl.ds(pl.multiple_of(j * TILE, TILE), TILE)]
    acc_ref[...] += dot(left, w, 1, 1)


def total_kernel(n_vocab, own_rows, *refs):
    st_refs = refs[:n_vocab]
    acc_ref, part_ref, own_ref, coef_ref, loss_ref = refs[n_vocab:]
    rows = coef_ref.shape[0]
    mine = st_refs[0][...]
    stats = [mine]
    for k in range(1, n_vocab):
        s = st_refs[k][...]
        cut = rows - k * own_rows
        stats.append(jnp.concatenate([s[cut:], s[:cut]], axis=0))
    top = tree([s[:, 0:1] for s in stats], jnp.maximum)
    total = tree([s[:, 1:2] * jnp.exp(s[:, 0:1] - top) for s in stats])
    hit_logit = tree([s[:, 2:3] for s in stats])
    log_total = top + jnp.log(total)
    loss = log_total - hit_logit + zloss_weight * log_total * log_total
    loss_ref[...] = jnp.broadcast_to(jnp.sum(loss, axis=0, keepdims=True), loss_ref.shape)
    lift = 1.0 + 2.0 * zloss_weight * log_total
    inv = mine[:, 3:4]
    lane = lanes(rows)
    coef_ref[...] = jnp.where(lane >= 8, jnp.exp(jnp.minimum(mine - log_total, 30.0)) * lift * inv, inv)
    scale = jnp.exp(mine[:, 0:1] - log_total) * lift
    part = acc_ref[:rows, :] * scale - acc_ref[rows:, :]
    part_ref[...] = part.astype(bf16)
    own_ref[...] = part[:own_rows]


def grad_kernel(firsts, cols, coef_ref, tgt_ref, *refs):
    n = len(firsts)
    for c, first in enumerate(firsts):
        e_ref, g_ref = refs[c], refs[n + c]
        at = first + lax.broadcasted_iota(i32, e_ref.shape, 1)
        hit = at == tgt_ref[:, 0:1]
        inv = coef_ref[:, 0:1]
        g = e_ref[...].astype(f32) * coef_ref[:, 8 + c : 9 + c] - jnp.where(hit, inv, 0.0)
        g_ref[...] = g.astype(bf16)


def head_kernel(n_dp, has_prev, ng_ref, *refs):
    g_refs = refs[:n_dp]
    out_ref = refs[-1]
    g = jnp.concatenate([r[...] for r in g_refs], axis=0)
    width = out_ref.shape[0]
    step = min(width, 512)
    for at in range(0, width, step):
        out_ref[at : at + step, :] = dot(ng_ref[at : at + step, :], g, 1, 0).astype(bf16)


def gate_kernel(n_got, *refs):
    own_ref, got_refs = refs[0], refs[1 : 1 + n_got]
    mixed_ref, gain_ref, gated_ref, dot_ref = refs[1 + n_got :]
    total = own_ref[...]
    for r in got_refs:
        total = total + r[...].astype(f32)
    gated = total * gain_ref[...]
    gated_ref[...] = gated
    inner = jnp.sum(gated * mixed_ref[...], axis=1, keepdims=True)
    dot_ref[...] = jnp.broadcast_to(inner, dot_ref.shape)


def mixed_grad_kernel(n_seq, features, gated_ref, mixed_ref, coef_ref, *refs):
    dot_refs, out_ref = refs[:n_seq], refs[n_seq]
    rows = out_ref.shape[0]
    inner = tree([r[:, 0:1] for r in dot_refs])
    inv = coef_ref[:rows, 0:1]
    out = gated_ref[...] * inv - mixed_ref[...] * (inv * inv * inv * inner / features)
    out_ref[...] = out.astype(bf16)


def back_project_kernel(mg_ref, p_ref, out_ref):
    out_ref[...] = dot(mg_ref[...], p_ref[...], 1, 1).astype(bf16)


def attend_back_kernel(n_seq, scal, *refs):
    a_refs = refs[:n_seq]
    q_ref, k_ref, v_ref, att_ref, lse_ref, kg_ref, vg_ref = refs[n_seq:]
    enc, features = k_ref.shape[1:]
    rows = q_ref.shape[0]
    valid = lax.broadcasted_iota(i32, (rows, enc), 1) < scal[1]
    for h in range(features // HDIM):
        at = slice(h * HDIM, (h + 1) * HDIM)
        grad = tree([r[:, at].astype(f32) for r in a_refs]).astype(bf16)
        q = q_ref[:, at]
        scores = dot(q, k_ref[0, :, at], 1, 1) * score_scale
        w = jnp.where(valid, jnp.exp(jnp.minimum(scores - lse_ref[:, h : h + 1], 0.5)), 0.0)
        prob_grad = dot(grad, v_ref[0, :, at], 1, 1)
        inner = jnp.sum(grad.astype(f32) * att_ref[:, at].astype(f32), axis=1, keepdims=True)
        sg = (w * (prob_grad - inner) * score_scale).astype(bf16)
        vg_ref[0, :, at] = dot(w.astype(bf16), grad, 0, 0)
        kg_ref[0, :, at] = dot(sg, q, 0, 0)


def body(
    queries, enc_keys, enc_values, enc_lengths, out_proj, residual, norm_gain, head_weight, targets
):
    n_seq, n_vocab, n_dp = lax.axis_size("seq"), lax.axis_size("vocab"), lax.axis_size("dp")
    seq, voc = lax.axis_index("seq"), lax.axis_index("vocab")
    tgt_rows, features = queries.shape[1:]
    enc = enc_keys.shape[1]
    rows = tgt_rows * n_seq
    own_rows = rows // n_vocab
    width, cols = head_weight.shape
    full_width = width * n_seq
    tiles = -(-cols // TILE)
    per = -(-tiles // MAX_CHUNKS)
    chunks = [(t, min(per, tiles - t)) for t in range(0, tiles, per)]
    firsts = [t * TILE for t, _ in chunks]
    gain = norm_gain.reshape(1, width)

    start = lax.rem(voc * own_rows - seq * tgt_rows + rows, rows).astype(i32)
    scal = jnp.stack(
        [start, enc_lengths[0] - seq * enc, voc * own_rows, voc * cols]
    ).astype(i32)

    q_parts = gather_ring(queries, "seq")
    tgt_parts = gather_ring(targets.reshape(tgt_rows), "seq")
    tgt_twice = jnp.concatenate(tgt_parts + tgt_parts)
    tgt = lax.dynamic_slice(tgt_twice, (start,), (rows,)) - voc * cols
    tgt = jnp.broadcast_to(tgt[:, None], (rows, LANES))

    o_part, q_all = pl.pallas_call(
        functools.partial(attend_kernel, n_seq),
        out_shape=[sds((rows, features + LANES), bf16), sds((rows, features), bf16)],
        in_specs=[SMEM] + [VMEM] * (n_seq + 2),
        out_specs=[VMEM, VMEM],
        scratch_shapes=[pltpu.VMEM((2 * rows, features), bf16)],
        compiler_params=params(),
        name="attend",
    )(scal, *q_parts, enc_keys, enc_values)

    o_all = gather_ring(o_part, "seq")
    ptile = min(TILE, width)
    whole = lambda shape: pl.BlockSpec(shape, lambda j: (0, 0))
    mixed_part, mixed_own, att, lse = pl.pallas_call(
        functools.partial(project_kernel, n_seq, own_rows),
        grid=(width // ptile,),
        out_shape=[
            sds((rows, width), bf16),
            sds((own_rows, width), f32),
            sds((rows, features), bf16),
            sds((rows, LANES), f32),
        ],
        in_specs=[whole((rows, features + LANES))] * n_seq
        + [pl.BlockSpec((features, ptile), lambda j: (0, j))],
        out_specs=[
            pl.BlockSpec((rows, ptile), lambda j: (0, j)),
            pl.BlockSpec((own_rows, ptile), lambda j: (0, j)),
            whole((rows, features)),
            whole((rows, LANES)),
        ],
        scratch_shapes=[pltpu.VMEM((rows, features), bf16)],
        compiler_params=params(),
        name="project",
    )(*o_all, out_proj)

    got = scatter_ring(mixed_part, "vocab", own_rows)
    mixed, ng_own = pl.pallas_call(
        functools.partial(norm_kernel, len(got)),
        out_shape=[sds((own_rows, width), f32), sds((own_rows, width + LANES), bf16)],
        in_specs=[SMEM] + [VMEM] * (len(got) + 3),
        out_specs=[VMEM, VMEM],
        compiler_params=params(),
        name="norm",
    )(scal, mixed_own, *got, residual, gain)
    ng = jnp.concatenate(gather_ring(ng_own, "vocab"), axis=0)

    ng_dp = gather_swaps(ng[:, :width], "dp")
    ng_turned = jnp.concatenate(ng_dp, axis=0).T

    codes, stats = [], []
    for tile0, n in chunks:
        size = n * TILE
        code, stat = pl.pallas_call(
            functools.partial(logits_kernel, tile0 * TILE, cols),
            grid=(n,),
            out_shape=[sds((rows, size), jnp.int16), sds((rows, LANES), f32)],
            in_specs=[
                whole((rows, width + LANES)),
                pl.BlockSpec((width, TILE), lambda j, t=tile0: (0, t + j)),
            ],
            out_specs=[whole((rows, size)), whole((rows, LANES))],
            scratch_shapes=[pltpu.VMEM((rows, size), f32)],
            compiler_params=params(),
            cost_estimate=cost(2 * 256 * width * size, 2 * width * size),
            name="logits",
        )(ng, head_weight)
        codes.append(gather_ring(code, "seq"))
        stats.append(gather_ring(stat, "seq"))

    acc = st = None
    exps = []
    for c, (tile0, n) in enumerate(chunks):
        size = n * TILE
        prev = [acc, st] if c else []
        acc, e, st = pl.pallas_call(
            functools.partial(hidden_kernel, c, tile0 * TILE, cols, n_seq, full_width),
            grid=(n,),
            out_shape=[sds((2 * rows, width), f32), sds((rows, size), bf16), sds((rows, LANES), f32)],
            in_specs=[SMEM]
            + [whole((rows, size))] * n_seq
            + [whole((rows, LANES))] * (n_seq + 1)
            + [pl.BlockSpec((width, TILE), lambda j, t=tile0: (0, t + j))]
            + ([whole((2 * rows, width)), whole((rows, LANES))] if c else []),
            out_specs=[whole((2 * rows, width)), whole((rows, size)), whole((rows, LANES))],
            scratch_shapes=[pltpu.VMEM((2 * rows, size), bf16)],
            compiler_params=params(),
            cost_estimate=cost(2 * 256 * width * size, 2 * width * size),
            name="hidden",
        )(scal, *codes[c], *stats[c], tgt, head_weight, *prev)
        exps.append(e)

    st_all = gather_ring(st, "vocab")
    hidden_part, hidden_own, coef, loss = pl.pallas_call(
        functools.partial(total_kernel, n_vocab, own_rows),
        out_shape=[
            sds((rows, width), bf16),
            sds((own_rows, width), f32),
            sds((rows, LANES), f32),
            sds((8, LANES), f32),
        ],
        in_specs=[VMEM] * (n_vocab + 1),
        out_specs=[VMEM] * 4,
        compiler_params=params(),
        name="total",
    )(*st_all, acc)
    got = scatter_ring(hidden_part, "vocab", own_rows)

    grads = pl.pallas_call(
        functools.partial(grad_kernel, firsts, cols),
        out_shape=[sds(e.shape, bf16) for e in exps],
        in_specs=[VMEM] * (2 + len(exps)),
        out_specs=[VMEM] * len(exps),
        compiler_params=params(),
        name="logit_grad",
    )(coef, tgt, *exps)
    bit = n_dp // 2
    while bit:
        loss = loss + swap(loss, "dp", bit)
        bit //= 2
    mean_loss = loss[0, 0] / (n_dp * rows)

    gated, inner = pl.pallas_call(
        functools.partial(gate_kernel, len(got)),
        out_shape=[sds((own_rows, width), f32), sds((own_rows, LANES), f32)],
        in_specs=[VMEM] * (len(got) + 3),
        out_specs=[VMEM, VMEM],
        compiler_params=params(),
        name="gate",
    )(hidden_own, *got, mixed, gain)
    inner_all = gather_ring(inner, "seq")
    mixed_grad = pl.pallas_call(
        functools.partial(mixed_grad_kernel, n_seq, full_width),
        out_shape=sds((own_rows, width), bf16),
        in_specs=[VMEM] * (3 + n_seq),
        out_specs=VMEM,
        compiler_params=params(),
        name="mixed_grad",
    )(gated, mixed, coef, *inner_all)
    mg = jnp.concatenate(gather_ring(mixed_grad, "vocab"), axis=0)

    ftile = min(256, features)
    back_part = pl.pallas_call(
        back_project_kernel,
        grid=(features // ftile,),
        out_shape=sds((rows, features), bf16),
        in_specs=[whole((rows, width)), pl.BlockSpec((ftile, width), lambda j: (j, 0))],
        out_specs=pl.BlockSpec((rows, ftile), lambda j: (0, j)),
        compiler_params=params(),
        name="back_project",
    )(mg, out_proj)
    back_all = gather_ring(back_part, "seq")
    key_grad, value_grad = pl.pallas_call(
        functools.partial(attend_back_kernel, n_seq),
        out_shape=[sds(enc_keys.shape, f32), sds(enc_values.shape, f32)],
        in_specs=[SMEM] + [VMEM] * (n_seq + 5),
        out_specs=[VMEM, VMEM],
        compiler_params=params(),
        name="attend_back",
    )(scal, *back_all, q_all, enc_keys, enc_values, att, lse)

    head = None
    for c, (tile0, n) in enumerate(chunks):
        g_all = gather_swaps(grads[c], "dp")
        place = pl.BlockSpec((width, TILE), lambda j, t=tile0: (0, t + j))
        prev = [head] if c else []
        head = pl.pallas_call(
            functools.partial(head_kernel, n_dp, bool(c)),
            grid=(n,),
            out_shape=sds((width, cols), bf16),
            in_specs=[whole((width, n_dp * rows))]
            + [pl.BlockSpec((rows, TILE), lambda j: (0, j))] * n_dp
            + [pl.BlockSpec(memory_space=pl.ANY)] * len(prev),
            out_specs=place,
            input_output_aliases={1 + n_dp: 0} if c else {},
            compiler_params=params(),
            cost_estimate=cost(2 * n_dp * rows * width * n * TILE, 2 * width * n * TILE),
            name="head_grad",
        )(ng_turned, *g_all, *prev)
    return (mean_loss, head, key_grad, value_grad)


def solution(mesh):
    placed = (
        P("dp", "seq", "vocab"),
        P("dp", "seq", "vocab"),
        P("dp", "seq", "vocab"),
        P("dp"),
        P("vocab", "seq"),
        P("dp", None, "seq"),
        P("seq"),
        P("seq", "vocab"),
        P("dp", "seq"),
    )
    return jax.shard_map(
        body,
        mesh=mesh,
        in_specs=placed,
        out_specs=(P(), P("seq", "vocab"), P("dp", "seq", "vocab"), P("dp", "seq", "vocab")),
        check_vma=False,
    )
```

```python
import functools
import jax
import jax.numpy as jnp
from jax import lax
from jax.experimental import pallas as pl
from jax.experimental.pallas import tpu as pltpu
from jax.sharding import PartitionSpec as P

HDIM = 256
LANES = 128
TILE = 512
MAX_CHUNKS = 3
LOW = -1e30
CODE_TOP = 32767.0

zloss_weight = 0.0001
norm_epsilon = 1e-06
score_scale = HDIM ** (-0.5)
f32, bf16, i32 = jnp.float32, jnp.bfloat16, jnp.int32

VMEM = pl.BlockSpec(memory_space=pltpu.VMEM)
SMEM = pl.BlockSpec(memory_space=pltpu.SMEM)


def sds(shape, dtype):
    return jax.ShapeDtypeStruct(shape, dtype)


def params(mib=40):
    return pltpu.CompilerParams(vmem_limit_bytes=mib * 1024 * 1024)


def cost(flops, nbytes):
    return pl.CostEstimate(flops=int(flops), bytes_accessed=int(nbytes), transcendentals=0)


def dot(a, b, ca, cb):
    return lax.dot_general(a, b, (((ca,), (cb,)), ((), ())), preferred_element_type=f32)


def from_ahead(x, axis, k):
    n = lax.axis_size(axis)
    return lax.ppermute(x, axis, [((i + k) % n, i) for i in range(n)])


def gather_ring(x, axis):
    return [x] + [from_ahead(x, axis, k) for k in range(1, lax.axis_size(axis))]


def gather_rows(x, axis):
    return lax.all_gather(x, axis, axis=0, tiled=True)


def exchange_rows(x, axis):
    return lax.all_to_all(x, axis, split_axis=0, concat_axis=0, tiled=True)


def swap(x, axis, bit):
    n = lax.axis_size(axis)
    return lax.ppermute(x, axis, [(i, i ^ bit) for i in range(n)])


def gather_swaps(x, axis):
    held = [x]
    bit = lax.axis_size(axis) // 2
    while bit:
        held = held + [swap(h, axis, bit) for h in held]
        bit //= 2
    return held


def tree(terms, op=jnp.add):
    while len(terms) > 1:
        half = len(terms) // 2
        rest = terms[2 * half :]
        terms = [op(terms[i], terms[i + half]) for i in range(half)] + rest
    return terms[0]


def three_parts(x):
    hi = x.astype(bf16).astype(f32)
    mid = (x - hi).astype(bf16).astype(f32)
    return hi, mid, x - hi - mid


def lanes(rows):
    return lax.broadcasted_iota(i32, (rows, LANES), 1)


def attend_kernel(n_seq, scal, *refs):
    q_refs = refs[:n_seq]
    k_ref, v_ref, o_ref, q_out, q_twice = refs[n_seq:]
    tgt_rows = q_refs[0].shape[1]
    rows = tgt_rows * n_seq
    enc, features = k_ref.shape[1:]
    for i, r in enumerate(q_refs):
        for at in (i * tgt_rows, rows + i * tgt_rows):
            q_twice[at : at + tgt_rows, :] = r[0]
    q = q_twice[pl.ds(pl.multiple_of(scal[0], 16), rows), :]
    q_out[...] = q
    valid = lax.broadcasted_iota(i32, (rows, enc), 1) < scal[1]
    lane = lanes(rows)
    stat = jnp.zeros((rows, LANES), f32)
    for h in range(features // HDIM):
        at = slice(h * HDIM, (h + 1) * HDIM)
        scores = dot(q[:, at], k_ref[0, :, at], 1, 1) * score_scale
        scores = jnp.where(valid, scores, LOW)
        peak = jnp.max(scores, axis=1, keepdims=True)
        e = jnp.where(valid, jnp.exp(scores - peak), 0.0)
        total = jnp.sum(e, axis=1, keepdims=True)
        some = total > 0.0
        safe = jnp.where(some, total, 1.0)
        o = dot(e.astype(bf16), v_ref[0, :, at], 1, 0) / safe
        o_ref[:, at] = o.astype(bf16)
        lse = jnp.where(some, peak + jnp.log(safe), LOW)
        for i, part in enumerate(three_parts(lse)):
            stat = jnp.where(lane == 3 * h + i, part, stat)
    o_ref[:, features:] = stat.astype(bf16)


def project_kernel(n_seq, *refs):
    o_refs = refs[:n_seq]
    p_ref, mixed_ref, att_ref, lse_ref, att = refs[n_seq:]
    rows, features = att.shape

    @pl.when(pl.program_id(0) == 0)
    def _():
        stats = [r[:, features:].astype(f32) for r in o_refs]
        lane = lanes(rows)
        lse_all = jnp.zeros((rows, LANES), f32)
        for h in range(features // HDIM):
            at = slice(h * HDIM, (h + 1) * HDIM)
            lses = [
                s[:, 3 * h : 3 * h + 1] + s[:, 3 * h + 1 : 3 * h + 2] + s[:, 3 * h + 2 : 3 * h + 3]
                for s in stats
            ]
            top = tree(lses, jnp.maximum)
            lse = top + jnp.log(tree([jnp.exp(x - top) for x in lses]))
            o = tree([jnp.exp(x - lse) * r[:, at].astype(f32) for x, r in zip(lses, o_refs)])
            att[:, at] = o.astype(bf16)
            lse_all = jnp.where(lane == h, lse, lse_all)
        att_ref[...] = att[...]
        lse_ref[...] = lse_all

    mixed_ref[...] = dot(att[...], p_ref[...], 1, 0).astype(bf16)


def block_sum(ref, rows):
    n = ref.shape[0] // rows
    return tree([ref[i * rows : (i + 1) * rows, :].astype(f32) for i in range(n)])


def norm_kernel(scal, got_ref, residual_ref, gain_ref, mixed_ref, ng_ref):
    rows, width = mixed_ref.shape
    res = residual_ref[0, pl.ds(pl.multiple_of(scal[2], 16), rows), :].astype(f32)
    mixed = res + block_sum(got_ref, rows)
    mixed_ref[...] = mixed
    ng_ref[:, :width] = (mixed * gain_ref[...]).astype(bf16)
    square = jnp.sum(mixed * mixed, axis=1, keepdims=True)
    lane = lanes(rows)
    stat = jnp.zeros((rows, LANES), f32)
    for i, part in enumerate(three_parts(square)):
        stat = jnp.where(lane == i, part, stat)
    ng_ref[:, width:] = stat.astype(bf16)


def logits_kernel(first, cols, ng_ref, w_ref, code_ref, stat_ref, z):
    j = pl.program_id(0)
    rows, width = z.shape[0], w_ref.shape[1]
    part = dot(ng_ref[:, :width], w_ref[...], 1, 1)
    if first + z.shape[1] > cols:
        at = first + j * TILE + lax.broadcasted_iota(i32, part.shape, 1)
        part = jnp.where(at < cols, part, 0.0)
    z[:, pl.ds(pl.multiple_of(j * TILE, TILE), TILE)] = part

    @pl.when(j == pl.num_programs(0) - 1)
    def _():
        val = z[...]
        peak = jnp.maximum(jnp.max(jnp.abs(val), axis=1, keepdims=True), 1e-30)
        code_ref[...] = jnp.round(val * (CODE_TOP / peak)).astype(i32).astype(jnp.int16)
        s = ng_ref[:, width:].astype(f32)
        square = s[:, 0:1] + s[:, 1:2] + s[:, 2:3]
        lane = lanes(rows)
        stat_ref[...] = jnp.where(lane == 0, peak / CODE_TOP, jnp.where(lane == 1, square, 0.0))


def hidden_kernel(chunk, first, cols, n_seq, features, scal, *refs):
    code_refs, sc_refs = refs[:n_seq], refs[n_seq : 2 * n_seq]
    refs = refs[2 * n_seq :]
    if chunk:
        tgt_ref, w_ref, acc_prev, st_prev, acc_ref, e_ref, st_ref, lhs = refs
    else:
        tgt_ref, w_ref, acc_ref, e_ref, st_ref, lhs = refs
    j = pl.program_id(0)
    rows, size = e_ref.shape
    partial_cols = first + size > cols

    @pl.when(j == 0)
    def _():
        z = tree([c[...].astype(i32).astype(f32) * s[:, 0:1] for c, s in zip(code_refs, sc_refs)])
        square = tree([s[:, 1:2] for s in sc_refs])
        inv = lax.rsqrt(square / features + norm_epsilon)
        z = z * inv
        at = first + lax.broadcasted_iota(i32, (rows, size), 1)
        hit = at == tgt_ref[:, 0:1]
        if partial_cols:
            z = jnp.where(at < cols, z, LOW)
            hit = hit & (at < cols)
        here = jnp.sum(jnp.where(hit, z, 0.0), axis=1, keepdims=True)
        peak = jnp.max(z, axis=1, keepdims=True)
        if chunk:
            old = st_prev[...]
            peak = jnp.maximum(peak, old[:, 0:1])
            fade = jnp.exp(old[:, 0:1] - peak)
            acc_ref[:rows, :] = acc_prev[:rows, :] * fade
            acc_ref[rows:, :] = acc_prev[rows:, :]
        else:
            old = jnp.zeros((rows, LANES), f32)
            fade = 0.0
            acc_ref[...] = jnp.zeros_like(acc_ref)
        e = jnp.exp(z - peak)
        total = jnp.sum(e, axis=1, keepdims=True) + old[:, 1:2] * fade
        eh = e.astype(bf16)
        e_ref[...] = eh
        lhs[:rows, :] = eh
        lhs[rows:, :] = hit.astype(f32).astype(bf16)
        lane = lanes(rows)
        st = jnp.where(lane == 0, peak, old)
        st = jnp.where(lane == 1, total, st)
        st = jnp.where(lane == 2, here + old[:, 2:3], st)
        st = jnp.where(lane == 3, inv, st)
        st_ref[...] = jnp.where(lane == 8 + chunk, peak, st)

    w = w_ref[...]
    if partial_cols:
        at = first + j * TILE + lax.broadcasted_iota(i32, (TILE, 1), 0)
        w = jnp.where(at < cols, w, jnp.zeros_like(w))
    left = lhs[:, pl.ds(pl.multiple_of(j * TILE, TILE), TILE)]
    acc_ref[...] += dot(left, w, 1, 0)


def total_kernel(n_vocab, st_ref, st_all_ref, acc_ref, part_ref, coef_ref):
    rows = coef_ref.shape[0]
    mine = st_ref[...]
    stats = [st_all_ref[k * rows : (k + 1) * rows, :] for k in range(n_vocab)]
    top = tree([s[:, 0:1] for s in stats], jnp.maximum)
    total = tree([s[:, 1:2] * jnp.exp(s[:, 0:1] - top) for s in stats])
    hit_logit = tree([s[:, 2:3] for s in stats])
    log_total = top + jnp.log(total)
    loss = log_total - hit_logit + zloss_weight * log_total * log_total
    lift = 1.0 + 2.0 * zloss_weight * log_total
    inv = mine[:, 3:4]
    lane = lanes(rows)
    coef = jnp.exp(jnp.minimum(mine - log_total, 30.0)) * lift * inv
    coef = jnp.where(lane >= 8, coef, inv)
    coef_ref[...] = jnp.where(lane == 1, loss, coef)
    scale = jnp.exp(mine[:, 0:1] - log_total) * lift
    part = acc_ref[:rows, :] * scale - acc_ref[rows:, :]
    part_ref[...] = part.astype(bf16)


def grad_kernel(firsts, cols, coef_ref, tgt_ref, *refs):
    n = len(firsts)
    for c, first in enumerate(firsts):
        e_ref, g_ref = refs[c], refs[n + c]
        at = first + lax.broadcasted_iota(i32, e_ref.shape, 1)
        hit = at == tgt_ref[:, 0:1]
        inv = coef_ref[:, 0:1]
        g = e_ref[...].astype(f32) * coef_ref[:, 8 + c : 9 + c] - jnp.where(hit, inv, 0.0)
        g_ref[...] = g.astype(bf16)
    last = refs[-1]
    rows, size = last.shape
    lane = lanes(rows)
    stat = last[:, size - LANES :].astype(f32)
    for i, part in enumerate(three_parts(coef_ref[:, 1:2])):
        stat = jnp.where(lane == LANES - 3 + i, part, stat)
    last[:, size - LANES :] = stat.astype(bf16)


def loss_kernel(rows_all, *refs):
    sums = []
    for r in refs[:-1]:
        s = r[...].astype(f32)
        sums.append(jnp.sum(s[:, -3:-2] + s[:, -2:-1] + s[:, -1:], axis=0, keepdims=True))
    refs[-1][...] = jnp.broadcast_to(tree(sums) / rows_all, refs[-1].shape)


def head_kernel(n_dp, *refs):
    ng_refs, g_refs = refs[:n_dp], refs[n_dp : 2 * n_dp]
    out_ref, ng = refs[-2], refs[-1]
    rows, width = ng_refs[0].shape[0], out_ref.shape[1]

    @pl.when(pl.program_id(0) == 0)
    def _():
        for i, r in enumerate(ng_refs):
            ng[i * rows : (i + 1) * rows, :] = r[:, :width]

    g = jnp.concatenate([r[...] for r in g_refs], axis=0)
    for at in range(0, TILE, 256):
        out_ref[at : at + 256, :] = dot(g[:, at : at + 256], ng[...], 0, 0).astype(bf16)


def gate_kernel(got_ref, mixed_ref, gain_ref, gated_ref, dot_ref):
    gated = block_sum(got_ref, mixed_ref.shape[0]) * gain_ref[...]
    gated_ref[...] = gated
    inner = jnp.sum(gated * mixed_ref[...], axis=1, keepdims=True)
    dot_ref[...] = jnp.broadcast_to(inner, dot_ref.shape)


def mixed_grad_kernel(n_seq, features, scal, gated_ref, mixed_ref, coef_ref, *refs):
    dot_refs, out_ref = refs[:n_seq], refs[n_seq]
    rows = out_ref.shape[0]
    inner = tree([r[:, 0:1] for r in dot_refs])
    inv = coef_ref[pl.ds(pl.multiple_of(scal[2], 16), rows), :][:, 0:1]
    out = gated_ref[...] * inv - mixed_ref[...] * (inv * inv * inv * inner / features)
    out_ref[...] = out.astype(bf16)


def back_project_kernel(mg_ref, p_ref, out_ref):
    out_ref[...] = dot(mg_ref[...], p_ref[...], 1, 1).astype(bf16)


def attend_back_kernel(n_seq, scal, *refs):
    a_refs = refs[:n_seq]
    q_ref, k_ref, v_ref, att_ref, lse_ref, kg_ref, vg_ref = refs[n_seq:]
    enc, features = k_ref.shape[1:]
    rows = q_ref.shape[0]
    valid = lax.broadcasted_iota(i32, (rows, enc), 1) < scal[1]
    for h in range(features // HDIM):
        at = slice(h * HDIM, (h + 1) * HDIM)
        grad = tree([r[:, at].astype(f32) for r in a_refs]).astype(bf16)
        q = q_ref[:, at]
        scores = dot(q, k_ref[0, :, at], 1, 1) * score_scale
        w = jnp.where(valid, jnp.exp(jnp.minimum(scores - lse_ref[:, h : h + 1], 0.5)), 0.0)
        prob_grad = dot(grad, v_ref[0, :, at], 1, 1)
        inner = jnp.sum(grad.astype(f32) * att_ref[:, at].astype(f32), axis=1, keepdims=True)
        sg = (w * (prob_grad - inner) * score_scale).astype(bf16)
        vg_ref[0, :, at] = dot(w.astype(bf16), grad, 0, 0)
        kg_ref[0, :, at] = dot(sg, q, 0, 0)


def body(
    queries, enc_keys, enc_values, enc_lengths, out_proj, residual, norm_gain, head_weight, targets
):
    n_seq, n_vocab, n_dp = lax.axis_size("seq"), lax.axis_size("vocab"), lax.axis_size("dp")
    seq, voc = lax.axis_index("seq"), lax.axis_index("vocab")
    tgt_rows, features = queries.shape[1:]
    enc = enc_keys.shape[1]
    rows = tgt_rows * n_seq
    own_rows = rows // n_vocab
    width, cols = head_weight.shape
    full_width = width * n_seq
    tiles = -(-cols // TILE)
    per = -(-tiles // MAX_CHUNKS)
    chunks = [(t, min(per, tiles - t)) for t in range(0, tiles, per)]
    firsts = [t * TILE for t, _ in chunks]
    gain = norm_gain.reshape(1, width)
    weight = head_weight.T

    start = lax.rem(rows - seq * tgt_rows, rows).astype(i32)
    scal = jnp.stack(
        [start, enc_lengths[0] - seq * enc, voc * own_rows, voc * cols]
    ).astype(i32)

    q_parts = gather_ring(queries, "seq")
    tgt_parts = gather_ring(targets.reshape(tgt_rows), "seq")
    tgt_twice = jnp.concatenate(tgt_parts + tgt_parts)
    tgt = lax.dynamic_slice(tgt_twice, (start,), (rows,)) - voc * cols
    tgt = jnp.broadcast_to(tgt[:, None], (rows, LANES))

    o_part, q_all = pl.pallas_call(
        functools.partial(attend_kernel, n_seq),
        out_shape=[sds((rows, features + LANES), bf16), sds((rows, features), bf16)],
        in_specs=[SMEM] + [VMEM] * (n_seq + 2),
        out_specs=[VMEM, VMEM],
        scratch_shapes=[pltpu.VMEM((2 * rows, features), bf16)],
        compiler_params=params(),
        name="attend",
    )(scal, *q_parts, enc_keys, enc_values)

    o_all = gather_ring(o_part, "seq")
    ptile = min(TILE, width)
    whole = lambda shape: pl.BlockSpec(shape, lambda j: (0, 0))
    mixed_part, att, lse = pl.pallas_call(
        functools.partial(project_kernel, n_seq),
        grid=(width // ptile,),
        out_shape=[
            sds((rows, width), bf16),
            sds((rows, features), bf16),
            sds((rows, LANES), f32),
        ],
        in_specs=[whole((rows, features + LANES))] * n_seq
        + [pl.BlockSpec((features, ptile), lambda j: (0, j))],
        out_specs=[
            pl.BlockSpec((rows, ptile), lambda j: (0, j)),
            whole((rows, features)),
            whole((rows, LANES)),
        ],
        scratch_shapes=[pltpu.VMEM((rows, features), bf16)],
        compiler_params=params(),
        name="project",
    )(*o_all, out_proj)

    mixed, ng_own = pl.pallas_call(
        norm_kernel,
        out_shape=[sds((own_rows, width), f32), sds((own_rows, width + LANES), bf16)],
        in_specs=[SMEM] + [VMEM] * 3,
        out_specs=[VMEM, VMEM],
        compiler_params=params(),
        name="norm",
    )(scal, exchange_rows(mixed_part, "vocab"), residual, gain)
    ng = gather_rows(ng_own, "vocab")
    ng_dp = gather_swaps(ng, "dp")

    codes, stats = [], []
    for tile0, n in chunks:
        size = n * TILE
        code, stat = pl.pallas_call(
            functools.partial(logits_kernel, tile0 * TILE, cols),
            grid=(n,),
            out_shape=[sds((rows, size), jnp.int16), sds((rows, LANES), f32)],
            in_specs=[
                whole((rows, width + LANES)),
                pl.BlockSpec((TILE, width), lambda j, t=tile0: (t + j, 0)),
            ],
            out_specs=[whole((rows, size)), whole((rows, LANES))],
            scratch_shapes=[pltpu.VMEM((rows, size), f32)],
            compiler_params=params(),
            cost_estimate=cost(2 * 256 * width * size, 2 * width * size),
            name="logits",
        )(ng, weight)
        codes.append(gather_ring(code, "seq"))
        stats.append(gather_ring(stat, "seq"))

    acc = st = None
    exps = []
    for c, (tile0, n) in enumerate(chunks):
        size = n * TILE
        prev = [acc, st] if c else []
        acc, e, st = pl.pallas_call(
            functools.partial(hidden_kernel, c, tile0 * TILE, cols, n_seq, full_width),
            grid=(n,),
            out_shape=[sds((2 * rows, width), f32), sds((rows, size), bf16), sds((rows, LANES), f32)],
            in_specs=[SMEM]
            + [whole((rows, size))] * n_seq
            + [whole((rows, LANES))] * (n_seq + 1)
            + [pl.BlockSpec((TILE, width), lambda j, t=tile0: (t + j, 0))]
            + ([whole((2 * rows, width)), whole((rows, LANES))] if c else []),
            out_specs=[whole((2 * rows, width)), whole((rows, size)), whole((rows, LANES))],
            scratch_shapes=[pltpu.VMEM((2 * rows, size), bf16)],
            compiler_params=params(),
            cost_estimate=cost(2 * 256 * width * size, 2 * width * size),
            name="hidden",
        )(scal, *codes[c], *stats[c], tgt, weight, *prev)
        exps.append(e)

    st_all = gather_rows(st, "vocab")
    hidden_part, coef = pl.pallas_call(
        functools.partial(total_kernel, n_vocab),
        out_shape=[sds((rows, width), bf16), sds((rows, LANES), f32)],
        in_specs=[VMEM] * 3,
        out_specs=[VMEM] * 2,
        compiler_params=params(),
        name="total",
    )(st, st_all, acc)
    got = exchange_rows(hidden_part, "vocab")

    assert cols + 3 <= tiles * TILE
    grads = pl.pallas_call(
        functools.partial(grad_kernel, firsts, cols),
        out_shape=[sds(e.shape, bf16) for e in exps],
        in_specs=[VMEM] * (2 + len(exps)),
        out_specs=[VMEM] * len(exps),
        compiler_params=params(),
        name="logit_grad",
    )(coef, tgt, *exps)
    grads_dp = [gather_swaps(g, "dp") for g in grads]
    last = chunks[-1][1] * TILE
    loss = pl.pallas_call(
        functools.partial(loss_kernel, n_dp * rows),
        grid=(1,),
        out_shape=sds((8, LANES), f32),
        in_specs=[pl.BlockSpec((rows, LANES), lambda j: (0, last // LANES - 1))] * n_dp,
        out_specs=whole((8, LANES)),
        compiler_params=params(),
        name="loss",
    )(*grads_dp[-1])
    mean_loss = loss[0, 0]

    gated, inner = pl.pallas_call(
        gate_kernel,
        out_shape=[sds((own_rows, width), f32), sds((own_rows, LANES), f32)],
        in_specs=[VMEM] * 3,
        out_specs=[VMEM, VMEM],
        compiler_params=params(),
        name="gate",
    )(got, mixed, gain)
    inner_all = gather_ring(inner, "seq")
    mixed_grad = pl.pallas_call(
        functools.partial(mixed_grad_kernel, n_seq, full_width),
        out_shape=sds((own_rows, width), bf16),
        in_specs=[SMEM] + [VMEM] * (3 + n_seq),
        out_specs=VMEM,
        compiler_params=params(),
        name="mixed_grad",
    )(scal, gated, mixed, coef, *inner_all)
    mg = gather_rows(mixed_grad, "vocab")

    ftile = min(256, features)
    back_part = pl.pallas_call(
        back_project_kernel,
        grid=(features // ftile,),
        out_shape=sds((rows, features), bf16),
        in_specs=[whole((rows, width)), pl.BlockSpec((ftile, width), lambda j: (j, 0))],
        out_specs=pl.BlockSpec((rows, ftile), lambda j: (0, j)),
        compiler_params=params(),
        name="back_project",
    )(mg, out_proj)
    back_all = gather_ring(back_part, "seq")
    key_grad, value_grad = pl.pallas_call(
        functools.partial(attend_back_kernel, n_seq),
        out_shape=[sds(enc_keys.shape, f32), sds(enc_values.shape, f32)],
        in_specs=[SMEM] + [VMEM] * (n_seq + 5),
        out_specs=[VMEM, VMEM],
        compiler_params=params(),
        name="attend_back",
    )(scal, *back_all, q_all, enc_keys, enc_values, att, lse)

    head = None
    for c, (tile0, n) in enumerate(chunks):
        prev = [head] if c else []
        head = pl.pallas_call(
            functools.partial(head_kernel, n_dp),
            grid=(n,),
            out_shape=sds((cols, width), bf16),
            in_specs=[whole((rows, width + LANES))] * n_dp
            + [pl.BlockSpec((rows, TILE), lambda j: (0, j))] * n_dp
            + [pl.BlockSpec(memory_space=pl.ANY)] * len(prev),
            out_specs=pl.BlockSpec((TILE, width), lambda j, t=tile0: (t + j, 0)),
            scratch_shapes=[pltpu.VMEM((n_dp * rows, width), bf16)],
            input_output_aliases={2 * n_dp: 0} if c else {},
            compiler_params=params(),
            cost_estimate=cost(2 * n_dp * rows * width * n * TILE, 2 * width * n * TILE),
            name="head_grad",
        )(*ng_dp, *grads_dp[c], *prev)
    return (mean_loss, head.T, key_grad, value_grad)


def solution(mesh):
    placed = (
        P("dp", "seq", "vocab"),
        P("dp", "seq", "vocab"),
        P("dp", "seq", "vocab"),
        P("dp"),
        P("vocab", "seq"),
        P("dp", None, "seq"),
        P("seq"),
        P("seq", "vocab"),
        P("dp", "seq"),
    )
    return jax.shard_map(
        body,
        mesh=mesh,
        in_specs=placed,
        out_specs=(P(), P("seq", "vocab"), P("dp", "seq", "vocab"), P("dp", "seq", "vocab")),
        check_vma=False,
    )
```

```python
import functools
import jax
import jax.numpy as jnp
from jax import lax
from jax.experimental import pallas as pl
from jax.experimental.pallas import tpu as pltpu
from jax.sharding import PartitionSpec as P

HDIM = 256
LANES = 128
TILE = 512
PARTS = 4
PART = TILE // PARTS
HEAD_TILE = 2 * TILE
MAX_CHUNKS = 3
LOW = -1e30
CODE_TOP = 32767.0

zloss_weight = 0.0001
norm_epsilon = 1e-06
score_scale = HDIM ** (-0.5)
f32, bf16, i32 = jnp.float32, jnp.bfloat16, jnp.int32

VMEM = pl.BlockSpec(memory_space=pltpu.VMEM)
SMEM = pl.BlockSpec(memory_space=pltpu.SMEM)


def sds(shape, dtype):
    return jax.ShapeDtypeStruct(shape, dtype)


def params(mib=40):
    return pltpu.CompilerParams(vmem_limit_bytes=mib * 1024 * 1024)


def cost(flops, nbytes):
    return pl.CostEstimate(flops=int(flops), bytes_accessed=int(nbytes), transcendentals=0)


def dot(a, b, ca, cb):
    return lax.dot_general(a, b, (((ca,), (cb,)), ((), ())), preferred_element_type=f32)


def from_ahead(x, axis, k):
    n = lax.axis_size(axis)
    return lax.ppermute(x, axis, [((i + k) % n, i) for i in range(n)])


def gather_ring(x, axis):
    return [x] + [from_ahead(x, axis, k) for k in range(1, lax.axis_size(axis))]


def exchange_rows(x, axis):
    return lax.all_to_all(x, axis, split_axis=0, concat_axis=0, tiled=True)


def swap(x, axis, bit):
    n = lax.axis_size(axis)
    return lax.ppermute(x, axis, [(i, i ^ bit) for i in range(n)])


def gather_swaps(x, axis):
    held = [x]
    bit = lax.axis_size(axis) // 2
    while bit:
        held = held + [swap(h, axis, bit) for h in held]
        bit //= 2
    return held


def tree(terms, op=jnp.add):
    while len(terms) > 1:
        half = len(terms) // 2
        rest = terms[2 * half :]
        terms = [op(terms[i], terms[i + half]) for i in range(half)] + rest
    return terms[0]


def three_parts(x):
    hi = x.astype(bf16).astype(f32)
    mid = (x - hi).astype(bf16).astype(f32)
    return hi, mid, x - hi - mid


def lanes(rows):
    return lax.broadcasted_iota(i32, (rows, LANES), 1)


def attend_kernel(n_seq, scal, *refs):
    q_refs = refs[:n_seq]
    tgt_ref, k_ref, v_ref, o_ref, q_out, q_twice = refs[n_seq:]
    tgt_rows = q_refs[0].shape[1]
    rows = tgt_rows * n_seq
    enc, features = k_ref.shape[1:]
    for i, r in enumerate(q_refs):
        for at in (i * tgt_rows, rows + i * tgt_rows):
            q_twice[at : at + tgt_rows, :] = r[0]
    q = q_twice[pl.ds(pl.multiple_of(scal[0], 16), rows), :]
    q_out[...] = q
    valid = lax.broadcasted_iota(i32, (rows, enc), 1) < scal[1]
    lane = lanes(rows)
    row = lax.broadcasted_iota(i32, (rows, LANES), 0)
    mine = (row >= scal[4]) & (row < scal[4] + tgt_rows)
    ids = jnp.concatenate([tgt_ref[...]] * n_seq, axis=0)
    ids = jnp.where(lane == LANES - 2, ids >> 8, ids & 255).astype(f32)
    stat = jnp.where(mine & (lane >= LANES - 2), ids, 0.0)
    for h in range(features // HDIM):
        at = slice(h * HDIM, (h + 1) * HDIM)
        scores = dot(q[:, at], k_ref[0, :, at], 1, 1) * score_scale
        scores = jnp.where(valid, scores, LOW)
        peak = jnp.max(scores, axis=1, keepdims=True)
        e = jnp.where(valid, jnp.exp(scores - peak), 0.0)
        total = jnp.sum(e, axis=1, keepdims=True)
        some = total > 0.0
        safe = jnp.where(some, total, 1.0)
        o = dot(e.astype(bf16), v_ref[0, :, at], 1, 0) / safe
        o_ref[:, at] = o.astype(bf16)
        lse = jnp.where(some, peak + jnp.log(safe), LOW)
        for i, part in enumerate(three_parts(lse)):
            stat = jnp.where(lane == 3 * h + i, part, stat)
    o_ref[:, features:] = stat.astype(bf16)


def project_kernel(n_seq, scal, *refs):
    o_refs = refs[:n_seq]
    p_ref, mixed_ref, att_ref, lse_ref, tgt_ref, att = refs[n_seq:]
    rows, features = att.shape

    @pl.when(pl.program_id(0) == 0)
    def _():
        stats = [r[:, features:].astype(f32) for r in o_refs]
        lane = lanes(rows)
        lse_all = jnp.zeros((rows, LANES), f32)
        for h in range(features // HDIM):
            at = slice(h * HDIM, (h + 1) * HDIM)
            lses = [
                s[:, 3 * h : 3 * h + 1] + s[:, 3 * h + 1 : 3 * h + 2] + s[:, 3 * h + 2 : 3 * h + 3]
                for s in stats
            ]
            top = tree(lses, jnp.maximum)
            lse = top + jnp.log(tree([jnp.exp(x - top) for x in lses]))
            o = tree([jnp.exp(x - lse) * r[:, at].astype(f32) for x, r in zip(lses, o_refs)])
            att[:, at] = o.astype(bf16)
            lse_all = jnp.where(lane == h, lse, lse_all)
        att_ref[...] = att[...]
        lse_ref[...] = lse_all
        ids = tree([s[:, LANES - 2 : LANES - 1] * 256.0 + s[:, LANES - 1 :] for s in stats])
        tgt_ref[...] = jnp.broadcast_to(ids.astype(i32), (rows, LANES)) - scal[3]

    mixed_ref[...] = dot(att[...], p_ref[...], 1, 0).astype(bf16)


def block_sum(ref, rows):
    n = ref.shape[0] // rows
    return tree([ref[i * rows : (i + 1) * rows, :].astype(f32) for i in range(n)])


def norm_kernel(got_ref, residual_ref, gain_ref, mixed_ref, ng_ref):
    rows, width = mixed_ref.shape
    mixed = residual_ref[...].astype(f32) + block_sum(got_ref, rows)
    mixed_ref[...] = mixed
    ng = (mixed * gain_ref[...]).astype(bf16)
    square = jnp.sum(mixed * mixed, axis=1, keepdims=True)
    lane = lanes(rows)
    stat = jnp.zeros((rows, LANES), f32)
    for i, part in enumerate(three_parts(square)):
        stat = jnp.where(lane == i, part, stat)
    for at in range(0, ng_ref.shape[0], rows):
        ng_ref[at : at + rows, :width] = ng
        ng_ref[at : at + rows, width:] = stat.astype(bf16)


def logits_kernel(first, cols, ng_ref, *refs):
    w_refs = refs[:PARTS]
    code_ref, stat_ref, z = refs[PARTS:]
    j = pl.program_id(0)
    rows, width = z.shape[0], w_refs[0].shape[1]
    w = jnp.concatenate([r[...] for r in w_refs], axis=0)
    part = dot(w, ng_ref[:, :width], 1, 1).T
    at = j * TILE
    if first + z.shape[1] > cols:
        here = first + at + lax.broadcasted_iota(i32, part.shape, 1)
        part = jnp.where(here < cols, part, 0.0)
    z[:, pl.ds(pl.multiple_of(at, TILE), TILE)] = part

    @pl.when(j == pl.num_programs(0) - 1)
    def _():
        val = z[...]
        peak = jnp.maximum(jnp.max(jnp.abs(val), axis=1, keepdims=True), 1e-30)
        code_ref[...] = jnp.round(val * (CODE_TOP / peak)).astype(i32).astype(jnp.int16)
        s = ng_ref[:, width:].astype(f32)
        square = s[:, 0:1] + s[:, 1:2] + s[:, 2:3]
        lane = lanes(rows)
        stat_ref[...] = jnp.where(lane == 0, peak / CODE_TOP, jnp.where(lane == 1, square, 0.0))


def hidden_kernel(chunk, first, cols, n_seq, features, scal, *refs):
    code_refs, sc_refs = refs[:n_seq], refs[n_seq : 2 * n_seq]
    refs = refs[2 * n_seq :]
    if chunk:
        acc_prev, st_prev, acc_ref, e_ref, st_ref, lhs = refs[1 + PARTS :]
    else:
        acc_ref, e_ref, st_ref, lhs = refs[1 + PARTS :]
    tgt_ref, w_refs = refs[0], refs[1 : 1 + PARTS]
    j = pl.program_id(0)
    rows, size = e_ref.shape
    partial_cols = first + size > cols

    @pl.when(j == 0)
    def _():
        z = tree([c[...].astype(i32).astype(f32) * s[:, 0:1] for c, s in zip(code_refs, sc_refs)])
        square = tree([s[:, 1:2] for s in sc_refs])
        inv = lax.rsqrt(square / features + norm_epsilon)
        z = z * inv
        at = first + lax.broadcasted_iota(i32, (rows, size), 1)
        hit = at == tgt_ref[:, 0:1]
        if partial_cols:
            z = jnp.where(at < cols, z, LOW)
            hit = hit & (at < cols)
        here = jnp.sum(jnp.where(hit, z, 0.0), axis=1, keepdims=True)
        peak = jnp.max(z, axis=1, keepdims=True)
        if chunk:
            old = st_prev[...]
            peak = jnp.maximum(peak, old[:, 0:1])
            fade = jnp.exp(old[:, 0:1] - peak)
            acc_ref[:rows, :] = acc_prev[:rows, :] * fade
            acc_ref[rows:, :] = acc_prev[rows:, :]
        else:
            old = jnp.zeros((rows, LANES), f32)
            fade = 0.0
            acc_ref[...] = jnp.zeros_like(acc_ref)
        e = jnp.exp(z - peak)
        total = jnp.sum(e, axis=1, keepdims=True) + old[:, 1:2] * fade
        eh = e.astype(bf16)
        e_ref[...] = eh
        lhs[:rows, :] = eh
        lhs[rows:, :] = hit.astype(f32).astype(bf16)
        lane = lanes(rows)
        st = jnp.where(lane == 0, peak, old)
        st = jnp.where(lane == 1, total, st)
        st = jnp.where(lane == 2, here + old[:, 2:3], st)
        st = jnp.where(lane == 3, inv, st)
        st = jnp.where(lane == 8 + chunk, peak, st)
        for at in range(0, st_ref.shape[0], rows):
            st_ref[at : at + rows, :] = st

    w = jnp.concatenate([r[...] for r in w_refs], axis=0)
    at = j * TILE
    if partial_cols:
        here = first + at + lax.broadcasted_iota(i32, (TILE, 1), 0)
        w = jnp.where(here < cols, w, jnp.zeros_like(w))
    acc_ref[...] += dot(lhs[:, pl.ds(pl.multiple_of(at, TILE), TILE)], w, 1, 0)


def total_kernel(n_vocab, st_rep_ref, st_all_ref, acc_ref, part_ref, coef_ref):
    rows = coef_ref.shape[0]
    mine = st_rep_ref[:rows, :]
    stats = [st_all_ref[k * rows : (k + 1) * rows, :] for k in range(n_vocab)]
    top = tree([s[:, 0:1] for s in stats], jnp.maximum)
    total = tree([s[:, 1:2] * jnp.exp(s[:, 0:1] - top) for s in stats])
    hit_logit = tree([s[:, 2:3] for s in stats])
    log_total = top + jnp.log(total)
    loss = log_total - hit_logit + zloss_weight * log_total * log_total
    lift = 1.0 + 2.0 * zloss_weight * log_total
    inv = mine[:, 3:4]
    lane = lanes(rows)
    coef = jnp.exp(jnp.minimum(mine - log_total, 30.0)) * lift * inv
    coef = jnp.where(lane >= 8, coef, inv)
    coef_ref[...] = jnp.where(lane == 1, loss, coef)
    scale = jnp.exp(mine[:, 0:1] - log_total) * lift
    part = acc_ref[:rows, :] * scale - acc_ref[rows:, :]
    part_ref[...] = part.astype(bf16)


def grad_kernel(firsts, cols, coef_ref, tgt_ref, *refs):
    n = len(firsts)
    for c, first in enumerate(firsts):
        e_ref, g_ref = refs[c], refs[n + c]
        at = first + lax.broadcasted_iota(i32, e_ref.shape, 1)
        hit = at == tgt_ref[:, 0:1]
        inv = coef_ref[:, 0:1]
        g = e_ref[...].astype(f32) * coef_ref[:, 8 + c : 9 + c] - jnp.where(hit, inv, 0.0)
        g_ref[...] = g.astype(bf16)
    last = refs[-1]
    rows, size = last.shape
    lane = lanes(rows)
    stat = last[:, size - LANES :].astype(f32)
    for i, part in enumerate(three_parts(coef_ref[:, 1:2])):
        stat = jnp.where(lane == LANES - 3 + i, part, stat)
    last[:, size - LANES :] = stat.astype(bf16)


def loss_kernel(rows_all, *refs):
    sums = []
    for r in refs[:-1]:
        s = r[...].astype(f32)
        sums.append(jnp.sum(s[:, -3:-2] + s[:, -2:-1] + s[:, -1:], axis=0, keepdims=True))
    refs[-1][...] = jnp.broadcast_to(tree(sums) / rows_all, refs[-1].shape)


def head_kernel(n_dp, *refs):
    ng_refs, g_refs = refs[:n_dp], refs[n_dp : 2 * n_dp]
    out_ref, ng, turned = refs[-3:]
    rows, width = ng_refs[0].shape[0], out_ref.shape[1]

    @pl.when(pl.program_id(0) == 0)
    def _():
        for i, r in enumerate(ng_refs):
            ng[i * rows : (i + 1) * rows, :] = r[:, :width]

    turned[...] = jnp.concatenate([r[...] for r in g_refs], axis=0).T
    for at in range(0, width, 256):
        out_ref[:, at : at + 256] = dot(turned[...], ng[:, at : at + 256], 1, 0).astype(bf16)


def gate_kernel(got_ref, mixed_ref, gain_ref, gated_ref, dot_ref):
    gated = block_sum(got_ref, mixed_ref.shape[0]) * gain_ref[...]
    gated_ref[...] = gated
    inner = jnp.sum(gated * mixed_ref[...], axis=1, keepdims=True)
    dot_ref[...] = jnp.broadcast_to(inner, dot_ref.shape)


def mixed_grad_kernel(n_seq, features, scal, gated_ref, mixed_ref, coef_ref, *refs):
    dot_refs, out_ref = refs[:n_seq], refs[n_seq]
    rows = gated_ref.shape[0]
    inner = tree([r[:, 0:1] for r in dot_refs])
    inv = coef_ref[pl.ds(pl.multiple_of(scal[2], 16), rows), :][:, 0:1]
    out = gated_ref[...] * inv - mixed_ref[...] * (inv * inv * inv * inner / features)
    for at in range(0, out_ref.shape[0], rows):
        out_ref[at : at + rows, :] = out.astype(bf16)


def back_project_kernel(mg_ref, p_ref, out_ref):
    out_ref[...] = dot(mg_ref[...], p_ref[...], 1, 1).astype(bf16)


def attend_back_kernel(n_seq, scal, *refs):
    a_refs = refs[:n_seq]
    q_ref, k_ref, v_ref, att_ref, lse_ref, kg_ref, vg_ref = refs[n_seq:]
    enc, features = k_ref.shape[1:]
    rows = q_ref.shape[0]
    valid = lax.broadcasted_iota(i32, (rows, enc), 1) < scal[1]
    for h in range(features // HDIM):
        at = slice(h * HDIM, (h + 1) * HDIM)
        grad = tree([r[:, at].astype(f32) for r in a_refs]).astype(bf16)
        q = q_ref[:, at]
        scores = dot(q, k_ref[0, :, at], 1, 1) * score_scale
        w = jnp.where(valid, jnp.exp(jnp.minimum(scores - lse_ref[:, h : h + 1], 0.5)), 0.0)
        prob_grad = dot(grad, v_ref[0, :, at], 1, 1)
        inner = jnp.sum(grad.astype(f32) * att_ref[:, at].astype(f32), axis=1, keepdims=True)
        sg = (w * (prob_grad - inner) * score_scale).astype(bf16)
        vg_ref[0, :, at] = dot(w.astype(bf16), grad, 0, 0)
        kg_ref[0, :, at] = dot(sg, q, 0, 0)


def weight_specs(tile0, width, cols):
    top = -(-cols // PART) - 1
    return [
        pl.BlockSpec(
            (PART, width),
            lambda j, i=i: (jnp.minimum(PARTS * (tile0 + j) + i, top), 0),
        )
        for i in range(PARTS)
    ]


def body(
    queries, enc_keys, enc_values, enc_lengths, out_proj, residual, norm_gain, head_weight, targets
):
    n_seq, n_vocab, n_dp = lax.axis_size("seq"), lax.axis_size("vocab"), lax.axis_size("dp")
    seq, voc = lax.axis_index("seq"), lax.axis_index("vocab")
    tgt_rows, features = queries.shape[1:]
    enc = enc_keys.shape[1]
    rows = tgt_rows * n_seq
    own_rows = rows // n_vocab
    width, cols = head_weight.shape
    full_width = width * n_seq
    tiles = -(-cols // TILE)
    per = 2 * -(-tiles // (2 * MAX_CHUNKS))
    assert tiles % 2 == 0
    chunks = [(t, min(per, tiles - t)) for t in range(0, tiles, per)]
    firsts = [t * TILE for t, _ in chunks]
    gain = norm_gain.reshape(1, width)
    weight = head_weight.T

    start = lax.rem(rows - seq * tgt_rows, rows).astype(i32)
    scal = jnp.stack(
        [start, enc_lengths[0] - seq * enc, voc * own_rows, voc * cols, seq * tgt_rows]
    ).astype(i32)

    q_parts = gather_ring(queries, "seq")
    tgt_own = jnp.broadcast_to(targets.reshape(tgt_rows, 1), (tgt_rows, LANES))
    res_own = lax.dynamic_slice(residual[0], (voc * own_rows, 0), (own_rows, width))
    o_part, q_all = pl.pallas_call(
        functools.partial(attend_kernel, n_seq),
        out_shape=[sds((rows, features + LANES), bf16), sds((rows, features), bf16)],
        in_specs=[SMEM] + [VMEM] * (n_seq + 3),
        out_specs=[VMEM, VMEM],
        scratch_shapes=[pltpu.VMEM((2 * rows, features), bf16)],
        compiler_params=params(),
        cost_estimate=cost(0, 7 * 1024 * 1024),
        name="attend",
    )(scal, *q_parts, tgt_own, enc_keys, enc_values)

    o_all = gather_ring(o_part, "seq")
    ptile = min(TILE, width)
    whole = lambda shape: pl.BlockSpec(shape, lambda j: (0, 0))
    mixed_part, att, lse, tgt = pl.pallas_call(
        functools.partial(project_kernel, n_seq),
        grid=(width // ptile,),
        out_shape=[
            sds((rows, width), bf16),
            sds((rows, features), bf16),
            sds((rows, LANES), f32),
            sds((rows, LANES), i32),
        ],
        in_specs=[SMEM]
        + [whole((rows, features + LANES))] * n_seq
        + [pl.BlockSpec((features, ptile), lambda j: (0, j))],
        out_specs=[
            pl.BlockSpec((rows, ptile), lambda j: (0, j)),
            whole((rows, features)),
            whole((rows, LANES)),
            whole((rows, LANES)),
        ],
        scratch_shapes=[pltpu.VMEM((rows, features), bf16)],
        compiler_params=params(),
        cost_estimate=cost(0, 7 * 1024 * 1024),
        name="project",
    )(scal, *o_all, out_proj)

    mixed, ng_own = pl.pallas_call(
        norm_kernel,
        out_shape=[sds((own_rows, width), f32), sds((rows, width + LANES), bf16)],
        in_specs=[VMEM] * 3,
        out_specs=[VMEM, VMEM],
        compiler_params=params(),
        cost_estimate=cost(0, 7 * 1024 * 1024),
        name="norm",
    )(exchange_rows(mixed_part, "vocab"), res_own, gain)
    ng = exchange_rows(ng_own, "vocab")
    ng_dp = gather_swaps(ng, "dp")

    codes, stats = [], []
    for tile0, n in chunks:
        size = n * TILE
        code, stat = pl.pallas_call(
            functools.partial(logits_kernel, tile0 * TILE, cols),
            grid=(n,),
            out_shape=[sds((rows, size), jnp.int16), sds((rows, LANES), f32)],
            in_specs=[whole((rows, width + LANES))] + weight_specs(tile0, width, cols),
            out_specs=[whole((rows, size)), whole((rows, LANES))],
            scratch_shapes=[pltpu.VMEM((rows, size), f32)],
            compiler_params=params(),
            cost_estimate=cost(2 * 256 * width * size, 2 * width * size),
            name="logits",
        )(ng, *[weight] * PARTS)
        codes.append(gather_ring(code, "seq"))
        stats.append(gather_ring(stat, "seq"))

    acc = st = None
    exps = []
    for c, (tile0, n) in enumerate(chunks):
        size = n * TILE
        prev = [acc, st] if c else []
        st_rows = rows * n_vocab if c == len(chunks) - 1 else rows
        acc, e, st = pl.pallas_call(
            functools.partial(hidden_kernel, c, tile0 * TILE, cols, n_seq, full_width),
            grid=(n,),
            out_shape=[sds((2 * rows, width), f32), sds((rows, size), bf16), sds((st_rows, LANES), f32)],
            in_specs=[SMEM]
            + [whole((rows, size))] * n_seq
            + [whole((rows, LANES))] * (n_seq + 1)
            + weight_specs(tile0, width, cols)
            + ([whole((2 * rows, width)), whole((rows, LANES))] if c else []),
            out_specs=[whole((2 * rows, width)), whole((rows, size)), whole((st_rows, LANES))],
            scratch_shapes=[pltpu.VMEM((2 * rows, size), bf16)],
            compiler_params=params(),
            cost_estimate=cost(2 * 256 * width * size, 2 * width * size),
            name="hidden",
        )(scal, *codes[c], *stats[c], tgt, *[weight] * PARTS, *prev)
        exps.append(e)

    st_all = exchange_rows(st, "vocab")
    hidden_part, coef = pl.pallas_call(
        functools.partial(total_kernel, n_vocab),
        out_shape=[sds((rows, width), bf16), sds((rows, LANES), f32)],
        in_specs=[VMEM] * 3,
        out_specs=[VMEM] * 2,
        compiler_params=params(),
        cost_estimate=cost(0, 7 * 1024 * 1024),
        name="total",
    )(st, st_all, acc)
    got = exchange_rows(hidden_part, "vocab")

    assert cols + 3 <= tiles * TILE
    grads = pl.pallas_call(
        functools.partial(grad_kernel, firsts, cols),
        out_shape=[sds(e.shape, bf16) for e in exps],
        in_specs=[VMEM] * (2 + len(exps)),
        out_specs=[VMEM] * len(exps),
        compiler_params=params(),
        cost_estimate=cost(0, 7 * 1024 * 1024),
        name="logit_grad",
    )(coef, tgt, *exps)
    grads_dp = [gather_swaps(g, "dp") for g in grads]
    last = chunks[-1][1] * TILE
    loss = pl.pallas_call(
        functools.partial(loss_kernel, n_dp * rows),
        grid=(1,),
        out_shape=sds((8, LANES), f32),
        in_specs=[pl.BlockSpec((rows, LANES), lambda j: (0, last // LANES - 1))] * n_dp,
        out_specs=whole((8, LANES)),
        compiler_params=params(),
        cost_estimate=cost(0, 7 * 1024 * 1024),
        name="loss",
    )(*grads_dp[-1])
    mean_loss = loss[0, 0]

    gated, inner = pl.pallas_call(
        gate_kernel,
        out_shape=[sds((own_rows, width), f32), sds((own_rows, LANES), f32)],
        in_specs=[VMEM] * 3,
        out_specs=[VMEM, VMEM],
        compiler_params=params(),
        cost_estimate=cost(0, 7 * 1024 * 1024),
        name="gate",
    )(got, mixed, gain)
    inner_all = gather_ring(inner, "seq")
    mixed_grad = pl.pallas_call(
        functools.partial(mixed_grad_kernel, n_seq, full_width),
        out_shape=sds((rows, width), bf16),
        in_specs=[SMEM] + [VMEM] * (3 + n_seq),
        out_specs=VMEM,
        compiler_params=params(),
        cost_estimate=cost(0, 7 * 1024 * 1024),
        name="mixed_grad",
    )(scal, gated, mixed, coef, *inner_all)
    mg = exchange_rows(mixed_grad, "vocab")

    ftile = min(256, features)
    back_part = pl.pallas_call(
        back_project_kernel,
        grid=(features // ftile,),
        out_shape=sds((rows, features), bf16),
        in_specs=[whole((rows, width)), pl.BlockSpec((ftile, width), lambda j: (j, 0))],
        out_specs=pl.BlockSpec((rows, ftile), lambda j: (0, j)),
        compiler_params=params(),
        cost_estimate=cost(0, 7 * 1024 * 1024),
        name="back_project",
    )(mg, out_proj)
    back_all = gather_ring(back_part, "seq")
    key_grad, value_grad = pl.pallas_call(
        functools.partial(attend_back_kernel, n_seq),
        out_shape=[sds(enc_keys.shape, f32), sds(enc_values.shape, f32)],
        in_specs=[SMEM] + [VMEM] * (n_seq + 5),
        out_specs=[VMEM, VMEM],
        compiler_params=params(),
        cost_estimate=cost(0, 7 * 1024 * 1024),
        name="attend_back",
    )(scal, *back_all, q_all, enc_keys, enc_values, att, lse)

    head = None
    for c, (tile0, n) in enumerate(chunks):
        prev = [head] if c else []
        head = pl.pallas_call(
            functools.partial(head_kernel, n_dp),
            grid=(n // 2,),
            out_shape=sds((cols, width), bf16),
            in_specs=[whole((rows, width + LANES))] * n_dp
            + [pl.BlockSpec((rows, HEAD_TILE), lambda j: (0, j))] * n_dp
            + [pl.BlockSpec(memory_space=pl.ANY)] * len(prev),
            out_specs=pl.BlockSpec((HEAD_TILE, width), lambda j, t=tile0: (t // 2 + j, 0)),
            scratch_shapes=[
                pltpu.VMEM((n_dp * rows, width), bf16),
                pltpu.VMEM((HEAD_TILE, n_dp * rows), bf16),
            ],
            input_output_aliases={2 * n_dp: 0} if c else {},
            compiler_params=params(),
            cost_estimate=cost(2 * n_dp * rows * width * n * TILE, 2 * width * n * TILE),
            name="head_grad",
        )(*ng_dp, *grads_dp[c], *prev)
    return (mean_loss, head.T, key_grad, value_grad)


def solution(mesh):
    placed = (
        P("dp", "seq", "vocab"),
        P("dp", "seq", "vocab"),
        P("dp", "seq", "vocab"),
        P("dp"),
        P("vocab", "seq"),
        P("dp", None, "seq"),
        P("seq"),
        P("seq", "vocab"),
        P("dp", "seq"),
    )
    return jax.shard_map(
        body,
        mesh=mesh,
        in_specs=placed,
        out_specs=(P(), P("seq", "vocab"), P("dp", "seq", "vocab"), P("dp", "seq", "vocab")),
        check_vma=False,
    )
```

```python
import functools
import jax
import jax.numpy as jnp
from jax import lax
from jax.experimental import pallas as pl
from jax.experimental.pallas import tpu as pltpu
from jax.sharding import PartitionSpec as P

HDIM = 256
LANES = 128
TILE = 512
PARTS = 4
PART = TILE // PARTS
HEAD_TILE = 2 * TILE
MAX_CHUNKS = 3
GROUPS = 1
LOW = -1e30
CODE_TOP = 32767.0

zloss_weight = 0.0001
norm_epsilon = 1e-06
score_scale = HDIM ** (-0.5)
f32, bf16, i32 = jnp.float32, jnp.bfloat16, jnp.int32

VMEM = pl.BlockSpec(memory_space=pltpu.VMEM)
SMEM = pl.BlockSpec(memory_space=pltpu.SMEM)


def sds(shape, dtype):
    return jax.ShapeDtypeStruct(shape, dtype)


def params(mib=40):
    return pltpu.CompilerParams(vmem_limit_bytes=mib * 1024 * 1024)


def cost(flops, nbytes):
    return pl.CostEstimate(flops=int(flops), bytes_accessed=int(nbytes), transcendentals=0)


def dot(a, b, ca, cb):
    return lax.dot_general(a, b, (((ca,), (cb,)), ((), ())), preferred_element_type=f32)


def from_ahead(x, axis, k):
    n = lax.axis_size(axis)
    return lax.ppermute(x, axis, [((i + k) % n, i) for i in range(n)])


def gather_ring(x, axis):
    return [x] + [from_ahead(x, axis, k) for k in range(1, lax.axis_size(axis))]


def scatter_ring(x, axis, rows):
    n = lax.axis_size(axis)
    return [
        lax.ppermute(x[k * rows : (k + 1) * rows], axis, [(i, (i + k) % n) for i in range(n)])
        for k in range(1, n)
    ]


def swap(x, axis, bit):
    n = lax.axis_size(axis)
    return lax.ppermute(x, axis, [(i, i ^ bit) for i in range(n)])


def gather_swaps(x, axis):
    held = [x]
    bit = lax.axis_size(axis) // 2
    while bit:
        held = held + [swap(h, axis, bit) for h in held]
        bit //= 2
    return held


def tree(terms, op=jnp.add):
    while len(terms) > 1:
        half = len(terms) // 2
        rest = terms[2 * half :]
        terms = [op(terms[i], terms[i + half]) for i in range(half)] + rest
    return terms[0]


def three_parts(x):
    hi = x.astype(bf16).astype(f32)
    mid = (x - hi).astype(bf16).astype(f32)
    return hi, mid, x - hi - mid


def lanes(rows):
    return lax.broadcasted_iota(i32, (rows, LANES), 1)


def attend_kernel(n_seq, scal, *refs):
    q_refs = refs[:n_seq]
    tgt_ref, k_ref, v_ref, o_ref, q_out, q_twice, t_twice = refs[n_seq:]
    tgt_rows = q_refs[0].shape[1]
    rows = tgt_rows * n_seq
    enc, features = k_ref.shape[1:]
    for i, r in enumerate(q_refs):
        for at in (i * tgt_rows, rows + i * tgt_rows):
            q_twice[at : at + tgt_rows, :] = r[0]
    q = q_twice[pl.ds(pl.multiple_of(scal[0], 16), rows), :]
    q_out[...] = q
    valid = lax.broadcasted_iota(i32, (rows, enc), 1) < scal[1]
    lane = lanes(rows)
    corner = (tgt_rows, tgt_rows)
    same = lax.broadcasted_iota(i32, corner, 0) == lax.broadcasted_iota(i32, corner, 1)
    here = lanes(tgt_rows)
    digits = jnp.zeros((tgt_rows, LANES), f32)
    ids = jnp.broadcast_to(tgt_ref[...], corner)
    for at, digit in ((LANES - 2, ids >> 8), (LANES - 1, ids & 255)):
        column = jnp.sum(jnp.where(same, digit.astype(f32), 0.0), axis=1, keepdims=True)
        digits = jnp.where(here == at, column, digits)
    t_twice[...] = jnp.zeros_like(t_twice)
    t_twice[:tgt_rows, :] = digits
    t_twice[rows : rows + tgt_rows, :] = digits
    stat = t_twice[pl.ds(pl.multiple_of(scal[0], 16), rows), :]
    for h in range(features // HDIM):
        at = slice(h * HDIM, (h + 1) * HDIM)
        scores = dot(q[:, at], k_ref[0, :, at], 1, 1) * score_scale
        scores = jnp.where(valid, scores, LOW)
        peak = jnp.max(scores, axis=1, keepdims=True)
        e = jnp.where(valid, jnp.exp(scores - peak), 0.0)
        total = jnp.sum(e, axis=1, keepdims=True)
        some = total > 0.0
        safe = jnp.where(some, total, 1.0)
        o = dot(e.astype(bf16), v_ref[0, :, at], 1, 0) / safe
        o_ref[:, at] = o.astype(bf16)
        lse = jnp.where(some, peak + jnp.log(safe), LOW)
        for i, part in enumerate(three_parts(lse)):
            stat = jnp.where(lane == 3 * h + i, part, stat)
    o_ref[:, features:] = stat.astype(bf16)


def project_kernel(n_seq, own_rows, ptile, scal, *refs):
    o_refs = refs[:n_seq]
    p_ref, mixed_ref, own_ref, att_ref, lse_ref, tgt_ref, p_buf, sems = refs[n_seq:]
    rows, features = att_ref.shape
    columns = [pl.ds(at, ptile) for at in range(0, p_buf.shape[1], ptile)]
    copies = [
        pltpu.make_async_copy(p_ref.at[:, c], p_buf.at[:, c], sems.at[i])
        for i, c in enumerate(columns)
    ]
    for c in copies:
        c.start()
    stats = [r[:, features:].astype(f32) for r in o_refs]
    lane = lanes(rows)
    lse_all = jnp.zeros((rows, LANES), f32)
    for h in range(features // HDIM):
        at = slice(h * HDIM, (h + 1) * HDIM)
        lses = [
            s[:, 3 * h : 3 * h + 1] + s[:, 3 * h + 1 : 3 * h + 2] + s[:, 3 * h + 2 : 3 * h + 3]
            for s in stats
        ]
        top = tree(lses, jnp.maximum)
        lse = top + jnp.log(tree([jnp.exp(x - top) for x in lses]))
        o = tree([jnp.exp(x - lse) * r[:, at].astype(f32) for x, r in zip(lses, o_refs)])
        att_ref[:, at] = o.astype(bf16)
        lse_all = jnp.where(lane == h, lse, lse_all)
    lse_ref[...] = lse_all
    ids = tree([s[:, LANES - 2 : LANES - 1] * 256.0 + s[:, LANES - 1 :] for s in stats])
    tgt_ref[...] = jnp.broadcast_to(ids.astype(i32), (rows, LANES)) - scal[2]
    for c, copy in zip(columns, copies):
        copy.wait()
        part = dot(att_ref[...], p_buf[:, c], 1, 0)
        mixed_ref[:, c] = part.astype(bf16)
        own_ref[:, c] = part[:own_rows]


def norm_kernel(n_got, *refs):
    own_ref, got_refs = refs[0], refs[1 : 1 + n_got]
    residual_ref, gain_ref, mixed_ref, ng_ref = refs[1 + n_got :]
    rows, width = mixed_ref.shape
    mixed = own_ref[...] + residual_ref[...].astype(f32)
    for r in got_refs:
        mixed = mixed + r[...].astype(f32)
    mixed_ref[...] = mixed
    ng_ref[:, :width] = (mixed * gain_ref[...]).astype(bf16)
    square = jnp.sum(mixed * mixed, axis=1, keepdims=True)
    lane = lanes(rows)
    stat = jnp.zeros((rows, LANES), f32)
    for i, part in enumerate(three_parts(square)):
        stat = jnp.where(lane == i, part, stat)
    ng_ref[:, width:] = stat.astype(bf16)


def start_weights(first, cols, w_ref, edge_ref, buf, sems):
    copies = []
    for i in range(buf.shape[0] // PART):
        at = first + i * PART
        n = PART if at + PART <= cols else cols - at
        if n == PART or (n > 0 and cols % 16 == 0):
            here = buf.at[i * PART : i * PART + n]
            copies.append(pltpu.make_async_copy(w_ref.at[at : at + n], here, sems.at[i]))
    for c in copies:
        c.start()
    for i in range(buf.shape[0] // PART):
        n = min(max(cols - first - i * PART, 0), PART)
        if n == PART:
            continue
        if i < len(copies):
            buf[i * PART + n : (i + 1) * PART, :] = jnp.zeros((PART - n, buf.shape[1]), bf16)
        elif n:
            rows = lax.broadcasted_iota(i32, (PART, 1), 0)
            edge = edge_ref[...]
            buf[i * PART : (i + 1) * PART, :] = jnp.where(rows < n, edge, jnp.zeros_like(edge))
        else:
            buf[i * PART : (i + 1) * PART, :] = jnp.zeros((PART, buf.shape[1]), bf16)
    return copies


def wait_tile(copies, t):
    for c in copies[t * PARTS : (t + 1) * PARTS]:
        c.wait()


def logits_kernel(first, cols, n_vocab, *refs):
    ng_refs, (w_ref, edge_ref) = refs[:n_vocab], refs[n_vocab : n_vocab + 2]
    outs = refs[n_vocab + 2 :]
    code_ref, stat_ref = outs[:2]
    z, buf, sems = outs[-3:]
    width = buf.shape[1]
    copies = start_weights(first, cols, w_ref, edge_ref, buf, sems)
    ng = jnp.concatenate([r[...] for r in ng_refs], axis=0)
    if len(outs) > 5:
        outs[2][...] = ng[:, :width]
    for t in range(z.shape[1] // TILE):
        wait_tile(copies, t)
        at = slice(t * TILE, (t + 1) * TILE)
        z[:, at] = dot(buf[at, :], ng[:, :width], 1, 1).T
    val = z[...]
    peak = jnp.maximum(jnp.max(jnp.abs(val), axis=1, keepdims=True), 1e-30)
    code_ref[...] = jnp.round(val * (CODE_TOP / peak)).astype(i32).astype(jnp.int16)
    s = ng[:, width:].astype(f32)
    square = s[:, 0:1] + s[:, 1:2] + s[:, 2:3]
    lane = lanes(z.shape[0])
    stat_ref[...] = jnp.where(lane == 0, peak / CODE_TOP, jnp.where(lane == 1, square, 0.0))


def exp_rows(chunk, first, cols, n_seq, features, refs, e_ref, st_ref, lhs):
    code_refs, sc_refs, tgt_ref = refs[:n_seq], refs[n_seq : 2 * n_seq], refs[2 * n_seq]
    rows, size = e_ref.shape
    z = tree([c[...].astype(i32).astype(f32) * s[:, 0:1] for c, s in zip(code_refs, sc_refs)])
    square = tree([s[:, 1:2] for s in sc_refs])
    inv = lax.rsqrt(square / features + norm_epsilon)
    z = z * inv
    at = first + lax.broadcasted_iota(i32, (rows, size), 1)
    hit = at == tgt_ref[:, 0:1]
    if first + size > cols:
        z = jnp.where(at < cols, z, LOW)
        hit = hit & (at < cols)
    here = jnp.sum(jnp.where(hit, z, 0.0), axis=1, keepdims=True)
    peak = jnp.max(z, axis=1, keepdims=True)
    if chunk:
        old = refs[2 * n_seq + 1][...]
        peak = jnp.maximum(peak, old[:, 0:1])
        fade = jnp.exp(old[:, 0:1] - peak)
    else:
        old = jnp.zeros((rows, LANES), f32)
        fade = jnp.zeros((rows, 1), f32)
    e = jnp.exp(z - peak)
    total = jnp.sum(e, axis=1, keepdims=True) + old[:, 1:2] * fade
    eh = e.astype(bf16)
    e_ref[...] = eh
    lhs[:rows, :] = eh
    lhs[rows:, :] = hit.astype(f32).astype(bf16)
    lane = lanes(rows)
    st = jnp.where(lane == 0, peak, old)
    st = jnp.where(lane == 1, total, st)
    st = jnp.where(lane == 2, here + old[:, 2:3], st)
    st = jnp.where(lane == 3, inv, st)
    st_ref[...] = jnp.where(lane == 8 + chunk, peak, st)
    return fade


def hidden_sum(chunk, copies, buf, lhs, acc_prev, fade, acc_ref):
    rows = acc_ref.shape[0] // 2
    if chunk:
        acc_ref[:rows, :] = acc_prev[:rows, :] * fade
        acc_ref[rows:, :] = acc_prev[rows:, :]
    for t in range(buf.shape[0] // TILE):
        wait_tile(copies, t)
        at = slice(t * TILE, (t + 1) * TILE)
        part = dot(lhs[:, at], buf[at, :], 1, 0)
        if chunk or t:
            acc_ref[...] += part
        else:
            acc_ref[...] = part


def hidden_kernel(chunk, first, cols, n_seq, features, *refs):
    n = 2 * n_seq + 1 + (1 if chunk else 0)
    ins, refs = refs[:n], refs[n:]
    acc_prev = None
    if chunk:
        acc_prev, refs = refs[0], refs[1:]
    w_ref, edge_ref, acc_ref, e_ref, st_ref, lhs, buf, sems = refs
    copies = start_weights(first, cols, w_ref, edge_ref, buf, sems)
    fade = exp_rows(chunk, first, cols, n_seq, features, ins, e_ref, st_ref, lhs)
    hidden_sum(chunk, copies, buf, lhs, acc_prev, fade, acc_ref)


def last_exp_kernel(chunk, first, cols, n_seq, features, *refs):
    ins, (e_ref, st_ref, lhs_ref) = refs[:-3], refs[-3:]
    exp_rows(chunk, first, cols, n_seq, features, ins, e_ref, st_ref, lhs_ref)


def last_hidden_kernel(
    chunk, first, cols, st_prev, st_ref, lhs_ref, acc_prev, w_ref, edge_ref, acc_ref, buf, sems
):
    copies = start_weights(first, cols, w_ref, edge_ref, buf, sems)
    fade = jnp.exp(st_prev[:, 0:1] - st_ref[:, 0:1])
    hidden_sum(chunk, copies, buf, lhs_ref, acc_prev, fade, acc_ref)


def total_kernel(n_vocab, own_rows, *refs):
    st_refs = refs[:n_vocab]
    acc_ref, part_ref, own_ref, coef_ref = refs[n_vocab:]
    rows = coef_ref.shape[0]
    mine = st_refs[0][...]
    stats = [mine]
    for k in range(1, n_vocab):
        s = st_refs[k][...]
        cut = rows - k * own_rows
        stats.append(jnp.concatenate([s[cut:], s[:cut]], axis=0))
    top = tree([s[:, 0:1] for s in stats], jnp.maximum)
    total = tree([s[:, 1:2] * jnp.exp(s[:, 0:1] - top) for s in stats])
    hit_logit = tree([s[:, 2:3] for s in stats])
    log_total = top + jnp.log(total)
    loss = log_total - hit_logit + zloss_weight * log_total * log_total
    lift = 1.0 + 2.0 * zloss_weight * log_total
    inv = mine[:, 3:4]
    lane = lanes(rows)
    coef = jnp.exp(jnp.minimum(mine - log_total, 30.0)) * lift * inv
    coef = jnp.where(lane >= 8, coef, inv)
    coef_ref[...] = jnp.where(lane == 1, loss, coef)
    scale = jnp.exp(mine[:, 0:1] - log_total) * lift
    part = acc_ref[:rows, :] * scale - acc_ref[rows:, :]
    part_ref[...] = part.astype(bf16)
    own_ref[...] = part[:own_rows]


def grad_kernel(firsts, n_out, coef_ref, tgt_ref, *refs):
    n = len(firsts)
    outs = refs[n : n + n_out]
    inv = coef_ref[:, 0:1]
    for c, first in enumerate(firsts):
        e_ref = refs[c]
        for off in range(0, e_ref.shape[1], TILE):
            e = e_ref[:, off : off + TILE]
            at = first + off + lax.broadcasted_iota(i32, e.shape, 1)
            hit = at == tgt_ref[:, 0:1]
            g = e.astype(f32) * coef_ref[:, 8 + c : 9 + c] - jnp.where(hit, inv, 0.0)
            group, place = divmod(first + off, outs[0].shape[1])
            outs[group][:, place : place + TILE] = g.astype(bf16)
    last = refs[-1]
    rows, size = last.shape
    lane = lanes(rows)
    stat = last[:, size - LANES :].astype(f32)
    for i, part in enumerate(three_parts(coef_ref[:, 1:2])):
        stat = jnp.where(lane == LANES - 3 + i, part, stat)
    last[:, size - LANES :] = stat.astype(bf16)


def loss_kernel(rows_all, *refs):
    sums = []
    for r in refs[:-1]:
        s = r[...].astype(f32)
        sums.append(jnp.sum(s[:, -3:-2] + s[:, -2:-1] + s[:, -1:], axis=0, keepdims=True))
    refs[-1][...] = jnp.broadcast_to(tree(sums) / rows_all, refs[-1].shape)


def head_kernel(n_dp, *refs):
    ng_refs, g_refs = refs[:n_dp], refs[n_dp : 2 * n_dp]
    out_ref, ng, turned = refs[-3:]
    rows, width = ng_refs[0].shape[0], out_ref.shape[1]

    @pl.when(pl.program_id(0) == 0)
    def _():
        for i, r in enumerate(ng_refs):
            ng[i * rows : (i + 1) * rows, :] = r[:, :width]

    turned[...] = jnp.concatenate([r[...] for r in g_refs], axis=0).T
    for at in range(0, width, 256):
        out_ref[:, at : at + 256] = dot(turned[...], ng[:, at : at + 256], 1, 0).astype(bf16)


def gate_kernel(n_got, *refs):
    own_ref, got_refs = refs[0], refs[1 : 1 + n_got]
    mixed_ref, gain_ref, gated_ref, dot_ref = refs[1 + n_got :]
    total = own_ref[...]
    for r in got_refs:
        total = total + r[...].astype(f32)
    gated = total * gain_ref[...]
    gated_ref[...] = gated
    inner = jnp.sum(gated * mixed_ref[...], axis=1, keepdims=True)
    dot_ref[...] = jnp.broadcast_to(inner, dot_ref.shape)


def mixed_grad_kernel(n_seq, features, gated_ref, mixed_ref, coef_ref, *refs):
    dot_refs, out_ref = refs[:n_seq], refs[n_seq]
    inner = tree([r[:, 0:1] for r in dot_refs])
    inv = coef_ref[: out_ref.shape[0], 0:1]
    out = gated_ref[...] * inv - mixed_ref[...] * (inv * inv * inv * inner / features)
    out_ref[...] = out.astype(bf16)


def back_project_kernel(*refs):
    mg_refs, p_ref, out_ref = refs[:-2], refs[-2], refs[-1]
    mg = jnp.concatenate([r[...] for r in mg_refs], axis=0)
    out_ref[...] = dot(mg, p_ref[...], 1, 1).astype(bf16)


def attend_back_kernel(n_seq, scal, *refs):
    a_refs = refs[:n_seq]
    q_ref, k_ref, v_ref, att_ref, lse_ref, kg_ref, vg_ref = refs[n_seq:]
    enc, features = k_ref.shape[1:]
    rows = q_ref.shape[0]
    valid = lax.broadcasted_iota(i32, (rows, enc), 1) < scal[1]
    for h in range(features // HDIM):
        at = slice(h * HDIM, (h + 1) * HDIM)
        grad = tree([r[:, at].astype(f32) for r in a_refs]).astype(bf16)
        q = q_ref[:, at]
        scores = dot(q, k_ref[0, :, at], 1, 1) * score_scale
        w = jnp.where(valid, jnp.exp(jnp.minimum(scores - lse_ref[:, h : h + 1], 0.5)), 0.0)
        prob_grad = dot(grad, v_ref[0, :, at], 1, 1)
        inner = jnp.sum(grad.astype(f32) * att_ref[:, at].astype(f32), axis=1, keepdims=True)
        sg = (w * (prob_grad - inner) * score_scale).astype(bf16)
        vg_ref[0, :, at] = dot(w.astype(bf16), grad, 0, 0)
        kg_ref[0, :, at] = dot(sg, q, 0, 0)


def body(
    queries, enc_keys, enc_values, enc_lengths, out_proj, residual, norm_gain, head_weight, targets
):
    n_seq, n_vocab, n_dp = lax.axis_size("seq"), lax.axis_size("vocab"), lax.axis_size("dp")
    seq, voc = lax.axis_index("seq"), lax.axis_index("vocab")
    tgt_rows, features = queries.shape[1:]
    enc = enc_keys.shape[1]
    rows = tgt_rows * n_seq
    own_rows = rows // n_vocab
    width, cols = head_weight.shape
    full_width = width * n_seq
    tiles = -(-cols // TILE)
    per = 2 * -(-tiles // (2 * MAX_CHUNKS))
    assert tiles % 2 == 0
    chunks = [(t, min(per, tiles - t)) for t in range(0, tiles, per)]
    firsts = [t * TILE for t, _ in chunks]
    gain = norm_gain.reshape(1, width)
    weight = head_weight.T

    start = lax.rem(voc * own_rows - seq * tgt_rows + rows, rows).astype(i32)
    scal = jnp.stack([start, enc_lengths[0] - seq * enc, voc * cols]).astype(i32)

    q_parts = gather_ring(queries, "seq")
    res_own = lax.dynamic_slice(residual[0], (voc * own_rows, 0), (own_rows, width))
    o_part, q_all = pl.pallas_call(
        functools.partial(attend_kernel, n_seq),
        out_shape=[sds((rows, features + LANES), bf16), sds((rows, features), bf16)],
        in_specs=[SMEM] + [VMEM] * (n_seq + 3),
        out_specs=[VMEM, VMEM],
        scratch_shapes=[
            pltpu.VMEM((2 * rows, features), bf16),
            pltpu.VMEM((2 * rows, LANES), f32),
        ],
        compiler_params=params(),
        cost_estimate=cost(0, 7 * 1024 * 1024),
        name="attend",
    )(scal, *q_parts, targets, enc_keys, enc_values)

    o_all = gather_ring(o_part, "seq")
    ptile = min(TILE, width)
    whole = lambda shape: pl.BlockSpec(shape, lambda j: (0, 0))
    anywhere = pl.BlockSpec(memory_space=pl.ANY)
    mixed_part, mixed_own, att, lse, tgt = pl.pallas_call(
        functools.partial(project_kernel, n_seq, own_rows, ptile),
        out_shape=[
            sds((rows, width), bf16),
            sds((own_rows, width), f32),
            sds((rows, features), bf16),
            sds((rows, LANES), f32),
            sds((rows, LANES), i32),
        ],
        in_specs=[SMEM] + [VMEM] * n_seq + [anywhere],
        out_specs=[VMEM] * 5,
        scratch_shapes=[
            pltpu.VMEM((features, width), bf16),
            pltpu.SemaphoreType.DMA((width // ptile,)),
        ],
        compiler_params=params(),
        cost_estimate=cost(0, 7 * 1024 * 1024),
        name="project",
    )(scal, *o_all, out_proj)

    got = scatter_ring(mixed_part, "vocab", own_rows)
    mixed, ng_own = pl.pallas_call(
        functools.partial(norm_kernel, len(got)),
        out_shape=[sds((own_rows, width), f32), sds((own_rows, width + LANES), bf16)],
        in_specs=[VMEM] * (3 + len(got)),
        out_specs=[VMEM, VMEM],
        compiler_params=params(),
        cost_estimate=cost(0, 7 * 1024 * 1024),
        name="norm",
    )(mixed_own, *got, res_own, gain)
    ng_parts = gather_ring(ng_own, "vocab")

    last_part = pl.BlockSpec((PART, width), lambda j: (-(-cols // PART) - 1, 0))

    def in_vmem(shapes, odd):
        if not odd:
            return [VMEM] * len(shapes)
        return [pl.BlockSpec(x.shape, lambda j: (0, 0)) for x in shapes]

    weights = [weight, weight]
    codes, stats = [], []
    for c, (tile0, n) in enumerate(chunks):
        size = n * TILE
        odd = tile0 * TILE + size > cols and cols % 16 != 0
        edge = last_part if odd else anywhere
        stacked = [] if c else [sds((rows, width), bf16)]
        shapes = [sds((rows, size), jnp.int16), sds((rows, LANES), f32)] + stacked
        outs = pl.pallas_call(
            functools.partial(logits_kernel, tile0 * TILE, cols, n_vocab),
            grid=(1,) if odd else (),
            out_shape=shapes,
            in_specs=in_vmem(ng_parts, odd) + [anywhere, edge],
            out_specs=in_vmem(shapes, odd),
            scratch_shapes=[
                pltpu.VMEM((rows, size), f32),
                pltpu.VMEM((size, width), bf16),
                pltpu.SemaphoreType.DMA((size // PART,)),
            ],
            compiler_params=params(),
            cost_estimate=cost(2 * 256 * width * size, 2 * width * size),
            name="logits",
        )(*ng_parts, *weights)
        codes.append(gather_ring(outs[0], "seq"))
        stats.append(gather_ring(outs[1], "seq"))
        if stacked:
            ng_dp = gather_swaps(outs[2], "dp")

    if len(chunks) > 1:
        codes[1], ng_dp = lax.optimization_barrier((codes[1], ng_dp))
    acc = st = None
    exps = []
    for c, (tile0, n) in enumerate(chunks):
        size = n * TILE
        first = tile0 * TILE
        odd = first + size > cols and cols % 16 != 0
        edge = last_part if odd else anywhere
        estimate = cost(2 * 256 * width * size, 2 * width * size)
        acc_shape, e_shape = sds((2 * rows, width), f32), sds((rows, size), bf16)
        st_shape = sds((rows, LANES), f32)
        buffers = [
            pltpu.VMEM((size, width), bf16),
            pltpu.SemaphoreType.DMA((size // PART,)),
        ]
        prev = [st] if c else []
        ins = [*codes[c], *stats[c], tgt, *prev]
        if c == 0 or c < len(chunks) - 1:
            acc, e, st = pl.pallas_call(
                functools.partial(hidden_kernel, c, first, cols, n_seq, full_width),
                grid=(1,) if odd else (),
                out_shape=[acc_shape, e_shape, st_shape],
                in_specs=in_vmem(ins + ([acc] if c else []), odd) + [anywhere, edge],
                out_specs=in_vmem([acc_shape, e_shape, st_shape], odd),
                scratch_shapes=[pltpu.VMEM((2 * rows, size), bf16)] + buffers,
                compiler_params=params(),
                cost_estimate=estimate,
                name="hidden",
            )(*ins, *([acc] if c else []), *weights)
            st_all = gather_ring(st, "vocab") if c == len(chunks) - 1 else None
        else:
            before = st
            e, st, left = pl.pallas_call(
                functools.partial(last_exp_kernel, c, first, cols, n_seq, full_width),
                out_shape=[e_shape, st_shape, sds((2 * rows, size), bf16)],
                in_specs=[VMEM] * len(ins),
                out_specs=[VMEM] * 3,
                compiler_params=params(),
                cost_estimate=cost(0, 4 * 1024 * 1024),
                name="last_exp",
            )(*ins)
            st_all = gather_ring(st, "vocab")
            acc = pl.pallas_call(
                functools.partial(last_hidden_kernel, c, first, cols),
                grid=(1,) if odd else (),
                out_shape=acc_shape,
                in_specs=in_vmem([before, st, left, acc], odd) + [anywhere, edge],
                out_specs=in_vmem([acc_shape], odd)[0],
                scratch_shapes=buffers,
                compiler_params=params(),
                cost_estimate=estimate,
                name="last_hidden",
            )(before, st, left, acc, *weights)
        exps.append(e)

    hidden_part, hidden_own, coef = pl.pallas_call(
        functools.partial(total_kernel, n_vocab, own_rows),
        out_shape=[
            sds((rows, width), bf16),
            sds((own_rows, width), f32),
            sds((rows, LANES), f32),
        ],
        in_specs=[VMEM] * (n_vocab + 1),
        out_specs=[VMEM] * 3,
        compiler_params=params(),
        cost_estimate=cost(0, 7 * 1024 * 1024),
        name="total",
    )(*st_all, acc)
    got = scatter_ring(hidden_part, "vocab", own_rows)
    got, coef_later = lax.optimization_barrier((got, coef))

    group = tiles * TILE // GROUPS
    assert cols + 3 <= tiles * TILE and group % HEAD_TILE == 0
    grads = pl.pallas_call(
        functools.partial(grad_kernel, firsts, GROUPS),
        out_shape=[sds((rows, group), bf16)] * GROUPS,
        in_specs=[VMEM] * (2 + len(exps)),
        out_specs=[VMEM] * GROUPS,
        compiler_params=params(),
        cost_estimate=cost(0, 7 * 1024 * 1024),
        name="logit_grad",
    )(coef_later, tgt, *exps)
    bit = n_dp // 2
    across = [swap(g, "dp", bit) for g in grads] if bit else []
    gated, inner = pl.pallas_call(
        functools.partial(gate_kernel, len(got)),
        out_shape=[sds((own_rows, width), f32), sds((own_rows, LANES), f32)],
        in_specs=[VMEM] * (3 + len(got)),
        out_specs=[VMEM, VMEM],
        compiler_params=params(),
        cost_estimate=cost(0, 7 * 1024 * 1024),
        name="gate",
    )(hidden_own, *got, mixed, gain)
    inner_all = gather_ring(inner, "seq")
    mixed_grad = pl.pallas_call(
        functools.partial(mixed_grad_kernel, n_seq, full_width),
        out_shape=sds((own_rows, width), bf16),
        in_specs=[VMEM] * (3 + n_seq),
        out_specs=VMEM,
        compiler_params=params(),
        cost_estimate=cost(0, 7 * 1024 * 1024),
        name="mixed_grad",
    )(gated, mixed, coef, *inner_all)
    mg_parts = gather_ring(mixed_grad, "vocab")

    ftile = min(256, features)
    back_part = pl.pallas_call(
        back_project_kernel,
        grid=(features // ftile,),
        out_shape=sds((rows, features), bf16),
        in_specs=[whole((own_rows, width))] * n_vocab
        + [pl.BlockSpec((ftile, width), lambda j: (j, 0))],
        out_specs=pl.BlockSpec((rows, ftile), lambda j: (0, j)),
        compiler_params=params(),
        cost_estimate=cost(0, 7 * 1024 * 1024),
        name="back_project",
    )(*mg_parts, out_proj)
    back_all = gather_ring(back_part, "seq")
    back_all, across = lax.optimization_barrier((back_all, across))
    grads_dp = []
    for i, g in enumerate(grads):
        held, bit = ([g, across[i]] if across else [g]), n_dp // 4
        while bit:
            held = held + [swap(h, "dp", bit) for h in held]
            bit //= 2
        grads_dp.append(held)
    key_grad, value_grad = pl.pallas_call(
        functools.partial(attend_back_kernel, n_seq),
        out_shape=[sds(enc_keys.shape, f32), sds(enc_values.shape, f32)],
        in_specs=[SMEM] + [VMEM] * (n_seq + 5),
        out_specs=[VMEM, VMEM],
        compiler_params=params(),
        cost_estimate=cost(0, 7 * 1024 * 1024),
        name="attend_back",
    )(scal, *back_all, q_all, enc_keys, enc_values, att, lse)

    loss = pl.pallas_call(
        functools.partial(loss_kernel, n_dp * rows),
        grid=(1,),
        out_shape=sds((8, LANES), f32),
        in_specs=[pl.BlockSpec((rows, LANES), lambda j: (0, group // LANES - 1))] * n_dp,
        out_specs=whole((8, LANES)),
        compiler_params=params(),
        cost_estimate=cost(0, 7 * 1024 * 1024),
        name="loss",
    )(*grads_dp[-1])
    mean_loss = loss[0, 0]

    head = None
    for c in range(GROUPS):
        prev = [head] if c else []
        steps = group // HEAD_TILE
        head = pl.pallas_call(
            functools.partial(head_kernel, n_dp),
            grid=(steps,),
            out_shape=sds((cols, width), bf16),
            in_specs=[whole((rows, width))] * n_dp
            + [pl.BlockSpec((rows, HEAD_TILE), lambda j: (0, j))] * n_dp
            + [anywhere] * len(prev),
            out_specs=pl.BlockSpec((HEAD_TILE, width), lambda j, t=c * steps: (t + j, 0)),
            scratch_shapes=[
                pltpu.VMEM((n_dp * rows, width), bf16),
                pltpu.VMEM((HEAD_TILE, n_dp * rows), bf16),
            ],
            input_output_aliases={2 * n_dp: 0} if c else {},
            compiler_params=params(),
            cost_estimate=cost(2 * n_dp * rows * width * group, 2 * width * group),
            name="head_grad",
        )(*ng_dp, *grads_dp[c], *prev)
    return (mean_loss, head.T, key_grad, value_grad)


def solution(mesh):
    placed = (
        P("dp", "seq", "vocab"),
        P("dp", "seq", "vocab"),
        P("dp", "seq", "vocab"),
        P("dp"),
        P("vocab", "seq"),
        P("dp", None, "seq"),
        P("seq"),
        P("seq", "vocab"),
        P("dp", "seq"),
    )
    return jax.shard_map(
        body,
        mesh=mesh,
        in_specs=placed,
        out_specs=(P(), P("seq", "vocab"), P("dp", "seq", "vocab"), P("dp", "seq", "vocab")),
        check_vma=False,
    )
```

```python
import functools
import jax
import jax.numpy as jnp
from jax import lax
from jax.experimental import pallas as pl
from jax.experimental.pallas import tpu as pltpu
from jax.sharding import PartitionSpec as P

HDIM = 256
LANES = 128
TILE = 512
PARTS = 4
PART = TILE // PARTS
HEAD_TILE = 2 * TILE
MAX_CHUNKS = 3
GROUPS = 1
LOW = -1e30
CODE_TOP = 32767.0

zloss_weight = 0.0001
norm_epsilon = 1e-06
score_scale = HDIM ** (-0.5)
f32, bf16, i32 = jnp.float32, jnp.bfloat16, jnp.int32

VMEM = pl.BlockSpec(memory_space=pltpu.VMEM)
SMEM = pl.BlockSpec(memory_space=pltpu.SMEM)


def sds(shape, dtype):
    return jax.ShapeDtypeStruct(shape, dtype)


def params(mib=40):
    return pltpu.CompilerParams(vmem_limit_bytes=mib * 1024 * 1024)


def cost(flops, nbytes):
    return pl.CostEstimate(flops=int(flops), bytes_accessed=int(nbytes), transcendentals=0)


def dot(a, b, ca, cb):
    return lax.dot_general(a, b, (((ca,), (cb,)), ((), ())), preferred_element_type=f32)


def from_ahead(x, axis, k):
    n = lax.axis_size(axis)
    return lax.ppermute(x, axis, [((i + k) % n, i) for i in range(n)])


def gather_ring(x, axis):
    return [x] + [from_ahead(x, axis, k) for k in range(1, lax.axis_size(axis))]


def swap(x, axis, bit):
    n = lax.axis_size(axis)
    return lax.ppermute(x, axis, [(i, i ^ bit) for i in range(n)])


def gather_pairs(x, axis):
    return [x] + [swap(x, axis, k) for k in range(1, lax.axis_size(axis))]


def scatter_pairs(x, axis, rows):
    n = lax.axis_size(axis)
    return [swap(x[k * rows : (k + 1) * rows], axis, k) for k in range(1, n)]


def spread(held, axis, bit):
    while bit:
        held = held + [swap(h, axis, bit) for h in held]
        bit //= 2
    return held


def tree(terms, op=jnp.add):
    while len(terms) > 1:
        half = len(terms) // 2
        rest = terms[2 * half :]
        terms = [op(terms[i], terms[i + half]) for i in range(half)] + rest
    return terms[0]


def three_parts(x):
    hi = x.astype(bf16).astype(f32)
    mid = (x - hi).astype(bf16).astype(f32)
    return hi, mid, x - hi - mid


def lanes(rows):
    return lax.broadcasted_iota(i32, (rows, LANES), 1)


def attend_kernel(n_seq, n_vocab, scal, *refs):
    q_refs = refs[:n_seq]
    tgt_ref, k_ref, v_ref, o_ref, q_out, q_rows, t_rows = refs[n_seq:]
    tgt_rows = q_refs[0].shape[1]
    rows = tgt_rows * n_seq
    enc, features = k_ref.shape[1:]
    for i, r in enumerate(q_refs):
        q_rows[i * tgt_rows : (i + 1) * tgt_rows, :] = r[0]
    own_rows = rows // n_vocab
    blocks = [pl.ds(pl.multiple_of(scal[2 + k], 16), own_rows) for k in range(n_vocab)]
    q = jnp.concatenate([q_rows[b, :] for b in blocks], axis=0)
    q_out[...] = q
    valid = lax.broadcasted_iota(i32, (rows, enc), 1) < scal[0]
    lane = lanes(rows)
    corner = (tgt_rows, tgt_rows)
    same = lax.broadcasted_iota(i32, corner, 0) == lax.broadcasted_iota(i32, corner, 1)
    here = lanes(tgt_rows)
    digits = jnp.zeros((tgt_rows, LANES), f32)
    ids = jnp.broadcast_to(tgt_ref[...], corner)
    for at, digit in ((LANES - 2, ids >> 8), (LANES - 1, ids & 255)):
        column = jnp.sum(jnp.where(same, digit.astype(f32), 0.0), axis=1, keepdims=True)
        digits = jnp.where(here == at, column, digits)
    t_rows[...] = jnp.zeros_like(t_rows)
    t_rows[:tgt_rows, :] = digits
    stat = jnp.concatenate([t_rows[b, :] for b in blocks], axis=0)
    for h in range(features // HDIM):
        at = slice(h * HDIM, (h + 1) * HDIM)
        scores = dot(q[:, at], k_ref[0, :, at], 1, 1) * score_scale
        scores = jnp.where(valid, scores, LOW)
        peak = jnp.max(scores, axis=1, keepdims=True)
        e = jnp.where(valid, jnp.exp(scores - peak), 0.0)
        total = jnp.sum(e, axis=1, keepdims=True)
        some = total > 0.0
        safe = jnp.where(some, total, 1.0)
        o = dot(e.astype(bf16), v_ref[0, :, at], 1, 0) / safe
        o_ref[:, at] = o.astype(bf16)
        lse = jnp.where(some, peak + jnp.log(safe), LOW)
        for i, part in enumerate(three_parts(lse)):
            stat = jnp.where(lane == 3 * h + i, part, stat)
    o_ref[:, features:] = stat.astype(bf16)


def project_kernel(n_seq, own_rows, ptile, scal, *refs):
    o_refs = refs[:n_seq]
    p_ref, mixed_ref, own_ref, att_ref, lse_ref, tgt_ref, p_buf, sems = refs[n_seq:]
    rows, features = att_ref.shape
    columns = [pl.ds(at, ptile) for at in range(0, p_buf.shape[1], ptile)]
    copies = [
        pltpu.make_async_copy(p_ref.at[:, c], p_buf.at[:, c], sems.at[i])
        for i, c in enumerate(columns)
    ]
    for c in copies:
        c.start()
    stats = [r[:, features:].astype(f32) for r in o_refs]
    lane = lanes(rows)
    lse_all = jnp.zeros((rows, LANES), f32)
    for h in range(features // HDIM):
        at = slice(h * HDIM, (h + 1) * HDIM)
        lses = [
            s[:, 3 * h : 3 * h + 1] + s[:, 3 * h + 1 : 3 * h + 2] + s[:, 3 * h + 2 : 3 * h + 3]
            for s in stats
        ]
        top = tree(lses, jnp.maximum)
        lse = top + jnp.log(tree([jnp.exp(x - top) for x in lses]))
        o = tree([jnp.exp(x - lse) * r[:, at].astype(f32) for x, r in zip(lses, o_refs)])
        att_ref[:, at] = o.astype(bf16)
        lse_all = jnp.where(lane == h, lse, lse_all)
    lse_ref[...] = lse_all
    ids = tree([s[:, LANES - 2 : LANES - 1] * 256.0 + s[:, LANES - 1 :] for s in stats])
    tgt_ref[...] = jnp.broadcast_to(ids.astype(i32), (rows, LANES)) - scal[1]
    for c, copy in zip(columns, copies):
        copy.wait()
        part = dot(att_ref[...], p_buf[:, c], 1, 0)
        mixed_ref[:, c] = part.astype(bf16)
        own_ref[:, c] = part[:own_rows]


def norm_kernel(n_got, *refs):
    own_ref, got_refs = refs[0], refs[1 : 1 + n_got]
    residual_ref, gain_ref, mixed_ref, ng_ref = refs[1 + n_got :]
    rows, width = mixed_ref.shape
    mixed = own_ref[...] + residual_ref[...].astype(f32)
    for r in got_refs:
        mixed = mixed + r[...].astype(f32)
    mixed_ref[...] = mixed
    ng_ref[:, :width] = (mixed * gain_ref[...]).astype(bf16)
    square = jnp.sum(mixed * mixed, axis=1, keepdims=True)
    lane = lanes(rows)
    stat = jnp.zeros((rows, LANES), f32)
    for i, part in enumerate(three_parts(square)):
        stat = jnp.where(lane == i, part, stat)
    ng_ref[:, width:] = stat.astype(bf16)


def start_weights(first, cols, w_ref, edge_ref, buf, sems):
    copies = []
    for i in range(buf.shape[0] // PART):
        at = first + i * PART
        n = PART if at + PART <= cols else cols - at
        if n == PART or (n > 0 and cols % 16 == 0):
            here = buf.at[i * PART : i * PART + n]
            copies.append(pltpu.make_async_copy(w_ref.at[at : at + n], here, sems.at[i]))
    for c in copies:
        c.start()
    for i in range(buf.shape[0] // PART):
        n = min(max(cols - first - i * PART, 0), PART)
        if n == PART:
            continue
        if i < len(copies):
            buf[i * PART + n : (i + 1) * PART, :] = jnp.zeros((PART - n, buf.shape[1]), bf16)
        elif n:
            rows = lax.broadcasted_iota(i32, (PART, 1), 0)
            edge = edge_ref[...]
            buf[i * PART : (i + 1) * PART, :] = jnp.where(rows < n, edge, jnp.zeros_like(edge))
        else:
            buf[i * PART : (i + 1) * PART, :] = jnp.zeros((PART, buf.shape[1]), bf16)
    return copies


def wait_tile(copies, t):
    for c in copies[t * PARTS : (t + 1) * PARTS]:
        c.wait()


def logits_kernel(first, cols, n_vocab, *refs):
    ng_refs, (w_ref, edge_ref) = refs[:n_vocab], refs[n_vocab : n_vocab + 2]
    outs = refs[n_vocab + 2 :]
    code_ref, stat_ref = outs[:2]
    z, buf, sems = outs[-3:]
    width = buf.shape[1]
    copies = start_weights(first, cols, w_ref, edge_ref, buf, sems)
    ng = jnp.concatenate([r[...] for r in ng_refs], axis=0)
    if len(outs) > 5:
        outs[2][...] = ng[:, :width]
    for t in range(z.shape[1] // TILE):
        wait_tile(copies, t)
        at = slice(t * TILE, (t + 1) * TILE)
        z[:, at] = dot(ng[:, :width], buf[at, :], 1, 1)
    val = z[...]
    peak = jnp.maximum(jnp.max(jnp.abs(val), axis=1, keepdims=True), 1e-30)
    code_ref[...] = jnp.round(val * (CODE_TOP / peak)).astype(i32).astype(jnp.int16)
    s = ng[:, width:].astype(f32)
    square = s[:, 0:1] + s[:, 1:2] + s[:, 2:3]
    lane = lanes(z.shape[0])
    stat_ref[...] = jnp.where(lane == 0, peak / CODE_TOP, jnp.where(lane == 1, square, 0.0))


def exp_rows(chunk, first, cols, n_seq, features, refs, e_ref, st_ref, lhs):
    code_refs, sc_refs, tgt_ref = refs[:n_seq], refs[n_seq : 2 * n_seq], refs[2 * n_seq]
    rows, size = e_ref.shape
    z = tree([c[...].astype(i32).astype(f32) * s[:, 0:1] for c, s in zip(code_refs, sc_refs)])
    square = tree([s[:, 1:2] for s in sc_refs])
    inv = lax.rsqrt(square / features + norm_epsilon)
    z = z * inv
    at = first + lax.broadcasted_iota(i32, (rows, size), 1)
    hit = at == tgt_ref[:, 0:1]
    if first + size > cols:
        z = jnp.where(at < cols, z, LOW)
        hit = hit & (at < cols)
    here = jnp.sum(jnp.where(hit, z, 0.0), axis=1, keepdims=True)
    peak = jnp.max(z, axis=1, keepdims=True)
    if chunk:
        old = refs[2 * n_seq + 1][...]
        peak = jnp.maximum(peak, old[:, 0:1])
        fade = jnp.exp(old[:, 0:1] - peak)
    else:
        old = jnp.zeros((rows, LANES), f32)
        fade = jnp.zeros((rows, 1), f32)
    e = jnp.exp(z - peak)
    total = jnp.sum(e, axis=1, keepdims=True) + old[:, 1:2] * fade
    eh = e.astype(bf16)
    e_ref[...] = eh
    lhs[:rows, :] = eh
    lhs[rows:, :] = hit.astype(f32).astype(bf16)
    lane = lanes(rows)
    st = jnp.where(lane == 0, peak, old)
    st = jnp.where(lane == 1, total, st)
    st = jnp.where(lane == 2, here + old[:, 2:3], st)
    st = jnp.where(lane == 3, inv, st)
    st_ref[...] = jnp.where(lane == 8 + chunk, peak, st)
    return fade


def hidden_sum(chunk, copies, buf, lhs, acc_prev, fade, acc_ref):
    rows = acc_ref.shape[0] // 2
    if chunk:
        acc_ref[:rows, :] = acc_prev[:rows, :] * fade
        acc_ref[rows:, :] = acc_prev[rows:, :]
    for t in range(buf.shape[0] // TILE):
        wait_tile(copies, t)
        at = slice(t * TILE, (t + 1) * TILE)
        part = dot(lhs[:, at], buf[at, :], 1, 0)
        if chunk or t:
            acc_ref[...] += part
        else:
            acc_ref[...] = part


def hidden_kernel(chunk, first, cols, n_seq, features, *refs):
    n = 2 * n_seq + 1 + (1 if chunk else 0)
    ins, refs = refs[:n], refs[n:]
    acc_prev = None
    if chunk:
        acc_prev, refs = refs[0], refs[1:]
    w_ref, edge_ref, acc_ref, e_ref, st_ref, lhs, buf, sems = refs
    copies = start_weights(first, cols, w_ref, edge_ref, buf, sems)
    fade = exp_rows(chunk, first, cols, n_seq, features, ins, e_ref, st_ref, lhs)
    hidden_sum(chunk, copies, buf, lhs, acc_prev, fade, acc_ref)


def last_exp_kernel(chunk, first, cols, n_seq, features, *refs):
    ins, (e_ref, st_ref, lhs_ref) = refs[:-3], refs[-3:]
    exp_rows(chunk, first, cols, n_seq, features, ins, e_ref, st_ref, lhs_ref)


def last_hidden_kernel(
    chunk, first, cols, st_prev, st_ref, lhs_ref, acc_prev, w_ref, edge_ref, acc_ref, buf, sems
):
    copies = start_weights(first, cols, w_ref, edge_ref, buf, sems)
    fade = jnp.exp(st_prev[:, 0:1] - st_ref[:, 0:1])
    hidden_sum(chunk, copies, buf, lhs_ref, acc_prev, fade, acc_ref)


def total_kernel(n_vocab, own_rows, *refs):
    st_refs = refs[:n_vocab]
    acc_ref, part_ref, own_ref, coef_ref = refs[n_vocab:]
    rows = coef_ref.shape[0]
    mine = st_refs[0][...]
    stats = [mine]
    for k in range(1, n_vocab):
        s = st_refs[k][...]
        places = [(i ^ k) * own_rows for i in range(n_vocab)]
        stats.append(jnp.concatenate([s[p : p + own_rows] for p in places], axis=0))
    top = tree([s[:, 0:1] for s in stats], jnp.maximum)
    total = tree([s[:, 1:2] * jnp.exp(s[:, 0:1] - top) for s in stats])
    hit_logit = tree([s[:, 2:3] for s in stats])
    log_total = top + jnp.log(total)
    loss = log_total - hit_logit + zloss_weight * log_total * log_total
    lift = 1.0 + 2.0 * zloss_weight * log_total
    inv = mine[:, 3:4]
    lane = lanes(rows)
    coef = jnp.exp(jnp.minimum(mine - log_total, 30.0)) * lift * inv
    coef = jnp.where(lane >= 8, coef, inv)
    coef_ref[...] = jnp.where(lane == 1, loss, coef)
    scale = jnp.exp(mine[:, 0:1] - log_total) * lift
    part = acc_ref[:rows, :] * scale - acc_ref[rows:, :]
    part_ref[...] = part.astype(bf16)
    own_ref[...] = part[:own_rows]


def grad_kernel(firsts, n_out, coef_ref, tgt_ref, *refs):
    n = len(firsts)
    outs = refs[n : n + n_out]
    inv = coef_ref[:, 0:1]
    for c, first in enumerate(firsts):
        e_ref = refs[c]
        for off in range(0, e_ref.shape[1], TILE):
            e = e_ref[:, off : off + TILE]
            at = first + off + lax.broadcasted_iota(i32, e.shape, 1)
            hit = at == tgt_ref[:, 0:1]
            g = e.astype(f32) * coef_ref[:, 8 + c : 9 + c] - jnp.where(hit, inv, 0.0)
            group, place = divmod(first + off, outs[0].shape[1])
            outs[group][:, place : place + TILE] = g.astype(bf16)
    last = refs[-1]
    rows, size = last.shape
    lane = lanes(rows)
    stat = last[:, size - LANES :].astype(f32)
    for i, part in enumerate(three_parts(coef_ref[:, 1:2])):
        stat = jnp.where(lane == LANES - 3 + i, part, stat)
    last[:, size - LANES :] = stat.astype(bf16)


def loss_kernel(rows_all, *refs):
    sums = []
    for r in refs[:-1]:
        s = r[...].astype(f32)
        sums.append(jnp.sum(s[:, -3:-2] + s[:, -2:-1] + s[:, -1:]))
    refs[-1][0, 0] = tree(sums) * (1.0 / rows_all)


def head_kernel(n_dp, *refs):
    ng_refs, g_refs = refs[:n_dp], refs[n_dp : 2 * n_dp]
    out_ref, ng, turned = refs[-3:]
    rows, width = ng_refs[0].shape[0], out_ref.shape[1]

    @pl.when(pl.program_id(0) == 0)
    def _():
        for i, r in enumerate(ng_refs):
            ng[i * rows : (i + 1) * rows, :] = r[:, :width]

    turned[...] = jnp.concatenate([r[...] for r in g_refs], axis=0).T
    for at in range(0, width, 256):
        out_ref[:, at : at + 256] = dot(turned[...], ng[:, at : at + 256], 1, 0).astype(bf16)


def gate_kernel(n_got, *refs):
    own_ref, got_refs = refs[0], refs[1 : 1 + n_got]
    mixed_ref, gain_ref, gated_ref, dot_ref = refs[1 + n_got :]
    total = own_ref[...]
    for r in got_refs:
        total = total + r[...].astype(f32)
    gated = total * gain_ref[...]
    gated_ref[...] = gated
    inner = jnp.sum(gated * mixed_ref[...], axis=1, keepdims=True)
    dot_ref[...] = jnp.broadcast_to(inner, dot_ref.shape)


def mixed_grad_kernel(n_seq, features, gated_ref, mixed_ref, coef_ref, *refs):
    dot_refs, out_ref = refs[:n_seq], refs[n_seq]
    inner = tree([r[:, 0:1] for r in dot_refs])
    inv = coef_ref[: out_ref.shape[0], 0:1]
    out = gated_ref[...] * inv - mixed_ref[...] * (inv * inv * inv * inner / features)
    out_ref[...] = out.astype(bf16)


def back_project_kernel(*refs):
    mg_refs, p_ref, out_ref = refs[:-2], refs[-2], refs[-1]
    mg = jnp.concatenate([r[...] for r in mg_refs], axis=0)
    out_ref[...] = dot(mg, p_ref[...], 1, 1).astype(bf16)


def attend_back_kernel(n_seq, scal, *refs):
    a_refs = refs[:n_seq]
    q_ref, k_ref, v_ref, att_ref, lse_ref, kg_ref, vg_ref = refs[n_seq:]
    enc, features = k_ref.shape[1:]
    rows = q_ref.shape[0]
    valid = lax.broadcasted_iota(i32, (rows, enc), 1) < scal[0]
    for h in range(features // HDIM):
        at = slice(h * HDIM, (h + 1) * HDIM)
        grad = tree([r[:, at].astype(f32) for r in a_refs]).astype(bf16)
        q = q_ref[:, at]
        scores = dot(q, k_ref[0, :, at], 1, 1) * score_scale
        w = jnp.where(valid, jnp.exp(jnp.minimum(scores - lse_ref[:, h : h + 1], 0.5)), 0.0)
        prob_grad = dot(grad, v_ref[0, :, at], 1, 1)
        inner = jnp.sum(grad.astype(f32) * att_ref[:, at].astype(f32), axis=1, keepdims=True)
        sg = (w * (prob_grad - inner) * score_scale).astype(bf16)
        vg_ref[0, :, at] = dot(w.astype(bf16), grad, 0, 0)
        kg_ref[0, :, at] = dot(sg, q, 0, 0)


def body(
    queries, enc_keys, enc_values, enc_lengths, out_proj, residual, norm_gain, head_weight, targets
):
    n_seq, n_vocab, n_dp = lax.axis_size("seq"), lax.axis_size("vocab"), lax.axis_size("dp")
    seq, voc = lax.axis_index("seq"), lax.axis_index("vocab")
    tgt_rows, features = queries.shape[1:]
    enc = enc_keys.shape[1]
    rows = tgt_rows * n_seq
    own_rows = rows // n_vocab
    width, cols = head_weight.shape
    full_width = width * n_seq
    tiles = -(-cols // TILE)
    per = 2 * -(-tiles // (2 * MAX_CHUNKS))
    assert tiles % 2 == 0
    chunks = [(t, min(per, tiles - t)) for t in range(0, tiles, per)]
    firsts = [t * TILE for t, _ in chunks]
    gain = norm_gain.reshape(1, width)
    weight = head_weight.T

    starts = [
        lax.rem((voc ^ k) * own_rows - seq * tgt_rows + rows, rows) for k in range(n_vocab)
    ]
    scal = jnp.stack([enc_lengths[0] - seq * enc, voc * cols] + starts).astype(i32)

    q_parts = gather_ring(queries, "seq")
    res_own = lax.dynamic_slice(residual[0], (voc * own_rows, 0), (own_rows, width))
    o_part, q_all = pl.pallas_call(
        functools.partial(attend_kernel, n_seq, n_vocab),
        out_shape=[sds((rows, features + LANES), bf16), sds((rows, features), bf16)],
        in_specs=[SMEM] + [VMEM] * (n_seq + 3),
        out_specs=[VMEM, VMEM],
        scratch_shapes=[
            pltpu.VMEM((rows, features), bf16),
            pltpu.VMEM((rows, LANES), f32),
        ],
        compiler_params=params(),
        cost_estimate=cost(0, 7 * 1024 * 1024),
        name="attend",
    )(scal, *q_parts, targets, enc_keys, enc_values)

    o_all = gather_ring(o_part, "seq")
    ptile = min(TILE, width)
    whole = lambda shape: pl.BlockSpec(shape, lambda j: (0, 0))
    anywhere = pl.BlockSpec(memory_space=pl.ANY)
    mixed_part, mixed_own, att, lse, tgt = pl.pallas_call(
        functools.partial(project_kernel, n_seq, own_rows, ptile),
        out_shape=[
            sds((rows, width), bf16),
            sds((own_rows, width), f32),
            sds((rows, features), bf16),
            sds((rows, LANES), f32),
            sds((rows, LANES), i32),
        ],
        in_specs=[SMEM] + [VMEM] * n_seq + [anywhere],
        out_specs=[VMEM] * 5,
        scratch_shapes=[
            pltpu.VMEM((features, width), bf16),
            pltpu.SemaphoreType.DMA((width // ptile,)),
        ],
        compiler_params=params(),
        cost_estimate=cost(0, 7 * 1024 * 1024),
        name="project",
    )(scal, *o_all, out_proj)

    got = scatter_pairs(mixed_part, "vocab", own_rows)
    mixed, ng_own = pl.pallas_call(
        functools.partial(norm_kernel, len(got)),
        out_shape=[sds((own_rows, width), f32), sds((own_rows, width + LANES), bf16)],
        in_specs=[VMEM] * (3 + len(got)),
        out_specs=[VMEM, VMEM],
        compiler_params=params(),
        cost_estimate=cost(0, 7 * 1024 * 1024),
        name="norm",
    )(mixed_own, *got, res_own, gain)
    ng_parts = gather_pairs(ng_own, "vocab")

    last_part = pl.BlockSpec((PART, width), lambda j: (-(-cols // PART) - 1, 0))

    def in_vmem(shapes, odd):
        if not odd:
            return [VMEM] * len(shapes)
        return [pl.BlockSpec(x.shape, lambda j: (0, 0)) for x in shapes]

    weights = [weight, weight]
    codes, stats = [], []
    for c, (tile0, n) in enumerate(chunks):
        size = n * TILE
        odd = tile0 * TILE + size > cols and cols % 16 != 0
        edge = last_part if odd else anywhere
        stacked = [] if c else [sds((rows, width), bf16)]
        shapes = [sds((rows, size), jnp.int16), sds((rows, LANES), f32)] + stacked
        outs = pl.pallas_call(
            functools.partial(logits_kernel, tile0 * TILE, cols, n_vocab),
            grid=(1,) if odd else (),
            out_shape=shapes,
            in_specs=in_vmem(ng_parts, odd) + [anywhere, edge],
            out_specs=in_vmem(shapes, odd),
            scratch_shapes=[
                pltpu.VMEM((rows, size), f32),
                pltpu.VMEM((size, width), bf16),
                pltpu.SemaphoreType.DMA((size // PART,)),
            ],
            compiler_params=params(),
            cost_estimate=cost(2 * 256 * width * size, 2 * width * size),
            name="logits",
        )(*ng_parts, *weights)
        codes.append(gather_ring(outs[0], "seq"))
        stats.append(gather_ring(outs[1], "seq"))
        if stacked:
            ng_dp = [outs[2]] + ([swap(outs[2], "dp", n_dp // 2)] if n_dp > 1 else [])

    if len(chunks) > 1:
        codes[1], ng_dp = lax.optimization_barrier((codes[1], ng_dp))
    acc = st = None
    exps = []
    for c, (tile0, n) in enumerate(chunks):
        size = n * TILE
        first = tile0 * TILE
        odd = first + size > cols and cols % 16 != 0
        edge = last_part if odd else anywhere
        estimate = cost(2 * 256 * width * size, 2 * width * size)
        acc_shape, e_shape = sds((2 * rows, width), f32), sds((rows, size), bf16)
        st_shape = sds((rows, LANES), f32)
        buffers = [
            pltpu.VMEM((size, width), bf16),
            pltpu.SemaphoreType.DMA((size // PART,)),
        ]
        prev = [st] if c else []
        ins = [*codes[c], *stats[c], tgt, *prev]
        if c == 0 or c < len(chunks) - 1:
            acc, e, st = pl.pallas_call(
                functools.partial(hidden_kernel, c, first, cols, n_seq, full_width),
                grid=(1,) if odd else (),
                out_shape=[acc_shape, e_shape, st_shape],
                in_specs=in_vmem(ins + ([acc] if c else []), odd) + [anywhere, edge],
                out_specs=in_vmem([acc_shape, e_shape, st_shape], odd),
                scratch_shapes=[pltpu.VMEM((2 * rows, size), bf16)] + buffers,
                compiler_params=params(),
                cost_estimate=estimate,
                name="hidden",
            )(*ins, *([acc] if c else []), *weights)
            st_all = gather_pairs(st, "vocab") if c == len(chunks) - 1 else None
        else:
            before = st
            e, st, left = pl.pallas_call(
                functools.partial(last_exp_kernel, c, first, cols, n_seq, full_width),
                out_shape=[e_shape, st_shape, sds((2 * rows, size), bf16)],
                in_specs=[VMEM] * len(ins),
                out_specs=[VMEM] * 3,
                compiler_params=params(),
                cost_estimate=cost(0, 4 * 1024 * 1024),
                name="last_exp",
            )(*ins)
            st_all = gather_pairs(st, "vocab")
            acc = pl.pallas_call(
                functools.partial(last_hidden_kernel, c, first, cols),
                grid=(1,) if odd else (),
                out_shape=acc_shape,
                in_specs=in_vmem([before, st, left, acc], odd) + [anywhere, edge],
                out_specs=in_vmem([acc_shape], odd)[0],
                scratch_shapes=buffers,
                compiler_params=params(),
                cost_estimate=estimate,
                name="last_hidden",
            )(before, st, left, acc, *weights)
        exps.append(e)

    hidden_part, hidden_own, coef = pl.pallas_call(
        functools.partial(total_kernel, n_vocab, own_rows),
        out_shape=[
            sds((rows, width), bf16),
            sds((own_rows, width), f32),
            sds((rows, LANES), f32),
        ],
        in_specs=[VMEM] * (n_vocab + 1),
        out_specs=[VMEM] * 3,
        compiler_params=params(),
        cost_estimate=cost(0, 7 * 1024 * 1024),
        name="total",
    )(*st_all, acc)
    group = tiles * TILE // GROUPS
    assert cols + 3 <= tiles * TILE and group % HEAD_TILE == 0
    grads = pl.pallas_call(
        functools.partial(grad_kernel, firsts, GROUPS),
        out_shape=[sds((rows, group), bf16)] * GROUPS,
        in_specs=[VMEM] * (2 + len(exps)),
        out_specs=[VMEM] * GROUPS,
        compiler_params=params(),
        cost_estimate=cost(0, 7 * 1024 * 1024),
        name="logit_grad",
    )(coef, tgt, *exps)
    hidden_part, grads = lax.optimization_barrier((hidden_part, grads))
    got = scatter_pairs(hidden_part, "vocab", own_rows)
    bit = n_dp // 2
    across = [swap(g, "dp", bit) for g in grads] if bit else []
    gated, inner = pl.pallas_call(
        functools.partial(gate_kernel, len(got)),
        out_shape=[sds((own_rows, width), f32), sds((own_rows, LANES), f32)],
        in_specs=[VMEM] * (3 + len(got)),
        out_specs=[VMEM, VMEM],
        compiler_params=params(),
        cost_estimate=cost(0, 7 * 1024 * 1024),
        name="gate",
    )(hidden_own, *got, mixed, gain)
    inner_all = gather_ring(inner, "seq")
    mixed_grad = pl.pallas_call(
        functools.partial(mixed_grad_kernel, n_seq, full_width),
        out_shape=sds((own_rows, width), bf16),
        in_specs=[VMEM] * (3 + n_seq),
        out_specs=VMEM,
        compiler_params=params(),
        cost_estimate=cost(0, 7 * 1024 * 1024),
        name="mixed_grad",
    )(gated, mixed, coef, *inner_all)
    mg_parts = gather_pairs(mixed_grad, "vocab")
    if n_vocab > 1:
        mg_parts[1], ng_dp = lax.optimization_barrier((mg_parts[1], ng_dp))
    ng_dp = spread(ng_dp, "dp", n_dp // 4)
    mg_parts, ng_dp = lax.optimization_barrier((mg_parts, ng_dp))

    ftile = min(256, features)
    back_part = pl.pallas_call(
        back_project_kernel,
        grid=(features // ftile,),
        out_shape=sds((rows, features), bf16),
        in_specs=[whole((own_rows, width))] * n_vocab
        + [pl.BlockSpec((ftile, width), lambda j: (j, 0))],
        out_specs=pl.BlockSpec((rows, ftile), lambda j: (0, j)),
        compiler_params=params(),
        cost_estimate=cost(0, 7 * 1024 * 1024),
        name="back_project",
    )(*mg_parts, out_proj)
    back_all = gather_ring(back_part, "seq")
    back_all, across = lax.optimization_barrier((back_all, across))
    grads_dp = []
    for i, g in enumerate(grads):
        grads_dp.append(spread([g, across[i]] if across else [g], "dp", n_dp // 4))
    key_grad, value_grad = pl.pallas_call(
        functools.partial(attend_back_kernel, n_seq),
        out_shape=[sds(enc_keys.shape, f32), sds(enc_values.shape, f32)],
        in_specs=[SMEM] + [VMEM] * (n_seq + 5),
        out_specs=[VMEM, VMEM],
        compiler_params=params(),
        cost_estimate=cost(0, 7 * 1024 * 1024),
        name="attend_back",
    )(scal, *back_all, q_all, enc_keys, enc_values, att, lse)

    loss = pl.pallas_call(
        functools.partial(loss_kernel, n_dp * rows),
        grid=(1,),
        out_shape=sds((1, 1), f32),
        in_specs=[pl.BlockSpec((rows, LANES), lambda j: (0, group // LANES - 1))] * n_dp,
        out_specs=SMEM,
        compiler_params=params(),
        cost_estimate=cost(0, 7 * 1024 * 1024),
        name="loss",
    )(*grads_dp[-1])
    mean_loss = loss.reshape(())

    head = None
    for c in range(GROUPS):
        prev = [head] if c else []
        steps = group // HEAD_TILE
        head = pl.pallas_call(
            functools.partial(head_kernel, n_dp),
            grid=(steps,),
            out_shape=sds((cols, width), bf16),
            in_specs=[whole((rows, width))] * n_dp
            + [pl.BlockSpec((rows, HEAD_TILE), lambda j: (0, j))] * n_dp
            + [anywhere] * len(prev),
            out_specs=pl.BlockSpec((HEAD_TILE, width), lambda j, t=c * steps: (t + j, 0)),
            scratch_shapes=[
                pltpu.VMEM((n_dp * rows, width), bf16),
                pltpu.VMEM((HEAD_TILE, n_dp * rows), bf16),
            ],
            input_output_aliases={2 * n_dp: 0} if c else {},
            compiler_params=params(),
            cost_estimate=cost(2 * n_dp * rows * width * group, 2 * width * group),
            name="head_grad",
        )(*ng_dp, *grads_dp[c], *prev)
    return (mean_loss, head.T, key_grad, value_grad)


def solution(mesh):
    placed = (
        P("dp", "seq", "vocab"),
        P("dp", "seq", "vocab"),
        P("dp", "seq", "vocab"),
        P("dp"),
        P("vocab", "seq"),
        P("dp", None, "seq"),
        P("seq"),
        P("seq", "vocab"),
        P("dp", "seq"),
    )
    return jax.shard_map(
        body,
        mesh=mesh,
        in_specs=placed,
        out_specs=(P(), P("seq", "vocab"), P("dp", "seq", "vocab"), P("dp", "seq", "vocab")),
        check_vma=False,
    )
```

```python
import functools
import jax
import jax.numpy as jnp
from jax import lax
from jax.experimental import pallas as pl
from jax.experimental.pallas import tpu as pltpu
from jax.sharding import PartitionSpec as P

HDIM = 256
LANES = 128
TILE = 512
PARTS = 4
PART = TILE // PARTS
HEAD_TILE = 2 * TILE
MAX_CHUNKS = 3
GROUPS = 1
LOW = -1e30
CODE_TOP = 32767.0
LOG_STEPS = 256.0
FINE_STEPS = 1e7

zloss_weight = 0.0001
norm_epsilon = 1e-06
score_scale = HDIM ** (-0.5)
f32, bf16, i32 = jnp.float32, jnp.bfloat16, jnp.int32

VMEM = pl.BlockSpec(memory_space=pltpu.VMEM)
SMEM = pl.BlockSpec(memory_space=pltpu.SMEM)


def sds(shape, dtype):
    return jax.ShapeDtypeStruct(shape, dtype)


def params(mib=40):
    return pltpu.CompilerParams(vmem_limit_bytes=mib * 1024 * 1024)


def cost(flops, nbytes):
    return pl.CostEstimate(flops=int(flops), bytes_accessed=int(nbytes), transcendentals=0)


def dot(a, b, ca, cb):
    return lax.dot_general(a, b, (((ca,), (cb,)), ((), ())), preferred_element_type=f32)


def from_ahead(x, axis, k):
    n = lax.axis_size(axis)
    return lax.ppermute(x, axis, [((i + k) % n, i) for i in range(n)])


def gather_ring(x, axis):
    return [x] + [from_ahead(x, axis, k) for k in range(1, lax.axis_size(axis))]


def scatter_ring(x, axis, rows):
    n = lax.axis_size(axis)
    return [
        lax.ppermute(x[k * rows : (k + 1) * rows], axis, [(i, (i + k) % n) for i in range(n)])
        for k in range(1, n)
    ]


def swap(x, axis, bit):
    n = lax.axis_size(axis)
    return lax.ppermute(x, axis, [(i, i ^ bit) for i in range(n)])


def spread(held, axis, bit):
    while bit:
        held = held + [swap(h, axis, bit) for h in held]
        bit //= 2
    return held


def tree(terms, op=jnp.add):
    while len(terms) > 1:
        half = len(terms) // 2
        rest = terms[2 * half :]
        terms = [op(terms[i], terms[i + half]) for i in range(half)] + rest
    return terms[0]


def three_parts(x):
    hi = x.astype(bf16).astype(f32)
    mid = (x - hi).astype(bf16).astype(f32)
    return hi, mid, x - hi - mid


def lanes(rows):
    return lax.broadcasted_iota(i32, (rows, LANES), 1)


def attend_kernel(n_seq, scal, *refs):
    q_refs = refs[:n_seq]
    k_ref, v_ref, o_ref, q_out, q_twice, t_twice = refs[n_seq:]
    tgt_rows = q_refs[0].shape[1]
    rows = tgt_rows * n_seq
    enc, features = k_ref.shape[1:]
    for i, r in enumerate(q_refs):
        for at in (i * tgt_rows, rows + i * tgt_rows):
            q_twice[at : at + tgt_rows, :] = r[0]
    q = q_twice[pl.ds(pl.multiple_of(scal[0], 16), rows), :]
    q_out[...] = q
    valid = lax.broadcasted_iota(i32, (rows, enc), 1) < scal[1]
    lane = lanes(rows)
    here = lanes(tgt_rows)
    row = lax.broadcasted_iota(i32, here.shape, 0)
    ids = jnp.zeros(here.shape, i32)
    for i in range(tgt_rows):
        ids = jnp.where(row == i, scal[3 + i], ids)
    digits = jnp.where(here == LANES - 2, ids >> 8, jnp.where(here == LANES - 1, ids & 255, 0))
    digits = digits.astype(f32)
    t_twice[...] = jnp.zeros_like(t_twice)
    t_twice[:tgt_rows, :] = digits
    t_twice[rows : rows + tgt_rows, :] = digits
    stat = t_twice[pl.ds(pl.multiple_of(scal[0], 16), rows), :]
    for h in range(features // HDIM):
        at = slice(h * HDIM, (h + 1) * HDIM)
        scores = dot(q[:, at], k_ref[0, :, at], 1, 1) * score_scale
        scores = jnp.where(valid, scores, LOW)
        peak = jnp.max(scores, axis=1, keepdims=True)
        e = jnp.where(valid, jnp.exp(scores - peak), 0.0)
        total = jnp.sum(e, axis=1, keepdims=True)
        some = total > 0.0
        safe = jnp.where(some, total, 1.0)
        o = dot(e.astype(bf16), v_ref[0, :, at], 1, 0) / safe
        o_ref[:, at] = o.astype(bf16)
        lse = jnp.where(some, peak + jnp.log(safe), LOW)
        for i, part in enumerate(three_parts(lse)):
            stat = jnp.where(lane == 3 * h + i, part, stat)
    o_ref[:, features:] = stat.astype(bf16)


def project_kernel(n_seq, own_rows, ptile, scal, *refs):
    o_refs = refs[:n_seq]
    p_ref, mixed_ref, own_ref, att_ref, lse_ref, tgt_ref, p_buf, sems = refs[n_seq:]
    rows, features = att_ref.shape
    columns = [pl.ds(at, ptile) for at in range(0, p_buf.shape[1], ptile)]
    copies = [
        pltpu.make_async_copy(p_ref.at[:, c], p_buf.at[:, c], sems.at[i])
        for i, c in enumerate(columns)
    ]
    for c in copies:
        c.start()
    stats = [r[:, features:].astype(f32) for r in o_refs]
    lane = lanes(rows)
    lse_all = jnp.zeros((rows, LANES), f32)
    for h in range(features // HDIM):
        at = slice(h * HDIM, (h + 1) * HDIM)
        lses = [
            s[:, 3 * h : 3 * h + 1] + s[:, 3 * h + 1 : 3 * h + 2] + s[:, 3 * h + 2 : 3 * h + 3]
            for s in stats
        ]
        top = tree(lses, jnp.maximum)
        lse = top + jnp.log(tree([jnp.exp(x - top) for x in lses]))
        o = tree([jnp.exp(x - lse) * r[:, at].astype(f32) for x, r in zip(lses, o_refs)])
        att_ref[:, at] = o.astype(bf16)
        lse_all = jnp.where(lane == h, lse, lse_all)
    lse_ref[...] = lse_all
    ids = tree([s[:, LANES - 2 : LANES - 1] * 256.0 + s[:, LANES - 1 :] for s in stats])
    tgt_ref[...] = jnp.broadcast_to(ids.astype(i32), (rows, LANES)) - scal[2]
    for c, copy in zip(columns, copies):
        copy.wait()
        part = dot(att_ref[...], p_buf[:, c], 1, 0)
        mixed_ref[:, c] = part.astype(bf16)
        own_ref[:, c] = part[:own_rows]


def norm_kernel(n_got, *refs):
    own_ref, got_refs = refs[0], refs[1 : 1 + n_got]
    packed_ref, mixed_ref, ng_ref = refs[1 + n_got :]
    rows, width = mixed_ref.shape
    mixed = own_ref[...] + packed_ref[:rows, :]
    for r in got_refs:
        mixed = mixed + r[...].astype(f32)
    mixed_ref[...] = mixed
    ng_ref[:, :width] = (mixed * packed_ref[rows : rows + 1, :]).astype(bf16)
    square = jnp.sum(mixed * mixed, axis=1, keepdims=True)
    lane = lanes(rows)
    stat = jnp.zeros((rows, LANES), f32)
    for i, part in enumerate(three_parts(square)):
        stat = jnp.where(lane == i, part, stat)
    ng_ref[:, width:] = stat.astype(bf16)


def start_weights(first, cols, w_ref, edge_ref, buf, sems):
    copies = []
    for i in range(buf.shape[0] // PART):
        at = first + i * PART
        n = PART if at + PART <= cols else cols - at
        if n == PART or (n > 0 and cols % 16 == 0):
            here = buf.at[i * PART : i * PART + n]
            copies.append(pltpu.make_async_copy(w_ref.at[at : at + n], here, sems.at[i]))
    for c in copies:
        c.start()
    for i in range(buf.shape[0] // PART):
        n = min(max(cols - first - i * PART, 0), PART)
        if n == PART:
            continue
        if i < len(copies):
            buf[i * PART + n : (i + 1) * PART, :] = jnp.zeros((PART - n, buf.shape[1]), bf16)
        elif n:
            rows = lax.broadcasted_iota(i32, (PART, 1), 0)
            edge = edge_ref[...]
            buf[i * PART : (i + 1) * PART, :] = jnp.where(rows < n, edge, jnp.zeros_like(edge))
        else:
            buf[i * PART : (i + 1) * PART, :] = jnp.zeros((PART, buf.shape[1]), bf16)
    return copies


def wait_tile(copies, t):
    for c in copies[t * PARTS : (t + 1) * PARTS]:
        c.wait()


def logits_kernel(first, cols, n_vocab, *refs):
    ng_refs, (w_ref, edge_ref) = refs[:n_vocab], refs[n_vocab : n_vocab + 2]
    outs = refs[n_vocab + 2 :]
    code_ref = outs[0]
    z, buf, sems = outs[-3:]
    width = buf.shape[1]
    copies = start_weights(first, cols, w_ref, edge_ref, buf, sems)
    ng = jnp.concatenate([r[...] for r in ng_refs], axis=0)
    if len(outs) > 4:
        outs[1][...] = ng[:, :width]
    for t in range(z.shape[1] // TILE):
        wait_tile(copies, t)
        at = slice(t * TILE, (t + 1) * TILE)
        z[:, at] = dot(ng[:, :width], buf[at, :], 1, 1)
    val = z[...]
    peak = jnp.maximum(jnp.max(jnp.abs(val), axis=1, keepdims=True), 1e-30)
    s = ng[:, width:].astype(f32)
    square = jnp.maximum(s[:, 0:1] + s[:, 1:2] + s[:, 2:3], 1e-30)
    mark = jnp.floor(jnp.log(peak) * LOG_STEPS) + 2.0
    coarse = jnp.round(jnp.log(square) * LOG_STEPS)
    fine = jnp.round((square / jnp.exp(coarse / LOG_STEPS) - 1.0) * FINE_STEPS)
    size = z.shape[1]
    code = jnp.round(val / code_step(mark))
    code_ref[:, :size] = code.astype(i32).astype(jnp.int16)
    lane = lanes(z.shape[0])
    stat = jnp.where(lane == 0, mark, jnp.where(lane == 1, coarse, jnp.where(lane == 2, fine, 0.0)))
    code_ref[:, size:] = stat.astype(i32).astype(jnp.int16)


def code_step(mark):
    return jnp.exp(mark / LOG_STEPS) / CODE_TOP


def decode(code_ref, size):
    stat = code_ref[:, size:].astype(i32).astype(f32)
    square = jnp.exp(stat[:, 1:2] / LOG_STEPS) * (1.0 + stat[:, 2:3] / FINE_STEPS)
    return code_ref[:, :size].astype(i32).astype(f32) * code_step(stat[:, 0:1]), square


def exp_rows(chunk, first, cols, n_seq, features, refs, e_ref, st_ref, lhs):
    tgt_ref = refs[n_seq]
    rows, size = e_ref.shape
    members = [decode(r, size) for r in refs[:n_seq]]
    z = tree([m[0] for m in members])
    square = tree([m[1] for m in members])
    inv = lax.rsqrt(square / features + norm_epsilon)
    z = z * inv
    at = first + lax.broadcasted_iota(i32, (rows, size), 1)
    hit = at == tgt_ref[:, 0:1]
    if first + size > cols:
        z = jnp.where(at < cols, z, LOW)
        hit = hit & (at < cols)
    here = jnp.sum(jnp.where(hit, z, 0.0), axis=1, keepdims=True)
    peak = jnp.max(z, axis=1, keepdims=True)
    if chunk:
        old = refs[n_seq + 1][...]
        peak = jnp.maximum(peak, old[:, 0:1])
        fade = jnp.exp(old[:, 0:1] - peak)
    else:
        old = jnp.zeros((rows, LANES), f32)
        fade = jnp.zeros((rows, 1), f32)
    e = jnp.exp(z - peak)
    total = jnp.sum(e, axis=1, keepdims=True) + old[:, 1:2] * fade
    eh = e.astype(bf16)
    e_ref[...] = eh
    lhs[:rows, :] = eh
    lhs[rows:, :] = hit.astype(f32).astype(bf16)
    lane = lanes(rows)
    st = jnp.where(lane == 0, peak, old)
    st = jnp.where(lane == 1, total, st)
    st = jnp.where(lane == 2, here + old[:, 2:3], st)
    st = jnp.where(lane == 3, inv, st)
    st_ref[...] = jnp.where(lane == 8 + chunk, peak, st)
    return fade


def hidden_sum(chunk, copies, buf, lhs, acc_prev, fade, acc_ref):
    rows = acc_ref.shape[0] // 2
    if chunk:
        acc_ref[:rows, :] = acc_prev[:rows, :] * fade
        acc_ref[rows:, :] = acc_prev[rows:, :]
    for t in range(buf.shape[0] // TILE):
        wait_tile(copies, t)
        at = slice(t * TILE, (t + 1) * TILE)
        part = dot(lhs[:, at], buf[at, :], 1, 0)
        if chunk or t:
            acc_ref[...] += part
        else:
            acc_ref[...] = part


def hidden_kernel(chunk, first, cols, n_seq, features, *refs):
    n = n_seq + 1 + (1 if chunk else 0)
    ins, refs = refs[:n], refs[n:]
    acc_prev = None
    if chunk:
        acc_prev, refs = refs[0], refs[1:]
    w_ref, edge_ref, acc_ref, e_ref, st_ref, lhs, buf, sems = refs
    copies = start_weights(first, cols, w_ref, edge_ref, buf, sems)
    fade = exp_rows(chunk, first, cols, n_seq, features, ins, e_ref, st_ref, lhs)
    hidden_sum(chunk, copies, buf, lhs, acc_prev, fade, acc_ref)


def last_exp_kernel(chunk, first, cols, n_seq, features, *refs):
    ins, (e_ref, st_ref, lhs_ref) = refs[:-3], refs[-3:]
    exp_rows(chunk, first, cols, n_seq, features, ins, e_ref, st_ref, lhs_ref)


def last_hidden_kernel(
    chunk, first, cols, st_prev, st_ref, lhs_ref, acc_prev, w_ref, edge_ref, acc_ref, buf, sems
):
    copies = start_weights(first, cols, w_ref, edge_ref, buf, sems)
    fade = jnp.exp(st_prev[:, 0:1] - st_ref[:, 0:1])
    hidden_sum(chunk, copies, buf, lhs_ref, acc_prev, fade, acc_ref)


def total_kernel(n_vocab, own_rows, *refs):
    st_refs = refs[:n_vocab]
    acc_ref, part_ref, own_ref, coef_ref = refs[n_vocab:]
    rows = coef_ref.shape[0]
    mine = st_refs[0][...]
    stats = [mine]
    for k in range(1, n_vocab):
        s = st_refs[k][...]
        cut = rows - k * own_rows
        stats.append(jnp.concatenate([s[cut:], s[:cut]], axis=0))
    top = tree([s[:, 0:1] for s in stats], jnp.maximum)
    total = tree([s[:, 1:2] * jnp.exp(s[:, 0:1] - top) for s in stats])
    hit_logit = tree([s[:, 2:3] for s in stats])
    log_total = top + jnp.log(total)
    loss = log_total - hit_logit + zloss_weight * log_total * log_total
    lift = 1.0 + 2.0 * zloss_weight * log_total
    inv = mine[:, 3:4]
    lane = lanes(rows)
    coef = jnp.exp(jnp.minimum(mine - log_total, 30.0)) * lift * inv
    coef = jnp.where(lane >= 8, coef, inv)
    coef_ref[...] = jnp.where(lane == 1, loss, coef)
    scale = jnp.exp(mine[:, 0:1] - log_total) * lift
    part = acc_ref[:rows, :] * scale - acc_ref[rows:, :]
    part_ref[...] = part.astype(bf16)
    own_ref[...] = part[:own_rows]


def grad_kernel(firsts, n_out, coef_ref, tgt_ref, *refs):
    n = len(firsts)
    outs = refs[n : n + n_out]
    inv = coef_ref[:, 0:1]
    for c, first in enumerate(firsts):
        e_ref = refs[c]
        for off in range(0, e_ref.shape[1], TILE):
            e = e_ref[:, off : off + TILE]
            at = first + off + lax.broadcasted_iota(i32, e.shape, 1)
            hit = at == tgt_ref[:, 0:1]
            g = e.astype(f32) * coef_ref[:, 8 + c : 9 + c] - jnp.where(hit, inv, 0.0)
            group, place = divmod(first + off, outs[0].shape[1])
            outs[group][:, place : place + TILE] = g.astype(bf16)
    last = refs[-1]
    rows, size = last.shape
    lane = lanes(rows)
    stat = last[:, size - LANES :].astype(f32)
    for i, part in enumerate(three_parts(coef_ref[:, 1:2])):
        stat = jnp.where(lane == LANES - 3 + i, part, stat)
    last[:, size - LANES :] = stat.astype(bf16)


def head_kernel(n_dp, rows_all, *refs):
    ng_refs, g_refs = refs[:n_dp], refs[n_dp : 2 * n_dp]
    out_ref, loss_ref, ng, turned = refs[-4:]
    rows, width = ng_refs[0].shape[0], out_ref.shape[1]

    @pl.when(pl.program_id(0) == 0)
    def _():
        for i, r in enumerate(ng_refs):
            ng[i * rows : (i + 1) * rows, :] = r[:, :width]

    turned[...] = jnp.concatenate([r[...] for r in g_refs], axis=0).T
    for at in range(0, width, 256):
        out_ref[:, at : at + 256] = dot(turned[...], ng[:, at : at + 256], 1, 0).astype(bf16)

    @pl.when(pl.program_id(0) == pl.num_programs(0) - 1)
    def _():
        sums = []
        for r in g_refs:
            s = r[:, HEAD_TILE - LANES :].astype(f32)
            sums.append(jnp.sum(s[:, -3:-2] + s[:, -2:-1] + s[:, -1:]))
        loss_ref[0, 0] = tree(sums) * (1.0 / rows_all)


def gate_kernel(n_got, *refs):
    own_ref, got_refs = refs[0], refs[1 : 1 + n_got]
    mixed_ref, packed_ref, gated_ref, dot_ref = refs[1 + n_got :]
    total = own_ref[...]
    for r in got_refs:
        total = total + r[...].astype(f32)
    rows = mixed_ref.shape[0]
    gated = total * packed_ref[rows : rows + 1, :]
    gated_ref[...] = gated
    inner = jnp.sum(gated * mixed_ref[...], axis=1, keepdims=True)
    dot_ref[...] = jnp.broadcast_to(inner, dot_ref.shape)


def mixed_grad_kernel(n_seq, features, gated_ref, mixed_ref, coef_ref, *refs):
    dot_refs, out_ref = refs[:n_seq], refs[n_seq]
    inner = tree([r[:, 0:1] for r in dot_refs])
    inv = coef_ref[: out_ref.shape[0], 0:1]
    out = gated_ref[...] * inv - mixed_ref[...] * (inv * inv * inv * inner / features)
    out_ref[...] = out.astype(bf16)


def back_project_kernel(*refs):
    mg_refs, p_ref, out_ref = refs[:-2], refs[-2], refs[-1]
    mg = jnp.concatenate([r[...] for r in mg_refs], axis=0)
    out_ref[...] = dot(mg, p_ref[...], 1, 1).astype(bf16)


def attend_back_kernel(n_seq, scal, *refs):
    a_refs = refs[:n_seq]
    q_ref, k_ref, v_ref, att_ref, lse_ref, kg_ref, vg_ref = refs[n_seq:]
    enc, features = k_ref.shape[1:]
    rows = q_ref.shape[0]
    valid = lax.broadcasted_iota(i32, (rows, enc), 1) < scal[1]
    for h in range(features // HDIM):
        at = slice(h * HDIM, (h + 1) * HDIM)
        grad = tree([r[:, at].astype(f32) for r in a_refs]).astype(bf16)
        q = q_ref[:, at]
        scores = dot(q, k_ref[0, :, at], 1, 1) * score_scale
        w = jnp.where(valid, jnp.exp(jnp.minimum(scores - lse_ref[:, h : h + 1], 0.5)), 0.0)
        prob_grad = dot(grad, v_ref[0, :, at], 1, 1)
        inner = jnp.sum(grad.astype(f32) * att_ref[:, at].astype(f32), axis=1, keepdims=True)
        sg = (w * (prob_grad - inner) * score_scale).astype(bf16)
        vg_ref[0, :, at] = dot(w.astype(bf16), grad, 0, 0)
        kg_ref[0, :, at] = dot(sg, q, 0, 0)


def body(
    queries, enc_keys, enc_values, enc_lengths, out_proj, residual, norm_gain, head_weight, targets
):
    n_seq, n_vocab, n_dp = lax.axis_size("seq"), lax.axis_size("vocab"), lax.axis_size("dp")
    seq, voc = lax.axis_index("seq"), lax.axis_index("vocab")
    tgt_rows, features = queries.shape[1:]
    enc = enc_keys.shape[1]
    rows = tgt_rows * n_seq
    own_rows = rows // n_vocab
    width, cols = head_weight.shape
    full_width = width * n_seq
    tiles = -(-cols // TILE)
    per = 2 * -(-tiles // (2 * MAX_CHUNKS))
    assert tiles % 2 == 0
    chunks = [(t, min(per, tiles - t)) for t in range(0, tiles, per)]
    firsts = [t * TILE for t, _ in chunks]
    gain = norm_gain.reshape(1, width)
    weight = head_weight.T

    start = lax.rem(voc * own_rows - seq * tgt_rows + rows, rows).astype(i32)
    scal = jnp.stack([start, enc_lengths[0] - seq * enc, voc * cols]).astype(i32)
    scal = jnp.concatenate([scal, targets[0]])

    q_parts = gather_ring(queries, "seq")
    res_own = lax.dynamic_slice(residual[0], (voc * own_rows, 0), (own_rows, width)).astype(f32)
    packed = jnp.concatenate([res_own, jnp.broadcast_to(gain, (8, width))], axis=0)
    o_part, q_all = pl.pallas_call(
        functools.partial(attend_kernel, n_seq),
        out_shape=[sds((rows, features + LANES), bf16), sds((rows, features), bf16)],
        in_specs=[SMEM] + [VMEM] * (n_seq + 2),
        out_specs=[VMEM, VMEM],
        scratch_shapes=[
            pltpu.VMEM((2 * rows, features), bf16),
            pltpu.VMEM((2 * rows, LANES), f32),
        ],
        compiler_params=params(),
        cost_estimate=cost(0, 7 * 1024 * 1024),
        name="attend",
    )(scal, *q_parts, enc_keys, enc_values)

    o_all = gather_ring(o_part, "seq")
    ptile = min(TILE, width)
    whole = lambda shape: pl.BlockSpec(shape, lambda j: (0, 0))
    anywhere = pl.BlockSpec(memory_space=pl.ANY)
    mixed_part, mixed_own, att, lse, tgt = pl.pallas_call(
        functools.partial(project_kernel, n_seq, own_rows, ptile),
        out_shape=[
            sds((rows, width), bf16),
            sds((own_rows, width), f32),
            sds((rows, features), bf16),
            sds((rows, LANES), f32),
            sds((rows, LANES), i32),
        ],
        in_specs=[SMEM] + [VMEM] * n_seq + [anywhere],
        out_specs=[VMEM] * 5,
        scratch_shapes=[
            pltpu.VMEM((features, width), bf16),
            pltpu.SemaphoreType.DMA((width // ptile,)),
        ],
        compiler_params=params(),
        cost_estimate=cost(0, 7 * 1024 * 1024),
        name="project",
    )(scal, *o_all, out_proj)

    got = scatter_ring(mixed_part, "vocab", own_rows)
    mixed, ng_own = pl.pallas_call(
        functools.partial(norm_kernel, len(got)),
        out_shape=[sds((own_rows, width), f32), sds((own_rows, width + LANES), bf16)],
        in_specs=[VMEM] * (2 + len(got)),
        out_specs=[VMEM, VMEM],
        compiler_params=params(),
        cost_estimate=cost(0, 7 * 1024 * 1024),
        name="norm",
    )(mixed_own, *got, packed)
    ng_parts = gather_ring(ng_own, "vocab")

    last_part = pl.BlockSpec((PART, width), lambda j: (-(-cols // PART) - 1, 0))

    def in_vmem(shapes, odd):
        if not odd:
            return [VMEM] * len(shapes)
        return [pl.BlockSpec(x.shape, lambda j: (0, 0)) for x in shapes]

    weights = [weight, weight]
    codes = []
    for c, (tile0, n) in enumerate(chunks):
        size = n * TILE
        odd = tile0 * TILE + size > cols and cols % 16 != 0
        edge = last_part if odd else anywhere
        stacked = [] if c else [sds((rows, width), bf16)]
        shapes = [sds((rows, size + LANES), jnp.int16)] + stacked
        outs = pl.pallas_call(
            functools.partial(logits_kernel, tile0 * TILE, cols, n_vocab),
            grid=(1,) if odd else (),
            out_shape=shapes,
            in_specs=in_vmem(ng_parts, odd) + [anywhere, edge],
            out_specs=in_vmem(shapes, odd),
            scratch_shapes=[
                pltpu.VMEM((rows, size), f32),
                pltpu.VMEM((size, width), bf16),
                pltpu.SemaphoreType.DMA((size // PART,)),
            ],
            compiler_params=params(),
            cost_estimate=cost(2 * 256 * width * size, 2 * width * size),
            name="logits",
        )(*ng_parts, *weights)
        codes.append(gather_ring(outs[0], "seq"))
        if stacked:
            ng_dp = [outs[1]] + ([swap(outs[1], "dp", n_dp // 2)] if n_dp > 1 else [])

    codes[-1], ng_dp = lax.optimization_barrier((codes[-1], ng_dp))
    acc = st = None
    exps = []
    for c, (tile0, n) in enumerate(chunks):
        size = n * TILE
        first = tile0 * TILE
        odd = first + size > cols and cols % 16 != 0
        edge = last_part if odd else anywhere
        estimate = cost(2 * 256 * width * size, 2 * width * size)
        acc_shape, e_shape = sds((2 * rows, width), f32), sds((rows, size), bf16)
        st_shape = sds((rows, LANES), f32)
        buffers = [
            pltpu.VMEM((size, width), bf16),
            pltpu.SemaphoreType.DMA((size // PART,)),
        ]
        prev = [st] if c else []
        ins = [*codes[c], tgt, *prev]
        if c == 0 or c < len(chunks) - 1:
            acc, e, st = pl.pallas_call(
                functools.partial(hidden_kernel, c, first, cols, n_seq, full_width),
                grid=(1,) if odd else (),
                out_shape=[acc_shape, e_shape, st_shape],
                in_specs=in_vmem(ins + ([acc] if c else []), odd) + [anywhere, edge],
                out_specs=in_vmem([acc_shape, e_shape, st_shape], odd),
                scratch_shapes=[pltpu.VMEM((2 * rows, size), bf16)] + buffers,
                compiler_params=params(),
                cost_estimate=estimate,
                name="hidden",
            )(*ins, *([acc] if c else []), *weights)
            st_all = gather_ring(st, "vocab") if c == len(chunks) - 1 else None
        else:
            before = st
            e, st, left = pl.pallas_call(
                functools.partial(last_exp_kernel, c, first, cols, n_seq, full_width),
                out_shape=[e_shape, st_shape, sds((2 * rows, size), bf16)],
                in_specs=[VMEM] * len(ins),
                out_specs=[VMEM] * 3,
                compiler_params=params(),
                cost_estimate=cost(0, 4 * 1024 * 1024),
                name="last_exp",
            )(*ins)
            st_all = gather_ring(st, "vocab")
            acc = pl.pallas_call(
                functools.partial(last_hidden_kernel, c, first, cols),
                grid=(1,) if odd else (),
                out_shape=acc_shape,
                in_specs=in_vmem([before, st, left, acc], odd) + [anywhere, edge],
                out_specs=in_vmem([acc_shape], odd)[0],
                scratch_shapes=buffers,
                compiler_params=params(),
                cost_estimate=estimate,
                name="last_hidden",
            )(before, st, left, acc, *weights)
        exps.append(e)

    hidden_part, hidden_own, coef = pl.pallas_call(
        functools.partial(total_kernel, n_vocab, own_rows),
        out_shape=[
            sds((rows, width), bf16),
            sds((own_rows, width), f32),
            sds((rows, LANES), f32),
        ],
        in_specs=[VMEM] * (n_vocab + 1),
        out_specs=[VMEM] * 3,
        compiler_params=params(),
        cost_estimate=cost(0, 7 * 1024 * 1024),
        name="total",
    )(*st_all, acc)
    group = tiles * TILE // GROUPS
    assert cols + 3 <= tiles * TILE and group % HEAD_TILE == 0
    grads = pl.pallas_call(
        functools.partial(grad_kernel, firsts, GROUPS),
        out_shape=[sds((rows, group), bf16)] * GROUPS,
        in_specs=[VMEM] * (2 + len(exps)),
        out_specs=[VMEM] * GROUPS,
        compiler_params=params(),
        cost_estimate=cost(0, 7 * 1024 * 1024),
        name="logit_grad",
    )(coef, tgt, *exps)
    hidden_part, grads = lax.optimization_barrier((hidden_part, grads))
    got = scatter_ring(hidden_part, "vocab", own_rows)
    bit = n_dp // 2
    across = [swap(g, "dp", bit) for g in grads] if bit else []
    gated, inner = pl.pallas_call(
        functools.partial(gate_kernel, len(got)),
        out_shape=[sds((own_rows, width), f32), sds((own_rows, LANES), f32)],
        in_specs=[VMEM] * (3 + len(got)),
        out_specs=[VMEM, VMEM],
        compiler_params=params(),
        cost_estimate=cost(0, 7 * 1024 * 1024),
        name="gate",
    )(hidden_own, *got, mixed, packed)
    inner_all = gather_ring(inner, "seq")
    mixed_grad = pl.pallas_call(
        functools.partial(mixed_grad_kernel, n_seq, full_width),
        out_shape=sds((own_rows, width), bf16),
        in_specs=[VMEM] * (3 + n_seq),
        out_specs=VMEM,
        compiler_params=params(),
        cost_estimate=cost(0, 7 * 1024 * 1024),
        name="mixed_grad",
    )(gated, mixed, coef, *inner_all)
    mg_parts = gather_ring(mixed_grad, "vocab")

    ftile = min(256, features)
    back_part = pl.pallas_call(
        back_project_kernel,
        grid=(features // ftile,),
        out_shape=sds((rows, features), bf16),
        in_specs=[whole((own_rows, width))] * n_vocab
        + [pl.BlockSpec((ftile, width), lambda j: (j, 0))],
        out_specs=pl.BlockSpec((rows, ftile), lambda j: (0, j)),
        compiler_params=params(),
        cost_estimate=cost(0, 7 * 1024 * 1024),
        name="back_project",
    )(*mg_parts, out_proj)
    back_part, ng_dp = lax.optimization_barrier((back_part, ng_dp))
    back_all = gather_ring(back_part, "seq")
    ng_dp = spread(ng_dp, "dp", n_dp // 4)
    back_all, across = lax.optimization_barrier((back_all, across))
    grads_dp = []
    for i, g in enumerate(grads):
        grads_dp.append(spread([g, across[i]] if across else [g], "dp", n_dp // 4))
    key_grad, value_grad = pl.pallas_call(
        functools.partial(attend_back_kernel, n_seq),
        out_shape=[sds(enc_keys.shape, f32), sds(enc_values.shape, f32)],
        in_specs=[SMEM] + [VMEM] * (n_seq + 5),
        out_specs=[VMEM, VMEM],
        compiler_params=params(),
        cost_estimate=cost(0, 7 * 1024 * 1024),
        name="attend_back",
    )(scal, *back_all, q_all, enc_keys, enc_values, att, lse)

    head = None
    for c in range(GROUPS):
        prev = [head] if c else []
        steps = group // HEAD_TILE
        head, loss = pl.pallas_call(
            functools.partial(head_kernel, n_dp, n_dp * rows),
            grid=(steps,),
            out_shape=[sds((cols, width), bf16), sds((1, 1), f32)],
            in_specs=[whole((rows, width))] * n_dp
            + [pl.BlockSpec((rows, HEAD_TILE), lambda j: (0, j))] * n_dp
            + [anywhere] * len(prev),
            out_specs=[
                pl.BlockSpec((HEAD_TILE, width), lambda j, t=c * steps: (t + j, 0)),
                SMEM,
            ],
            scratch_shapes=[
                pltpu.VMEM((n_dp * rows, width), bf16),
                pltpu.VMEM((HEAD_TILE, n_dp * rows), bf16),
            ],
            input_output_aliases={2 * n_dp: 0} if c else {},
            compiler_params=params(),
            cost_estimate=cost(2 * n_dp * rows * width * group, 2 * width * group),
            name="head_grad",
        )(*ng_dp, *grads_dp[c], *prev)
    return (loss.reshape(()), head.T, key_grad, value_grad)


def solution(mesh):
    placed = (
        P("dp", "seq", "vocab"),
        P("dp", "seq", "vocab"),
        P("dp", "seq", "vocab"),
        P("dp"),
        P("vocab", "seq"),
        P("dp", None, "seq"),
        P("seq"),
        P("seq", "vocab"),
        P("dp", "seq"),
    )
    return jax.shard_map(
        body,
        mesh=mesh,
        in_specs=placed,
        out_specs=(P(), P("seq", "vocab"), P("dp", "seq", "vocab"), P("dp", "seq", "vocab")),
        check_vma=False,
    )
```

```python
import functools
import jax
import jax.numpy as jnp
from jax import lax
from jax.experimental import pallas as pl
from jax.experimental.pallas import tpu as pltpu
from jax.sharding import PartitionSpec as P

HDIM = 256
LANES = 128
TILE = 512
PARTS = 4
PART = TILE // PARTS
HEAD_TILE = 2 * TILE
MAX_CHUNKS = 3
GROUPS = 1
LOW = -1e30
CODE_TOP = 32767.0
LOG_STEPS = 256.0
FINE_STEPS = 1e7

zloss_weight = 0.0001
norm_epsilon = 1e-06
score_scale = HDIM ** (-0.5)
f32, bf16, i32 = jnp.float32, jnp.bfloat16, jnp.int32

VMEM = pl.BlockSpec(memory_space=pltpu.VMEM)
SMEM = pl.BlockSpec(memory_space=pltpu.SMEM)


def sds(shape, dtype):
    return jax.ShapeDtypeStruct(shape, dtype)


def params(mib=40):
    return pltpu.CompilerParams(vmem_limit_bytes=mib * 1024 * 1024)


def cost(flops, nbytes):
    return pl.CostEstimate(flops=int(flops), bytes_accessed=int(nbytes), transcendentals=0)


def dot(a, b, ca, cb):
    return lax.dot_general(a, b, (((ca,), (cb,)), ((), ())), preferred_element_type=f32)


def from_ahead(x, axis, k):
    n = lax.axis_size(axis)
    return lax.ppermute(x, axis, [((i + k) % n, i) for i in range(n)])


def gather_ring(x, axis):
    return [x] + [from_ahead(x, axis, k) for k in range(1, lax.axis_size(axis))]


def scatter_ring(x, axis, rows):
    n = lax.axis_size(axis)
    return [
        lax.ppermute(x[k * rows : (k + 1) * rows], axis, [(i, (i + k) % n) for i in range(n)])
        for k in range(1, n)
    ]


def swap(x, axis, bit):
    n = lax.axis_size(axis)
    return lax.ppermute(x, axis, [(i, i ^ bit) for i in range(n)])


def spread(held, axis, bit):
    while bit:
        held = held + [swap(h, axis, bit) for h in held]
        bit //= 2
    return held


def tree(terms, op=jnp.add):
    while len(terms) > 1:
        half = len(terms) // 2
        rest = terms[2 * half :]
        terms = [op(terms[i], terms[i + half]) for i in range(half)] + rest
    return terms[0]


def three_parts(x):
    hi = x.astype(bf16).astype(f32)
    mid = (x - hi).astype(bf16).astype(f32)
    return hi, mid, x - hi - mid


def lanes(rows):
    return lax.broadcasted_iota(i32, (rows, LANES), 1)


def attend_kernel(n_seq, scal, *refs):
    q_refs = refs[:n_seq]
    k_ref, v_ref, o_ref, q_out, q_twice, t_twice = refs[n_seq:]
    tgt_rows = q_refs[0].shape[1]
    rows = tgt_rows * n_seq
    enc, features = k_ref.shape[1:]
    for i, r in enumerate(q_refs):
        for at in (i * tgt_rows, rows + i * tgt_rows):
            q_twice[at : at + tgt_rows, :] = r[0]
    q = q_twice[pl.ds(pl.multiple_of(scal[0], 16), rows), :]
    q_out[...] = q
    valid = lax.broadcasted_iota(i32, (rows, enc), 1) < scal[1]
    lane = lanes(rows)
    here = lanes(tgt_rows)
    row = lax.broadcasted_iota(i32, here.shape, 0)
    ids = jnp.zeros(here.shape, i32)
    for i in range(tgt_rows):
        ids = jnp.where(row == i, scal[3 + i], ids)
    digits = jnp.where(here == LANES - 2, ids >> 8, jnp.where(here == LANES - 1, ids & 255, 0))
    digits = digits.astype(f32)
    t_twice[...] = jnp.zeros_like(t_twice)
    t_twice[:tgt_rows, :] = digits
    t_twice[rows : rows + tgt_rows, :] = digits
    stat = t_twice[pl.ds(pl.multiple_of(scal[0], 16), rows), :]
    for h in range(features // HDIM):
        at = slice(h * HDIM, (h + 1) * HDIM)
        scores = dot(q[:, at], k_ref[0, :, at], 1, 1)
        scores = jnp.where(valid, scores, LOW)
        peak = jnp.max(scores, axis=1, keepdims=True)
        e = jnp.where(valid, jnp.exp(scores - peak), 0.0)
        total = jnp.sum(e, axis=1, keepdims=True)
        some = total > 0.0
        safe = jnp.where(some, total, 1.0)
        o = dot(e.astype(bf16), v_ref[0, :, at], 1, 0) / safe
        o_ref[:, at] = o.astype(bf16)
        lse = jnp.where(some, peak + jnp.log(safe), LOW)
        for i, part in enumerate(three_parts(lse)):
            stat = jnp.where(lane == 3 * h + i, part, stat)
    o_ref[:, features:] = stat.astype(bf16)


def project_kernel(n_seq, own_rows, ptile, scal, *refs):
    o_refs = refs[:n_seq]
    p_ref, mixed_ref, own_ref, att_ref, lse_ref, tgt_ref = refs[n_seq:]
    rows, features = att_ref.shape
    stats = [r[:, features:].astype(f32) for r in o_refs]
    lane = lanes(rows)
    lse_all = jnp.zeros((rows, LANES), f32)
    for h in range(features // HDIM):
        at = slice(h * HDIM, (h + 1) * HDIM)
        lses = [
            s[:, 3 * h : 3 * h + 1] + s[:, 3 * h + 1 : 3 * h + 2] + s[:, 3 * h + 2 : 3 * h + 3]
            for s in stats
        ]
        top = tree(lses, jnp.maximum)
        lse = top + jnp.log(tree([jnp.exp(x - top) for x in lses]))
        o = tree([jnp.exp(x - lse) * r[:, at].astype(f32) for x, r in zip(lses, o_refs)])
        att_ref[:, at] = o.astype(bf16)
        lse_all = jnp.where(lane == h, lse, lse_all)
    lse_ref[...] = lse_all
    ids = tree([s[:, LANES - 2 : LANES - 1] * 256.0 + s[:, LANES - 1 :] for s in stats])
    tgt_ref[...] = jnp.broadcast_to(ids.astype(i32), (rows, LANES)) - scal[2]
    for at in range(0, mixed_ref.shape[1], ptile):
        c = slice(at, at + ptile)
        part = dot(att_ref[...], p_ref[:, c], 1, 0)
        mixed_ref[:, c] = part.astype(bf16)
        own_ref[:, c] = part[:own_rows]


def norm_kernel(n_got, *refs):
    own_ref, got_refs = refs[0], refs[1 : 1 + n_got]
    packed_ref, mixed_ref, ng_ref = refs[1 + n_got :]
    rows, width = mixed_ref.shape
    mixed = own_ref[...] + packed_ref[:rows, :]
    for r in got_refs:
        mixed = mixed + r[...].astype(f32)
    mixed_ref[...] = mixed
    ng_ref[:, :width] = (mixed * packed_ref[rows : rows + 1, :]).astype(bf16)
    square = jnp.sum(mixed * mixed, axis=1, keepdims=True)
    lane = lanes(rows)
    stat = jnp.zeros((rows, LANES), f32)
    for i, part in enumerate(three_parts(square)):
        stat = jnp.where(lane == i, part, stat)
    ng_ref[:, width:] = stat.astype(bf16)


def start_weights(first, cols, w_ref, edge_ref, buf, sems):
    copies = []
    for i in range(buf.shape[0] // PART):
        at = first + i * PART
        n = PART if at + PART <= cols else cols - at
        if n == PART or (n > 0 and cols % 16 == 0):
            here = buf.at[i * PART : i * PART + n]
            copies.append(pltpu.make_async_copy(w_ref.at[at : at + n], here, sems.at[i]))
    for c in copies:
        c.start()
    for i in range(buf.shape[0] // PART):
        n = min(max(cols - first - i * PART, 0), PART)
        if n == PART:
            continue
        if i < len(copies):
            buf[i * PART + n : (i + 1) * PART, :] = jnp.zeros((PART - n, buf.shape[1]), bf16)
        elif n:
            rows = lax.broadcasted_iota(i32, (PART, 1), 0)
            edge = edge_ref[...]
            buf[i * PART : (i + 1) * PART, :] = jnp.where(rows < n, edge, jnp.zeros_like(edge))
        else:
            buf[i * PART : (i + 1) * PART, :] = jnp.zeros((PART, buf.shape[1]), bf16)
    return copies


def wait_tile(copies, t):
    for c in copies[t * PARTS : (t + 1) * PARTS]:
        c.wait()


def logits_kernel(first, cols, n_vocab, *refs):
    ng_refs, (w_ref, edge_ref) = refs[:n_vocab], refs[n_vocab : n_vocab + 2]
    outs = refs[n_vocab + 2 :]
    code_ref = outs[0]
    z, buf, sems = outs[-3:]
    width = buf.shape[1]
    copies = start_weights(first, cols, w_ref, edge_ref, buf, sems)
    ng = jnp.concatenate([r[...] for r in ng_refs], axis=0)
    if len(outs) > 4:
        outs[1][...] = ng[:, :width]
    for t in range(z.shape[1] // TILE):
        wait_tile(copies, t)
        at = slice(t * TILE, (t + 1) * TILE)
        z[:, at] = dot(ng[:, :width], buf[at, :], 1, 1)
    val = z[...]
    peak = jnp.maximum(jnp.max(jnp.abs(val), axis=1, keepdims=True), 1e-30)
    s = ng[:, width:].astype(f32)
    square = jnp.maximum(s[:, 0:1] + s[:, 1:2] + s[:, 2:3], 1e-30)
    mark = jnp.floor(jnp.log(peak) * LOG_STEPS) + 2.0
    coarse = jnp.round(jnp.log(square) * LOG_STEPS)
    fine = jnp.round((square / jnp.exp(coarse / LOG_STEPS) - 1.0) * FINE_STEPS)
    size = z.shape[1]
    code = jnp.round(val / code_step(mark))
    code_ref[:, :size] = code.astype(i32).astype(jnp.int16)
    lane = lanes(z.shape[0])
    stat = jnp.where(lane == 0, mark, jnp.where(lane == 1, coarse, jnp.where(lane == 2, fine, 0.0)))
    code_ref[:, size:] = stat.astype(i32).astype(jnp.int16)


def code_step(mark):
    return jnp.exp(mark / LOG_STEPS) / CODE_TOP


def decode(code_ref, size):
    stat = code_ref[:, size:].astype(i32).astype(f32)
    square = jnp.exp(stat[:, 1:2] / LOG_STEPS) * (1.0 + stat[:, 2:3] / FINE_STEPS)
    return code_ref[:, :size].astype(i32).astype(f32) * code_step(stat[:, 0:1]), square


def exp_rows(chunk, first, cols, n_seq, features, refs, e_ref, st_ref, lhs):
    tgt_ref = refs[n_seq]
    rows, size = e_ref.shape
    members = [decode(r, size) for r in refs[:n_seq]]
    z = tree([m[0] for m in members])
    square = tree([m[1] for m in members])
    inv = lax.rsqrt(square / features + norm_epsilon)
    z = z * inv
    at = first + lax.broadcasted_iota(i32, (rows, size), 1)
    hit = at == tgt_ref[:, 0:1]
    if first + size > cols:
        z = jnp.where(at < cols, z, LOW)
        hit = hit & (at < cols)
    here = jnp.sum(jnp.where(hit, z, 0.0), axis=1, keepdims=True)
    peak = jnp.max(z, axis=1, keepdims=True)
    if chunk:
        old = refs[n_seq + 1][...]
        peak = jnp.maximum(peak, old[:, 0:1])
        fade = jnp.exp(old[:, 0:1] - peak)
    else:
        old = jnp.zeros((rows, LANES), f32)
        fade = jnp.zeros((rows, 1), f32)
    e = jnp.exp(z - peak)
    total = jnp.sum(e, axis=1, keepdims=True) + old[:, 1:2] * fade
    eh = e.astype(bf16)
    e_ref[...] = eh
    lhs[:rows, :] = eh
    lhs[rows:, :] = hit.astype(f32).astype(bf16)
    lane = lanes(rows)
    st = jnp.where(lane == 0, peak, old)
    st = jnp.where(lane == 1, total, st)
    st = jnp.where(lane == 2, here + old[:, 2:3], st)
    st = jnp.where(lane == 3, inv, st)
    st_ref[...] = jnp.where(lane == 8 + chunk, peak, st)
    return fade


def hidden_sum(chunk, copies, buf, lhs, acc_prev, fade, acc_ref):
    rows = acc_ref.shape[0] // 2
    if chunk:
        acc_ref[:rows, :] = acc_prev[:rows, :] * fade
        acc_ref[rows:, :] = acc_prev[rows:, :]
    for t in range(buf.shape[0] // TILE):
        wait_tile(copies, t)
        at = slice(t * TILE, (t + 1) * TILE)
        part = dot(lhs[:, at], buf[at, :], 1, 0)
        if chunk or t:
            acc_ref[...] += part
        else:
            acc_ref[...] = part


def hidden_kernel(chunk, first, cols, n_seq, features, *refs):
    n = n_seq + 1 + (1 if chunk else 0)
    ins, refs = refs[:n], refs[n:]
    acc_prev = None
    if chunk:
        acc_prev, refs = refs[0], refs[1:]
    w_ref, edge_ref, acc_ref, e_ref, st_ref, lhs, buf, sems = refs
    copies = start_weights(first, cols, w_ref, edge_ref, buf, sems)
    fade = exp_rows(chunk, first, cols, n_seq, features, ins, e_ref, st_ref, lhs)
    hidden_sum(chunk, copies, buf, lhs, acc_prev, fade, acc_ref)


def last_exp_kernel(chunk, first, cols, n_seq, features, *refs):
    ins, (e_ref, st_ref, lhs_ref) = refs[:-3], refs[-3:]
    exp_rows(chunk, first, cols, n_seq, features, ins, e_ref, st_ref, lhs_ref)


def last_hidden_kernel(
    chunk, first, cols, st_prev, st_ref, lhs_ref, acc_prev, w_ref, edge_ref, acc_ref, buf, sems
):
    copies = start_weights(first, cols, w_ref, edge_ref, buf, sems)
    fade = jnp.exp(st_prev[:, 0:1] - st_ref[:, 0:1])
    hidden_sum(chunk, copies, buf, lhs_ref, acc_prev, fade, acc_ref)


def total_kernel(n_vocab, own_rows, *refs):
    st_refs = refs[:n_vocab]
    acc_ref, part_ref, own_ref, coef_ref = refs[n_vocab:]
    rows = coef_ref.shape[0]
    mine = st_refs[0][...]
    stats = [mine]
    for k in range(1, n_vocab):
        s = st_refs[k][...]
        cut = rows - k * own_rows
        stats.append(jnp.concatenate([s[cut:], s[:cut]], axis=0))
    top = tree([s[:, 0:1] for s in stats], jnp.maximum)
    total = tree([s[:, 1:2] * jnp.exp(s[:, 0:1] - top) for s in stats])
    hit_logit = tree([s[:, 2:3] for s in stats])
    log_total = top + jnp.log(total)
    loss = log_total - hit_logit + zloss_weight * log_total * log_total
    lift = 1.0 + 2.0 * zloss_weight * log_total
    inv = mine[:, 3:4]
    lane = lanes(rows)
    coef = jnp.exp(jnp.minimum(mine - log_total, 30.0)) * lift * inv
    coef = jnp.where(lane >= 8, coef, inv)
    coef_ref[...] = jnp.where(lane == 1, loss, coef)
    scale = jnp.exp(mine[:, 0:1] - log_total) * lift
    part = acc_ref[:rows, :] * scale - acc_ref[rows:, :]
    part_ref[...] = part.astype(bf16)
    own_ref[...] = part[:own_rows]


def grad_kernel(firsts, n_out, coef_ref, tgt_ref, *refs):
    n = len(firsts)
    outs = refs[n : n + n_out]
    inv = coef_ref[:, 0:1]
    for c, first in enumerate(firsts):
        e_ref = refs[c]
        for off in range(0, e_ref.shape[1], TILE):
            e = e_ref[:, off : off + TILE]
            at = first + off + lax.broadcasted_iota(i32, e.shape, 1)
            hit = at == tgt_ref[:, 0:1]
            g = e.astype(f32) * coef_ref[:, 8 + c : 9 + c] - jnp.where(hit, inv, 0.0)
            group, place = divmod(first + off, outs[0].shape[1])
            outs[group][:, place : place + TILE] = g.astype(bf16)
    last = refs[-1]
    rows, size = last.shape
    lane = lanes(rows)
    stat = last[:, size - LANES :].astype(f32)
    for i, part in enumerate(three_parts(coef_ref[:, 1:2])):
        stat = jnp.where(lane == LANES - 3 + i, part, stat)
    last[:, size - LANES :] = stat.astype(bf16)


def head_kernel(n_dp, rows_all, *refs):
    ng_refs, g_refs = refs[:n_dp], refs[n_dp : 2 * n_dp]
    out_ref, loss_ref, ng, turned = refs[-4:]
    rows, width = ng_refs[0].shape[0], out_ref.shape[1]

    @pl.when(pl.program_id(0) == 0)
    def _():
        for i, r in enumerate(ng_refs):
            ng[i * rows : (i + 1) * rows, :] = r[:, :width]

    turned[...] = jnp.concatenate([r[...] for r in g_refs], axis=0).T
    for at in range(0, width, 256):
        out_ref[:, at : at + 256] = dot(turned[...], ng[:, at : at + 256], 1, 0).astype(bf16)

    @pl.when(pl.program_id(0) == pl.num_programs(0) - 1)
    def _():
        sums = []
        for r in g_refs:
            s = r[:, HEAD_TILE - LANES :].astype(f32)
            sums.append(jnp.sum(s[:, -3:-2] + s[:, -2:-1] + s[:, -1:]))
        loss_ref[0, 0] = tree(sums) * (1.0 / rows_all)


def gate_kernel(n_got, *refs):
    own_ref, got_refs = refs[0], refs[1 : 1 + n_got]
    mixed_ref, packed_ref, gated_ref, dot_ref = refs[1 + n_got :]
    total = own_ref[...]
    for r in got_refs:
        total = total + r[...].astype(f32)
    rows = mixed_ref.shape[0]
    gated = total * packed_ref[rows : rows + 1, :]
    gated_ref[...] = gated
    inner = jnp.sum(gated * mixed_ref[...], axis=1, keepdims=True)
    dot_ref[...] = jnp.broadcast_to(inner, dot_ref.shape)


def mixed_grad_kernel(n_seq, features, gated_ref, mixed_ref, coef_ref, *refs):
    dot_refs, out_ref = refs[:n_seq], refs[n_seq]
    inner = tree([r[:, 0:1] for r in dot_refs])
    inv = coef_ref[: out_ref.shape[0], 0:1]
    out = gated_ref[...] * inv - mixed_ref[...] * (inv * inv * inv * inner / features)
    out_ref[...] = out.astype(bf16)


def back_project_kernel(*refs):
    mg_refs, p_ref, out_ref = refs[:-2], refs[-2], refs[-1]
    mg = jnp.concatenate([r[...] for r in mg_refs], axis=0)
    for at in range(0, out_ref.shape[1], HDIM):
        part = dot(mg, p_ref[at : at + HDIM, :], 1, 1)
        out_ref[:, at : at + HDIM] = part.astype(bf16)


def attend_back_kernel(n_seq, scal, *refs):
    a_refs = refs[:n_seq]
    q_ref, k_ref, v_ref, att_ref, lse_ref, kg_ref, vg_ref = refs[n_seq:]
    enc, features = k_ref.shape[1:]
    rows = q_ref.shape[0]
    valid = lax.broadcasted_iota(i32, (rows, enc), 1) < scal[1]
    for h in range(features // HDIM):
        at = slice(h * HDIM, (h + 1) * HDIM)
        grad = tree([r[:, at].astype(f32) for r in a_refs]).astype(bf16)
        q = q_ref[:, at]
        scores = dot(q, k_ref[0, :, at], 1, 1)
        w = jnp.where(valid, jnp.exp(jnp.minimum(scores - lse_ref[:, h : h + 1], 0.5)), 0.0)
        prob_grad = dot(grad, v_ref[0, :, at], 1, 1)
        inner = jnp.sum(grad.astype(f32) * att_ref[:, at].astype(f32), axis=1, keepdims=True)
        sg = (w * (prob_grad - inner) * score_scale).astype(bf16)
        vg_ref[0, :, at] = dot(w.astype(bf16), grad, 0, 0)
        kg_ref[0, :, at] = dot(sg, q, 0, 0)


def body(
    queries, enc_keys, enc_values, enc_lengths, out_proj, residual, norm_gain, head_weight, targets
):
    n_seq, n_vocab, n_dp = lax.axis_size("seq"), lax.axis_size("vocab"), lax.axis_size("dp")
    seq, voc = lax.axis_index("seq"), lax.axis_index("vocab")
    tgt_rows, features = queries.shape[1:]
    enc = enc_keys.shape[1]
    rows = tgt_rows * n_seq
    own_rows = rows // n_vocab
    width, cols = head_weight.shape
    full_width = width * n_seq
    tiles = -(-cols // TILE)
    per = 2 * -(-tiles // (2 * MAX_CHUNKS))
    assert tiles % 2 == 0
    chunks = [(t, min(per, tiles - t)) for t in range(0, tiles, per)]
    firsts = [t * TILE for t, _ in chunks]
    gain = norm_gain.reshape(1, width)
    weight = head_weight.T

    start = lax.rem(voc * own_rows - seq * tgt_rows + rows, rows).astype(i32)
    scal = jnp.stack([start, enc_lengths[0] - seq * enc, voc * cols]).astype(i32)
    scal = jnp.concatenate([scal, targets[0]])

    q_parts = gather_ring(queries, "seq")
    keys = enc_keys * jnp.asarray(score_scale, bf16)
    res_own = lax.dynamic_slice(residual[0], (voc * own_rows, 0), (own_rows, width)).astype(f32)
    packed = jnp.concatenate([res_own, jnp.broadcast_to(gain, (8, width))], axis=0)
    o_part, q_all = pl.pallas_call(
        functools.partial(attend_kernel, n_seq),
        out_shape=[sds((rows, features + LANES), bf16), sds((rows, features), bf16)],
        in_specs=[SMEM] + [VMEM] * (n_seq + 2),
        out_specs=[VMEM, VMEM],
        scratch_shapes=[
            pltpu.VMEM((2 * rows, features), bf16),
            pltpu.VMEM((2 * rows, LANES), f32),
        ],
        compiler_params=params(),
        cost_estimate=cost(0, 7 * 1024 * 1024),
        name="attend",
    )(scal, *q_parts, keys, enc_values)

    o_all = gather_ring(o_part, "seq")
    ptile = min(TILE, width)
    whole = lambda shape: pl.BlockSpec(shape, lambda j: (0, 0))
    anywhere = pl.BlockSpec(memory_space=pl.ANY)
    mixed_part, mixed_own, att, lse, tgt = pl.pallas_call(
        functools.partial(project_kernel, n_seq, own_rows, ptile),
        out_shape=[
            sds((rows, width), bf16),
            sds((own_rows, width), f32),
            sds((rows, features), bf16),
            sds((rows, LANES), f32),
            sds((rows, LANES), i32),
        ],
        in_specs=[SMEM] + [VMEM] * (n_seq + 1),
        out_specs=[VMEM] * 5,
        compiler_params=params(),
        cost_estimate=cost(0, 7 * 1024 * 1024),
        name="project",
    )(scal, *o_all, out_proj)

    got = scatter_ring(mixed_part, "vocab", own_rows)
    mixed, ng_own = pl.pallas_call(
        functools.partial(norm_kernel, len(got)),
        out_shape=[sds((own_rows, width), f32), sds((own_rows, width + LANES), bf16)],
        in_specs=[VMEM] * (2 + len(got)),
        out_specs=[VMEM, VMEM],
        compiler_params=params(),
        cost_estimate=cost(0, 7 * 1024 * 1024),
        name="norm",
    )(mixed_own, *got, packed)
    ng_parts = gather_ring(ng_own, "vocab")

    last_part = pl.BlockSpec((PART, width), lambda j: (-(-cols // PART) - 1, 0))

    def in_vmem(shapes, odd):
        if not odd:
            return [VMEM] * len(shapes)
        return [pl.BlockSpec(x.shape, lambda j: (0, 0)) for x in shapes]

    weights = [weight, weight]
    codes = []
    for c, (tile0, n) in enumerate(chunks):
        size = n * TILE
        odd = tile0 * TILE + size > cols and cols % 16 != 0
        edge = last_part if odd else anywhere
        stacked = [] if c else [sds((rows, width), bf16)]
        shapes = [sds((rows, size + LANES), jnp.int16)] + stacked
        outs = pl.pallas_call(
            functools.partial(logits_kernel, tile0 * TILE, cols, n_vocab),
            grid=(1,) if odd else (),
            out_shape=shapes,
            in_specs=in_vmem(ng_parts, odd) + [anywhere, edge],
            out_specs=in_vmem(shapes, odd),
            scratch_shapes=[
                pltpu.VMEM((rows, size), f32),
                pltpu.VMEM((size, width), bf16),
                pltpu.SemaphoreType.DMA((size // PART,)),
            ],
            compiler_params=params(),
            cost_estimate=cost(2 * 256 * width * size, 2 * width * size),
            name="logits",
        )(*ng_parts, *weights)
        codes.append(gather_ring(outs[0], "seq"))
        if stacked:
            ng_dp = [outs[1]] + ([swap(outs[1], "dp", n_dp // 2)] if n_dp > 1 else [])

    codes[-1], ng_dp = lax.optimization_barrier((codes[-1], ng_dp))
    acc = st = None
    exps = []
    for c, (tile0, n) in enumerate(chunks):
        size = n * TILE
        first = tile0 * TILE
        odd = first + size > cols and cols % 16 != 0
        edge = last_part if odd else anywhere
        estimate = cost(2 * 256 * width * size, 2 * width * size)
        acc_shape, e_shape = sds((2 * rows, width), f32), sds((rows, size), bf16)
        st_shape = sds((rows, LANES), f32)
        buffers = [
            pltpu.VMEM((size, width), bf16),
            pltpu.SemaphoreType.DMA((size // PART,)),
        ]
        prev = [st] if c else []
        ins = [*codes[c], tgt, *prev]
        if c == 0 or c < len(chunks) - 1:
            acc, e, st = pl.pallas_call(
                functools.partial(hidden_kernel, c, first, cols, n_seq, full_width),
                grid=(1,) if odd else (),
                out_shape=[acc_shape, e_shape, st_shape],
                in_specs=in_vmem(ins + ([acc] if c else []), odd) + [anywhere, edge],
                out_specs=in_vmem([acc_shape, e_shape, st_shape], odd),
                scratch_shapes=[pltpu.VMEM((2 * rows, size), bf16)] + buffers,
                compiler_params=params(),
                cost_estimate=estimate,
                name="hidden",
            )(*ins, *([acc] if c else []), *weights)
            st_all = gather_ring(st, "vocab") if c == len(chunks) - 1 else None
        else:
            before = st
            e, st, left = pl.pallas_call(
                functools.partial(last_exp_kernel, c, first, cols, n_seq, full_width),
                out_shape=[e_shape, st_shape, sds((2 * rows, size), bf16)],
                in_specs=[VMEM] * len(ins),
                out_specs=[VMEM] * 3,
                compiler_params=params(),
                cost_estimate=cost(0, 4 * 1024 * 1024),
                name="last_exp",
            )(*ins)
            st_all = gather_ring(st, "vocab")
            acc = pl.pallas_call(
                functools.partial(last_hidden_kernel, c, first, cols),
                grid=(1,) if odd else (),
                out_shape=acc_shape,
                in_specs=in_vmem([before, st, left, acc], odd) + [anywhere, edge],
                out_specs=in_vmem([acc_shape], odd)[0],
                scratch_shapes=buffers,
                compiler_params=params(),
                cost_estimate=estimate,
                name="last_hidden",
            )(before, st, left, acc, *weights)
        exps.append(e)

    hidden_part, hidden_own, coef = pl.pallas_call(
        functools.partial(total_kernel, n_vocab, own_rows),
        out_shape=[
            sds((rows, width), bf16),
            sds((own_rows, width), f32),
            sds((rows, LANES), f32),
        ],
        in_specs=[VMEM] * (n_vocab + 1),
        out_specs=[VMEM] * 3,
        compiler_params=params(),
        cost_estimate=cost(0, 7 * 1024 * 1024),
        name="total",
    )(*st_all, acc)
    group = tiles * TILE // GROUPS
    assert cols + 3 <= tiles * TILE and group % HEAD_TILE == 0
    grads = pl.pallas_call(
        functools.partial(grad_kernel, firsts, GROUPS),
        out_shape=[sds((rows, group), bf16)] * GROUPS,
        in_specs=[VMEM] * (2 + len(exps)),
        out_specs=[VMEM] * GROUPS,
        compiler_params=params(),
        cost_estimate=cost(0, 7 * 1024 * 1024),
        name="logit_grad",
    )(coef, tgt, *exps)
    hidden_part, grads = lax.optimization_barrier((hidden_part, grads))
    got = scatter_ring(hidden_part, "vocab", own_rows)
    bit = n_dp // 2
    across = [swap(g, "dp", bit) for g in grads] if bit else []
    gated, inner = pl.pallas_call(
        functools.partial(gate_kernel, len(got)),
        out_shape=[sds((own_rows, width), f32), sds((own_rows, LANES), f32)],
        in_specs=[VMEM] * (3 + len(got)),
        out_specs=[VMEM, VMEM],
        compiler_params=params(),
        cost_estimate=cost(0, 7 * 1024 * 1024),
        name="gate",
    )(hidden_own, *got, mixed, packed)
    inner_all = gather_ring(inner, "seq")
    mixed_grad = pl.pallas_call(
        functools.partial(mixed_grad_kernel, n_seq, full_width),
        out_shape=sds((own_rows, width), bf16),
        in_specs=[VMEM] * (3 + n_seq),
        out_specs=VMEM,
        compiler_params=params(),
        cost_estimate=cost(0, 7 * 1024 * 1024),
        name="mixed_grad",
    )(gated, mixed, coef, *inner_all)
    mg_parts = gather_ring(mixed_grad, "vocab")

    back_part = pl.pallas_call(
        back_project_kernel,
        out_shape=sds((rows, features), bf16),
        in_specs=[VMEM] * (n_vocab + 1),
        out_specs=VMEM,
        compiler_params=params(),
        cost_estimate=cost(0, 7 * 1024 * 1024),
        name="back_project",
    )(*mg_parts, out_proj)
    back_part, ng_dp = lax.optimization_barrier((back_part, ng_dp))
    back_all = gather_ring(back_part, "seq")
    ng_dp = spread(ng_dp, "dp", n_dp // 4)
    back_all, across = lax.optimization_barrier((back_all, across))
    grads_dp = []
    for i, g in enumerate(grads):
        grads_dp.append(spread([g, across[i]] if across else [g], "dp", n_dp // 4))
    key_grad, value_grad = pl.pallas_call(
        functools.partial(attend_back_kernel, n_seq),
        out_shape=[sds(enc_keys.shape, f32), sds(enc_values.shape, f32)],
        in_specs=[SMEM] + [VMEM] * (n_seq + 5),
        out_specs=[VMEM, VMEM],
        compiler_params=params(),
        cost_estimate=cost(0, 7 * 1024 * 1024),
        name="attend_back",
    )(scal, *back_all, q_all, keys, enc_values, att, lse)

    head = None
    for c in range(GROUPS):
        prev = [head] if c else []
        steps = group // HEAD_TILE
        head, loss = pl.pallas_call(
            functools.partial(head_kernel, n_dp, n_dp * rows),
            grid=(steps,),
            out_shape=[sds((cols, width), bf16), sds((1, 1), f32)],
            in_specs=[whole((rows, width))] * n_dp
            + [pl.BlockSpec((rows, HEAD_TILE), lambda j: (0, j))] * n_dp
            + [anywhere] * len(prev),
            out_specs=[
                pl.BlockSpec((HEAD_TILE, width), lambda j, t=c * steps: (t + j, 0)),
                SMEM,
            ],
            scratch_shapes=[
                pltpu.VMEM((n_dp * rows, width), bf16),
                pltpu.VMEM((HEAD_TILE, n_dp * rows), bf16),
            ],
            input_output_aliases={2 * n_dp: 0} if c else {},
            compiler_params=params(),
            cost_estimate=cost(2 * n_dp * rows * width * group, 2 * width * group),
            name="head_grad",
        )(*ng_dp, *grads_dp[c], *prev)
    return (loss.reshape(()), head.T, key_grad, value_grad)


def solution(mesh):
    placed = (
        P("dp", "seq", "vocab"),
        P("dp", "seq", "vocab"),
        P("dp", "seq", "vocab"),
        P("dp"),
        P("vocab", "seq"),
        P("dp", None, "seq"),
        P("seq"),
        P("seq", "vocab"),
        P("dp", "seq"),
    )
    return jax.shard_map(
        body,
        mesh=mesh,
        in_specs=placed,
        out_specs=(P(), P("seq", "vocab"), P("dp", "seq", "vocab"), P("dp", "seq", "vocab")),
        check_vma=False,
    )
```
